32 devices in a mesh: dp: 4 (over z), mp: 2 (over x), dmod: 4 (over y, core).
Axes of the slice: x: 2, y: 2, z: 4, core: 2. Of those that a mesh axis runs over, the one named last changes fastest.
Arguments:
- block_input: bfloat16 [2, 4, 256, 2048], P(None, 'dp', None, 'dmod'), may hold values from -6 to 6
- segment_ids: int32 [2, 4, 256], P(None, 'dp'), may hold values from 0 to 5, never falling along the last dimension, each value on 1 to 128 neighbouring positions
- group_ids: int32 [2, 4, 256], P(None, 'dp'), may hold values from 0 to 7
- group_weight: float32 [8], replicated, may hold values from 0.5 to 2
- mixer_norm: bfloat16 [2048], P(('dmod', 'dp')), may hold values from 0.5 to 1.5
- w_mix: bfloat16 [2048, 4, 2048], P(('dmod', 'dp'), None, 'mp'), may hold values from -0.125 to 0.125
- w_beta: bfloat16 [2048, 16], P(('dmod', 'dp'), 'mp'), may hold values from -0.125 to 0.125
- conv_kernel: bfloat16 [3, 4, 2048], P(None, None, ('mp', 'dmod', 'dp')), may hold values from -3 to 3
- head_norm: bfloat16 [128], P('dp'), may hold values from 0.5 to 1.5
- w_out: bfloat16 [2048, 2048], P('mp', ('dmod', 'dp')), may hold values from -0.1875 to 0.1875
- ffn_norm: bfloat16 [2048], P(('dmod', 'dp')), may hold values from 0.5 to 1.5
- w_ffn_in: bfloat16 [2048, 2, 5632], P(('dmod', 'dp'), None, 'mp'), may hold values from -0.125 to 0.125
- w_ffn_down: bfloat16 [5632, 2048], P('mp', ('dmod', 'dp')), may hold values from -0.109375 to 0.109375
- cotangent: bfloat16 [2, 4, 256, 2048], P(None, 'dp', None, 'dmod'), may hold values from -6 to 6
Outputs:
- out: bfloat16 [2, 4, 256, 2048], P(None, 'dp', None, 'dmod')
- grad_input: float32 [2, 4, 256, 2048], P(None, 'dp', None, 'dmod')
- grad_mixer_norm: float32 [2048], P(('dmod', 'dp'))
- grad_w_mix: float32 [2048, 4, 2048], P(('dmod', 'dp'), None, 'mp')
- grad_w_beta: float32 [2048, 16], P(('dmod', 'dp'), 'mp')
- grad_conv_kernel: float32 [3, 4, 2048], P(None, None, ('mp', 'dmod', 'dp'))
- grad_head_norm: float32 [128], P('dp')
- grad_w_out: float32 [2048, 2048], P('mp', ('dmod', 'dp'))
- grad_ffn_norm: float32 [2048], P(('dmod', 'dp'))
- grad_w_ffn_in: float32 [2048, 2, 5632], P(('dmod', 'dp'), None, 'mp')
- grad_w_ffn_down: float32 [5632, 2048], P('mp', ('dmod', 'dp'))
The draws below stay inside these ranges and needn't reach their ends.
Inputs may be any that keep to these rules, and one draw needn't show every extreme that they name: `segment_ids`: never falls along a sequence; a document holds at most 128 tokens, and one holds exactly that many.
All inputs are finite; a program needn't handle non-finite values.
Results may differ from the reference program's by a relative error of at most 0.017.
Values may be sent and summed in bfloat16 or wider, within the bound.
No kernel may reach another device: no remote copies, remote signals or barrier semaphores. Data moves between devices by JAX's collectives and lax.ppermute only.
A program may use at most 192 MiB of HBM per device.

```python
import math
from functools import partial
import jax
import jax.numpy as jnp
import numpy as np
from jax import lax

D = 2048
HEADS = 16
HEAD = 128
FF = 5632
KEYS = 2048
CONV = 4
BLOCK = 64
LEN = 256
MICRO = 2
DOCS = 6
GROUPS = 8
SEQS = 4


def draw_group_ids(key, part):
    key = jax.random.fold_in(key, 11)
    first, second, third = jax.random.split(key, 3)
    shape = (MICRO, SEQS, LEN)
    rows = jnp.arange(SEQS, dtype=jnp.int32)
    limits = 1 + (GROUPS - 1) * rows // max(SEQS - 1, 1)
    narrow = jax.random.randint(first, shape, 0, limits[None, :, None])
    wide = jax.random.randint(second, shape, 0, GROUPS)
    picks = jax.random.randint(third, shape, 0, 2)
    return jnp.where(picks == 1, wide, narrow).astype(jnp.int32)


def spiked(values, own_key, source, target, shards_of, factor):
    def block_of(axis_at):
        return (jnp.arange(values.shape[axis_at]) // (values.shape[axis_at] // shards_of)).reshape((-1,) + (1,) * (values.ndim - 1 - axis_at))

    one_side = jax.random.permutation(own_key, shards_of)[block_of(target)]
    second = (block_of(target) + shards_of // 2) % shards_of
    return jnp.where((block_of(source) == one_side) | (block_of(source) == second), factor * values, values)


def level_of(stream_key, dims, pieces, low, top_value):
    def one(position, blocks):
        draws = jax.random.uniform(jax.random.fold_in(jax.random.fold_in(stream_key, 6), position), (blocks,), jnp.float32, low / len(pieces), top_value / len(pieces))
        return jnp.repeat(jnp.exp(draws), dims[position] // blocks).reshape((-1,) + (1,) * (len(dims) - position - 1))

    loudness = one(*pieces[0])
    for cut in pieces[1:]:
        loudness = loudness * one(*cut)
    return loudness


def profile(number_of, total, limit, lean):
    weights = [(1 << 20) // math.isqrt(rank ** lean) + 1 for rank in range(2, number_of + 1)]
    surplus, given = total - limit - (number_of - 1), [1] * (number_of - 1)
    while surplus > 0:
        candidates = [i for i in range(number_of - 1) if given[i] < limit]
        mass, left = sum([weights[i] for i in candidates]), surplus
        for i in candidates:
            addition = min(limit - given[i], max(1, left * weights[i] // mass), surplus)
            given[i] = given[i] + addition
            surplus = surplus - addition
    return np.array([limit] + given)


def ragged(own_key, count, total, bound, skew):
    if count == 2:
        one = jax.random.randint(own_key, (), max(1, total - bound), min(bound, total - 1) + 1)
        return jnp.stack([one, total - one])
    tallies = jnp.asarray(profile(count, total, bound, skew), jnp.int32)
    couples = (count - 1) // 2
    source_of, taker = tallies[1:1 + 2 * couples:2], tallies[2:2 + 2 * couples:2]
    room = jnp.minimum(source_of - 1, bound - taker)
    shifted = jax.random.randint(jax.random.fold_in(own_key, 1), (couples,), 0, 1 << 20) % (room + 1)
    tallies = tallies.at[1:1 + 2 * couples:2].set(source_of - shifted).at[2:2 + 2 * couples:2].set(taker + shifted)
    return tallies[jax.random.permutation(jax.random.fold_in(own_key, 2), count)]


def scatter_about(own_key, shape, deviation, reach, cuts=(), kind=jnp.bfloat16):
    values = jax.random.normal(own_key, shape, jnp.float32) * deviation
    if len(cuts) > 0:
        values = level_of(own_key, shape, cuts, -0.22, 0.18) * values
    return jnp.clip(values, min=-reach, max=reach).astype(kind)


def bell_draw_with(key, extent, width, bound, shards, heavy, kind=jnp.bfloat16):
    values = width * jax.random.normal(key, extent, jnp.float32)
    if shards:
        values = values * level_of(key, extent, shards, -0.22, 0.18)
    return jnp.clip(spiked(values, jax.random.fold_in(key, 3), *heavy), -bound, bound).astype(kind)


def setup_inputs(seed: int = 0) -> dict:
    key_list = jax.random.split(jax.random.key(seed), 15)
    block_input = scatter_about(key_list[0], (MICRO, SEQS, LEN, D), 1.0, 6.0, ((1, 4), (3, 4)))
    segment_ids = jax.vmap(lambda own: jnp.searchsorted(jnp.cumsum(ragged(own, DOCS, LEN, LEN // 2, 2)), jnp.arange(LEN), side="right"))(jax.random.split(key_list[1], MICRO * SEQS)).reshape((MICRO, SEQS, LEN)).astype(jnp.int32)
    group_ids = draw_group_ids(jax.random.fold_in(key_list[14], 71), 0)
    group_weight = jnp.clip(jnp.exp(jax.random.uniform(key_list[3], (GROUPS,), jnp.float32, math.log(0.5), math.log(2.0))), 0.5, 2.0)
    mixer_norm = jnp.clip(1.0 + 0.1 * jax.random.normal(key_list[4], (D,), jnp.float32), 0.5, 1.5).astype(jnp.bfloat16)
    w_mix = scatter_about(key_list[5], (D, 4, KEYS), D ** -0.5, 0.125, ((0, 16), (2, 2)))
    w_beta = scatter_about(key_list[6], (D, HEADS), D ** -0.5, 0.125, ((0, 16), (1, 2)))
    conv_kernel = scatter_about(key_list[7], (3, CONV, KEYS), 0.5, 3.0, ((2, 32),))
    head_norm = jnp.clip(1.0 + 0.1 * jax.random.normal(key_list[8], (HEAD,), jnp.float32), 0.5, 1.5).astype(jnp.bfloat16)
    w_out = scatter_about(key_list[9], (KEYS, D), (KEYS // 2) ** -0.5, 0.1875, ((0, 2), (1, 16)))
    ffn_norm = jnp.clip(1.0 + 0.1 * jax.random.normal(key_list[10], (D,), jnp.float32), 0.5, 1.5).astype(jnp.bfloat16)
    w_ffn_in = scatter_about(key_list[11], (D, 2, FF), D ** -0.5, 0.125, ((0, 16), (2, 2)))
    w_ffn_down = scatter_about(key_list[12], (FF, D), (FF // 2) ** -0.5, 0.109375, ((0, 2), (1, 16)))
    cotangent = bell_draw_with(key_list[13], (MICRO, SEQS, LEN, D), 1.0, 6.0, ((1, 4), (3, 4)), (1, 3, 4, 2.0))
    return {"block_input": block_input, "segment_ids": segment_ids, "group_ids": group_ids, "group_weight": group_weight, "mixer_norm": mixer_norm, "w_mix": w_mix, "w_beta": w_beta, "conv_kernel": conv_kernel, "head_norm": head_norm, "w_out": w_out, "ffn_norm": ffn_norm, "w_ffn_in": w_ffn_in, "w_ffn_down": w_ffn_down, "cotangent": cotangent}


@jax.custom_vjp
def low(v):
    return lax.optimization_barrier(v.astype(jnp.bfloat16)).astype(jnp.float32)

@jax.custom_vjp
def low_back(v):
    return v

def low_keep(v):
    return (low(v), None)

def low_pass(kept, grad):
    return (grad,)

def back_keep(v):
    return (v, None)

def back_low(kept, grad):
    return (low(grad),)
low.defvjp(low_keep, low_pass)
low_back.defvjp(back_keep, back_low)

def matmul_high(left, right):
    return jnp.dot(left.astype(jnp.float32), right.astype(jnp.float32), precision=lax.Precision.HIGHEST, preferred_element_type=jnp.float32)

def short_conv(signal, kernel, segment):
    length = signal.shape[0]
    total = signal * kernel[-1]
    for shift in range(1, kernel.shape[0]):
        moved = jnp.concatenate([jnp.zeros((shift, signal.shape[1]), signal.dtype), signal[:length - shift]], 0)
        earlier = jnp.concatenate([jnp.full((shift,), -1, jnp.int32), segment[:length - shift].astype(jnp.int32)], 0)
        keep = (earlier == segment.astype(jnp.int32)).astype(signal.dtype)
        total = total + moved * keep[:, None] * kernel[-1 - shift]
    return total

def delta_block(carry, inputs):
    state, previous = carry
    query, key, value, beta, segment = inputs
    highest = lax.Precision.HIGHEST
    size = segment.shape[0]
    same = (segment[:, None] == segment[None, :]).astype(query.dtype)
    carried = (segment == previous).astype(query.dtype)
    strict = jnp.tril(jnp.ones((size, size), query.dtype), -1)
    inclusive = jnp.tril(jnp.ones((size, size), query.dtype))
    gram = jnp.einsum('ihd,jhd->hij', key, key, precision=highest)
    system = jnp.eye(size, dtype=query.dtype)[None] + gram * beta.T[:, :, None] * (same * strict)[None]
    recalled = jnp.einsum('hvk,ihk->hiv', state, key, precision=highest) * carried[None, :, None]
    target = beta.T[:, :, None] * (jnp.transpose(value, (1, 0, 2)) - recalled)
    solver = jax.vmap(partial(jax.scipy.linalg.solve_triangular, lower=True, unit_diagonal=True))
    update = solver(system, target)
    scores = jnp.einsum('ihd,jhd->hij', query, key, precision=highest) * (same * inclusive)[None]
    output = jnp.einsum('hvk,ihk->hiv', state, query, precision=highest) * carried[None, :, None]
    output = output + jnp.einsum('hij,hjv->hiv', scores, update, precision=highest)
    last = (segment == segment[-1]).astype(query.dtype)
    state = carried[-1] * state + jnp.einsum('hjv,jhk->hvk', update * last[None, :, None], key, precision=highest)
    return ((state, segment[-1].astype(jnp.int32)), jnp.transpose(output, (1, 0, 2)))

def delta_rule(query, key, value, beta, segment):
    length, heads, size = query.shape
    blocks = length // BLOCK

    def blocked(values):
        return values.reshape((blocks, BLOCK) + values.shape[1:])
    start = (jnp.zeros((heads, size, size), query.dtype), jnp.array(-1, dtype=jnp.int32))
    carry_out, outputs = lax.scan(jax.checkpoint(delta_block), start, (blocked(query), blocked(key), blocked(value), blocked(beta), blocked(segment.astype(jnp.int32))))
    return outputs.reshape(length, heads, size)

def unit_heads(values, heads):
    split_view = values.reshape(values.shape[0], heads, -1)
    return split_view * lax.rsqrt(lax.optimization_barrier(jnp.sum(split_view * split_view, -1, keepdims=True)) + 1e-06)

def block_forward(params, tokens, segment):
    mixer_norm, w_mix, w_beta, conv_kernel, head_norm, w_out, ffn_norm, w_ffn_in, w_ffn_down = params
    highest = lax.Precision.HIGHEST
    heads = w_beta.shape[1]
    size = head_norm.shape[0]
    length = tokens.shape[0]
    mixer_in = low(tokens * lax.rsqrt(lax.optimization_barrier(jnp.mean(tokens * tokens, -1, keepdims=True)) + 1e-06) * mixer_norm)
    projected = low_back(jnp.einsum('td,dck->tck', mixer_in, w_mix, precision=highest))
    beta_in = low_back(matmul_high(mixer_in, w_beta))
    convolved = [jax.nn.silu(short_conv(projected[:, part], conv_kernel[part], segment)) for part in range(3)]
    query = unit_heads(convolved[0], heads) * size ** (-0.5)
    key = unit_heads(convolved[1], heads)
    value = convolved[2].reshape(length, heads, size)
    beta = jax.nn.sigmoid(beta_in)
    mixed = delta_rule(query, key, value, beta, segment)
    normed = mixed * lax.rsqrt(lax.optimization_barrier(jnp.mean(mixed * mixed, -1, keepdims=True)) + 1e-05) * head_norm
    gated = low(normed.reshape(length, -1) * jax.nn.silu(projected[:, 3]))
    branch = low_back(matmul_high(gated, w_out))
    middle = tokens + branch
    ffn_in = low(middle * lax.rsqrt(lax.optimization_barrier(jnp.mean(middle * middle, -1, keepdims=True)) + 1e-06) * ffn_norm)
    gate_up = low_back(jnp.einsum('td,dcf->tcf', ffn_in, w_ffn_in, precision=highest))
    active = low(jax.nn.silu(gate_up[:, 0]) * gate_up[:, 1])
    return middle + low_back(matmul_high(active, w_ffn_down))

def reference(block_input, segment_ids, group_ids, group_weight, mixer_norm, w_mix, w_beta, conv_kernel, head_norm, w_out, ffn_norm, w_ffn_in, w_ffn_down, cotangent):
    groups = group_weight.shape[0]
    marks = (group_ids[..., None] == jnp.arange(groups, dtype=jnp.int32)).astype(jnp.float32)
    counts = lax.optimization_barrier(jnp.sum(marks.reshape(-1, groups), 0))
    table = group_weight.astype(jnp.float32) * (group_ids.size / groups) / counts
    scales = lax.optimization_barrier(jnp.sum(marks * table, -1))
    weights = tuple((item.astype(jnp.float32) for item in (mixer_norm, w_mix, w_beta, conv_kernel, head_norm, w_out, ffn_norm, w_ffn_in, w_ffn_down)))
    tokens_all = block_input.astype(jnp.float32).reshape(-1, LEN, D)
    segments_all = segment_ids.reshape(-1, LEN).astype(jnp.int32)
    directions = (cotangent.astype(jnp.float32) * scales[..., None]).reshape(-1, LEN, D)

    def one_sequence(totals, inputs):
        tokens, segment, direction = inputs

        def forward(params, values):
            return block_forward(params, values, segment)
        output, pullback = jax.vjp(forward, weights, tokens)
        grads, grad_tokens = pullback(direction)
        totals = tuple((left + right for left, right in zip(totals, grads)))
        return (totals, (output.astype(jnp.bfloat16), grad_tokens))
    zeros = tuple((jnp.zeros_like(item) for item in weights))
    totals, (outputs, grad_rows) = lax.scan(one_sequence, zeros, (tokens_all, segments_all, directions))
    return (outputs.reshape(block_input.shape), grad_rows.reshape(block_input.shape), totals[0], totals[1], totals[2], totals[3], totals[4], totals[5], totals[6], totals[7], totals[8])
```

```python
import jax
import jax.numpy as jnp
from jax import lax
from jax.experimental import pallas as pl
from jax.experimental.pallas import tpu as pltpu
from jax.sharding import PartitionSpec as P

D = 2048
HEAD = 128
LOW = jnp.bfloat16
WIDE = jnp.float32
LONGEST_RING = 1
CORE = [(i, i ^ 1) for i in range(4)]
ACROSS = [(i, i ^ 2) for i in range(4)]
SWAP = [(0, 1), (1, 0)]


def halves(values):
    high = values.astype(LOW)
    return high, (values - high.astype(WIDE)).astype(LOW)


def product(left, right, left_dim, right_dim):
    def one(a, b):
        return lax.dot_general(
            a, b, (((left_dim,), (right_dim,)), ((), ())), preferred_element_type=WIDE
        )

    return one(left[0], right[0]) + (one(left[0], right[1]) + one(left[1], right[0]))


def sigmoid(values):
    return 1.0 / (1.0 + jnp.exp(-values))


def masks_of(seg_col, seg_row):
    length = seg_col.shape[0]
    rows = lax.broadcasted_iota(jnp.int32, (length, length), 0)
    cols = lax.broadcasted_iota(jnp.int32, (length, length), 1)
    same = seg_col == seg_row
    return rows, cols, same & (cols < rows), same & (cols <= rows)


def kept_of(seg_col, taps):
    length = seg_col.shape[0]
    wide = jnp.broadcast_to(seg_col, (length, HEAD))
    place = lax.broadcasted_iota(jnp.int32, (length, HEAD), 0)
    return [
        ((pltpu.roll(wide, shift, 0) == wide) & (place >= shift)).astype(WIDE)
        for shift in range(1, taps)
    ]


def convolve(signal, kernel, kept):
    taps = kernel.shape[0]
    total = signal * kernel[taps - 1 : taps]
    for shift in range(1, taps):
        moved = pltpu.roll(signal, shift, 0) * kept[shift - 1]
        total = total + moved * kernel[taps - 1 - shift : taps - shift]
    return total


def invert(lower, rows, cols):
    length = lower.shape[0]
    eye = (rows == cols).astype(WIDE)
    base = -jnp.where((rows // 8) == (cols // 8), lower, 0.0)
    parts = halves(base)
    second = product(parts, parts, 1, 0)
    second_parts = halves(second)
    third = product(parts, second_parts, 1, 0)
    fourth = product(second_parts, second_parts, 1, 0)
    inverse = eye + base + second + third
    inverse = inverse + product(halves(inverse), halves(fourth), 1, 0)
    size = 8
    while size < length:
        cross = ((rows // (2 * size)) == (cols // (2 * size))) & ((rows // size) != (cols // size))
        off = halves(jnp.where(cross, lower, 0.0))
        own = halves(inverse)
        inverse = inverse - product(halves(product(own, off, 1, 0)), own, 1, 0)
        size *= 2
    return inverse


def mixer_forward_kernel(
    first_ref, second_ref, beta_ref, col_ref, row_ref, conv_ref, head_ref,
    gated_ref, inverse_ref, update_ref, mixed_ref,
):
    seg_col = col_ref[...]
    rows, cols, strict, inclusive = masks_of(seg_col, row_ref[0])
    taps = conv_ref.shape[0] // 3
    kept = kept_of(seg_col, taps)
    heads = gated_ref.shape[1] // HEAD
    span = heads * HEAD
    gain = head_ref[...]
    for head in range(heads):
        own = slice(head * HEAD, (head + 1) * HEAD)
        past = slice(span + head * HEAD, span + (head + 1) * HEAD)
        signals = [first_ref[:, own], first_ref[:, past], second_ref[:, own]]
        convolved = []
        for part in range(3):
            pre = convolve(signals[part], conv_ref[part * taps : (part + 1) * taps, own], kept)
            convolved.append(pre * sigmoid(pre))
        query = convolved[0] * (
            lax.rsqrt(jnp.sum(convolved[0] * convolved[0], 1, keepdims=True) + 1e-06) * HEAD**-0.5
        )
        key = convolved[1] * lax.rsqrt(
            jnp.sum(convolved[1] * convolved[1], 1, keepdims=True) + 1e-06
        )
        beta = sigmoid(beta_ref[:, head : head + 1])
        key_parts = halves(key)
        gram = product(key_parts, key_parts, 1, 1)
        inverse = invert(jnp.where(strict, gram * beta, 0.0), rows, cols)
        update = product(halves(inverse), halves(convolved[2] * beta), 1, 0)
        scores = jnp.where(inclusive, product(halves(query), key_parts, 1, 1), 0.0)
        mixed = product(halves(scores), halves(update), 1, 0)
        scale = lax.rsqrt(jnp.sum(mixed * mixed, 1, keepdims=True) * (1.0 / HEAD) + 1e-05)
        gate = second_ref[:, past]
        gated_ref[:, own] = (mixed * scale * gain * (gate * sigmoid(gate))).astype(LOW)
        inverse_ref[0, head] = inverse
        update_ref[:, own] = update
        mixed_ref[:, own] = mixed


def mixer_backward_kernel(
    first_ref, second_ref, beta_ref, col_ref, row_ref, conv_ref, head_ref,
    inverse_ref, update_ref, mixed_ref, grad_ref,
    out_ref, beta_grad_ref, conv_grad_ref, head_grad_ref,
):
    seg_col = col_ref[...]
    rows, cols, strict, inclusive = masks_of(seg_col, row_ref[0])
    length = seg_col.shape[0]
    taps = conv_ref.shape[0] // 3
    kept = kept_of(seg_col, taps)
    heads = grad_ref.shape[1] // HEAD
    span = heads * HEAD
    gain = head_ref[...]
    head_grad = jnp.zeros((1, HEAD), WIDE)
    for head in range(heads):
        own = slice(head * HEAD, (head + 1) * HEAD)
        past = slice(span + head * HEAD, span + (head + 1) * HEAD)
        signals = [first_ref[:, own], first_ref[:, past], second_ref[:, own]]
        before, gates, convolved = [], [], []
        for part in range(3):
            pre = convolve(signals[part], conv_ref[part * taps : (part + 1) * taps, own], kept)
            before.append(pre)
            gates.append(sigmoid(pre))
            convolved.append(pre * gates[part])
        query_unit = lax.rsqrt(jnp.sum(convolved[0] * convolved[0], 1, keepdims=True) + 1e-06)
        key_unit = lax.rsqrt(jnp.sum(convolved[1] * convolved[1], 1, keepdims=True) + 1e-06)
        query = convolved[0] * (query_unit * HEAD**-0.5)
        key = convolved[1] * key_unit
        beta = sigmoid(beta_ref[:, head : head + 1])
        mixed = mixed_ref[:, own]
        update = update_ref[:, own]
        grad = grad_ref[:, own]
        gate = second_ref[:, past]
        gate_sigma = sigmoid(gate)
        opened = gate * gate_sigma
        scale = lax.rsqrt(jnp.sum(mixed * mixed, 1, keepdims=True) * (1.0 / HEAD) + 1e-05)
        normed = mixed * scale
        head_grad = head_grad + jnp.sum(grad * opened * normed, 0, keepdims=True)
        inner = grad * opened * gain
        mixed_grad = scale * inner - mixed * (
            scale * scale * scale * (jnp.sum(inner * mixed, 1, keepdims=True) * (1.0 / HEAD))
        )
        gate_grad = grad * normed * gain * gate_sigma * (1.0 + gate * (1.0 - gate_sigma))
        key_parts = halves(key)
        query_parts = halves(query)
        update_parts = halves(update)
        mixed_parts = halves(mixed_grad)
        gram = product(key_parts, key_parts, 1, 1)
        scores = jnp.where(inclusive, product(query_parts, key_parts, 1, 1), 0.0)
        scores_grad = halves(jnp.where(inclusive, product(mixed_parts, update_parts, 1, 1), 0.0))
        update_grad = product(halves(scores), mixed_parts, 0, 0)
        solved = product(halves(inverse_ref[0, head]), halves(update_grad), 0, 0)
        system_grad = jnp.where(strict, -product(halves(solved), update_parts, 1, 1), 0.0)
        gram_grad = halves(system_grad * beta)
        query_grad = product(scores_grad, key_parts, 1, 0)
        key_grad = (
            product(scores_grad, query_parts, 0, 0)
            + product(gram_grad, key_parts, 1, 0)
            + product(gram_grad, key_parts, 0, 0)
        )
        beta_grad = jnp.sum(system_grad * gram, 1, keepdims=True) + jnp.sum(
            solved * convolved[2], 1, keepdims=True
        )
        beta_grad_ref[:, head : head + 1] = beta_grad * beta * (1.0 - beta)
        conv_grads = [
            HEAD**-0.5
            * (
                query_grad * query_unit
                - convolved[0]
                * (
                    query_unit * query_unit * query_unit
                    * jnp.sum(convolved[0] * query_grad, 1, keepdims=True)
                )
            ),
            key_grad * key_unit
            - convolved[1]
            * (
                key_unit * key_unit * key_unit
                * jnp.sum(convolved[1] * key_grad, 1, keepdims=True)
            ),
            solved * beta,
        ]
        for part in range(3):
            sigma = gates[part]
            error = conv_grads[part] * sigma * (1.0 + before[part] * (1.0 - sigma))
            kernel = conv_ref[part * taps : (part + 1) * taps, own]
            total = error * kernel[taps - 1 : taps]
            line = part * taps + taps - 1
            conv_grad_ref[0, line : line + 1, own] = jnp.sum(
                error * signals[part], 0, keepdims=True
            )
            for shift in range(1, taps):
                held = error * kept[shift - 1]
                line = part * taps + taps - 1 - shift
                conv_grad_ref[0, line : line + 1, own] = jnp.sum(
                    held * pltpu.roll(signals[part], shift, 0), 0, keepdims=True
                )
                total = total + pltpu.roll(held, length - shift, 0) * (
                    kernel[taps - 1 - shift : taps - shift]
                )
            start = part * span + head * HEAD
            out_ref[:, start : start + HEAD] = total.astype(LOW)
        start = 3 * span + head * HEAD
        out_ref[:, start : start + HEAD] = gate_grad.astype(LOW)
    head_grad_ref[0] = head_grad


def mixer_specs(length, span, lines):
    return [
        pl.BlockSpec((length, 2 * span), lambda i: (i, 0)),
        pl.BlockSpec((length, 2 * span), lambda i: (i, 0)),
        pl.BlockSpec((length, span // HEAD), lambda i: (i, 0)),
        pl.BlockSpec((length, 1), lambda i: (i, 0)),
        pl.BlockSpec((1, 1, length), lambda i: (i, 0, 0)),
        pl.BlockSpec((lines, span), lambda i: (0, 0)),
        pl.BlockSpec((1, HEAD), lambda i: (0, 0)),
    ]


def mixer_forward(first, second, beta_in, seg_col, seg_row, conv, head_gain):
    tokens = first.shape[0]
    count, _, length = seg_row.shape
    span = conv.shape[1]
    heads = span // HEAD
    return pl.pallas_call(
        mixer_forward_kernel,
        grid=(count,),
        in_specs=mixer_specs(length, span, conv.shape[0]),
        out_specs=[
            pl.BlockSpec((length, span), lambda i: (i, 0)),
            pl.BlockSpec((1, heads, length, length), lambda i: (i, 0, 0, 0)),
            pl.BlockSpec((length, span), lambda i: (i, 0)),
            pl.BlockSpec((length, span), lambda i: (i, 0)),
        ],
        out_shape=[
            jax.ShapeDtypeStruct((tokens, span), LOW),
            jax.ShapeDtypeStruct((count, heads, length, length), WIDE),
            jax.ShapeDtypeStruct((tokens, span), WIDE),
            jax.ShapeDtypeStruct((tokens, span), WIDE),
        ],
        compiler_params=pltpu.CompilerParams(vmem_limit_bytes=32 << 20),
        cost_estimate=pl.CostEstimate(
            flops=count * heads * 100 * length**3, bytes_accessed=8 << 20, transcendentals=0
        ),
        name="mixer_forward",
    )(first, second, beta_in, seg_col, seg_row, conv, head_gain)


def mixer_backward(first, second, beta_in, seg_col, seg_row, conv, head_gain, saved, grad):
    tokens = first.shape[0]
    count, _, length = seg_row.shape
    lines, span = conv.shape
    heads = span // HEAD
    return pl.pallas_call(
        mixer_backward_kernel,
        grid=(count,),
        in_specs=mixer_specs(length, span, lines)
        + [
            pl.BlockSpec((1, heads, length, length), lambda i: (i, 0, 0, 0)),
            pl.BlockSpec((length, span), lambda i: (i, 0)),
            pl.BlockSpec((length, span), lambda i: (i, 0)),
            pl.BlockSpec((length, span), lambda i: (i, 0)),
        ],
        out_specs=[
            pl.BlockSpec((length, 4 * span), lambda i: (i, 0)),
            pl.BlockSpec((length, heads), lambda i: (i, 0)),
            pl.BlockSpec((1, lines, span), lambda i: (i, 0, 0)),
            pl.BlockSpec((1, 1, HEAD), lambda i: (i, 0, 0)),
        ],
        out_shape=[
            jax.ShapeDtypeStruct((tokens, 4 * span), LOW),
            jax.ShapeDtypeStruct((tokens, heads), WIDE),
            jax.ShapeDtypeStruct((count, lines, span), WIDE),
            jax.ShapeDtypeStruct((count, 1, HEAD), WIDE),
        ],
        compiler_params=pltpu.CompilerParams(vmem_limit_bytes=32 << 20),
        cost_estimate=pl.CostEstimate(
            flops=count * heads * 100 * length**3, bytes_accessed=8 << 20, transcendentals=0
        ),
        name="mixer_backward",
    )(first, second, beta_in, seg_col, seg_row, conv, head_gain, *saved, grad)


def contract(left, right, left_dim, right_dim):
    return lax.dot_general(
        left, right, (((left_dim,), (right_dim,)), ((), ())), preferred_element_type=WIDE
    )


def after(values, earlier):
    return lax.optimization_barrier((values, earlier))[0]


def exclusive_order(blocks):
    place = lax.axis_index("dmod")
    for bit in (1, 2):
        flip = (place & bit) != 0
        blocks = [jnp.where(flip, blocks[i ^ bit], blocks[i]) for i in range(4)]
    return blocks


def trade(blocks):
    return [blocks[0]] + [
        lax.ppermute(blocks[m], "dmod", [(i, i ^ m) for i in range(4)]) for m in (1, 2, 3)
    ]


def gather_width(values):
    far = lax.ppermute(values, "dmod", ACROSS)
    near = lax.ppermute(values, "dmod", CORE)
    return [values, near, far, lax.ppermute(far, "dmod", CORE)]


def scatter_width(blocks):
    near = lax.ppermute(blocks[1].astype(LOW), "dmod", CORE)
    cross = lax.ppermute(blocks[3].astype(LOW), "dmod", CORE)
    far = lax.ppermute((blocks[2] + cross.astype(WIDE)).astype(LOW), "dmod", ACROSS)
    return blocks[0] + near.astype(WIDE) + far.astype(WIDE)


def sum_pair(values):
    low = values.astype(LOW)
    return low.astype(WIDE) + lax.ppermute(low, "mp", SWAP).astype(WIDE)


def row_total(values):
    return lax.psum(values, "dmod")


class Ring:
    def __init__(self):
        self.size = lax.axis_size("dp")
        self.short = self.size <= LONGEST_RING
        self.parts = self.size if self.short else 1
        self.steps = [(i, (i + 1) % self.size) for i in range(self.size)]

    def order(self, values):
        if not self.short:
            return values
        place = lax.axis_index("dp")
        blocks = jnp.split(values, self.size, axis=-1)
        blocks = [blocks[-k % self.size] for k in range(self.size)]
        bit = 1
        while bit < self.size:
            turn = (place & bit) != 0
            blocks = [
                jnp.where(turn, blocks[(k - bit) % self.size], blocks[k]) for k in range(self.size)
            ]
            bit *= 2
        return jnp.concatenate(blocks, -1)

    def gather(self, values):
        if not self.short:
            return [lax.all_gather(values, "dp", axis=1, tiled=True)]
        parts = [values]
        for _ in range(self.size - 1):
            parts.append(lax.ppermute(parts[-1], "dp", self.steps))
        return parts

    def scatter(self, make):
        if not self.short:
            return lax.psum_scatter(
                make(0).astype(LOW), "dp", scatter_dimension=1, tiled=True
            ).astype(WIDE)
        total = make(1)
        for k in range(2, self.size + 1):
            total = lax.ppermute(total.astype(LOW), "dp", self.steps).astype(WIDE) + make(
                k % self.size
            )
        return total


def body(
    block_input,
    segment_ids,
    group_ids,
    group_weight,
    mixer_norm,
    w_mix,
    w_beta,
    conv_kernel,
    head_norm,
    w_out,
    ffn_norm,
    w_ffn_in,
    w_ffn_down,
    cotangent,
):
    ring = Ring()
    parts = ring.parts
    micro, seqs, length, width = block_input.shape
    tokens = micro * seqs * length
    block = width // parts
    strip = w_mix.shape[0]
    span = w_mix.shape[2] // 4
    hidden = w_ffn_in.shape[2] // 4
    dmod = lax.axis_index("dmod")
    data_size = ring.size
    place = lax.axis_index("dp")

    lines = conv_kernel.shape[0] * conv_kernel.shape[1]
    pack = jnp.concatenate(
        [
            conv_kernel.reshape(-1),
            head_norm,
            mixer_norm,
            ffn_norm,
            w_beta.T.reshape(-1),
        ]
    )
    packs = lax.all_gather(pack, "dp", axis=0)
    sizes = [conv_kernel.size, head_norm.size, strip, strip, w_beta.size]
    cuts = [sum(sizes[:i]) for i in range(6)]
    conv = (
        packs[:, cuts[0] : cuts[1]]
        .reshape(data_size, lines, -1)
        .transpose(1, 0, 2)
        .reshape(lines, span)
        .astype(WIDE)
    )
    head_gain = packs[:, cuts[1] : cuts[2]].reshape(1, -1).astype(WIDE)
    gain_one = ring.order(packs[:, cuts[2] : cuts[3]].reshape(1, -1).astype(WIDE))
    gain_two = ring.order(packs[:, cuts[3] : cuts[4]].reshape(1, -1).astype(WIDE))
    beta_weights = ring.order(
        packs[:, cuts[4] : cuts[5]]
        .reshape(data_size, -1, strip)
        .transpose(1, 0, 2)
        .reshape(-1, width)
    )

    out_rows = jnp.concatenate(exclusive_order(jnp.split(w_out, 4, axis=0)), 0)
    out_halves = jnp.split(out_rows.T, 2, axis=1)
    mix_own = jnp.stack(trade(exclusive_order(jnp.split(w_mix, 4, axis=2))))
    mix_halves = [
        mix_own[:, :, :2].reshape(4, strip, 2 * span),
        mix_own[:, :, 2:].reshape(4, strip, 2 * span),
    ]
    ffn_own = jnp.stack(trade(exclusive_order(jnp.split(w_ffn_in, 4, axis=2))))
    ffn_halves = [ffn_own[:, :, 0], ffn_own[:, :, 1]]
    down_own = trade(exclusive_order(jnp.split(w_ffn_down, 4, axis=0)))
    down_halves = [
        jnp.stack([down_own[0].T, down_own[1].T]),
        jnp.stack([down_own[2].T, down_own[3].T]),
    ]

    def chain(half):
        first = ring.gather(out_halves[half][None])
        second = ring.gather(after(mix_halves[half], first[-1]))
        third = ring.gather(after(ffn_halves[half], second[-1]))
        fourth = ring.gather(after(down_halves[half], third[-1]))
        return first, second, third, fourth

    chains = [chain(0), chain(1)]
    out_weights = jnp.concatenate(
        [
            jnp.concatenate([part[0] for part in chains[0][0]], 0),
            jnp.concatenate([part[0] for part in chains[1][0]], 0),
        ],
        1,
    )
    mix_parts = [[part.reshape(4 * block, -1) for part in each[1]] for each in chains]
    ffn_parts = [[part.reshape(4 * block, -1) for part in each[2]] for each in chains]
    down_parts = [[part.reshape(2 * block, -1) for part in each[3]] for each in chains]

    marks = (group_ids.reshape(tokens, 1) == jnp.arange(group_weight.shape[0])[None]).astype(WIDE)
    counts = lax.psum(jnp.sum(marks, 0), "dp")
    table = group_weight * (tokens * data_size / group_weight.shape[0]) / counts
    scales = jnp.sum(marks * table, -1, keepdims=True)
    direction = ring.order(cotangent.reshape(tokens, width).astype(WIDE)) * scales
    direction_low = direction.astype(LOW)

    def by_part(slots):
        return [
            jnp.concatenate([slot[:, k * block : (k + 1) * block] for slot in slots], 1)
            for k in range(parts)
        ]

    def by_slot(pieces):
        return [
            jnp.concatenate([piece[:, m * block : (m + 1) * block] for piece in pieces], 1)
            for m in range(pieces[0].shape[1] // block)
        ]

    direction_parts = by_part(gather_width(direction_low))

    rows = ring.order(block_input.reshape(tokens, width).astype(WIDE))
    first_scale = lax.rsqrt(row_total(jnp.sum(rows * rows, -1, keepdims=True)) / D + 1e-06)
    mixer_in = (rows * first_scale * gain_one).astype(LOW)
    mixer_parts = by_part(gather_width(mixer_in))
    projected = [
        sum(jnp.dot(mixer_parts[k], mix_parts[half][k], preferred_element_type=WIDE) for k in range(parts))
        for half in (0, 1)
    ]
    beta_all = row_total(contract(beta_weights, mixer_in, 1, 1))
    heads = span // HEAD
    beta_in = lax.dynamic_slice_in_dim(beta_all, dmod * heads, heads, 0).T
    seg_col = segment_ids.reshape(tokens, 1)
    seg_row = segment_ids.reshape(micro * seqs, 1, length)
    mixer_args = (projected[0], projected[1], beta_in, seg_col, seg_row, conv, head_gain)
    gated, *saved = mixer_forward(*mixer_args)
    gated_all = jnp.concatenate(gather_width(gated), 1)
    middle = rows + sum_pair(contract(gated_all, out_weights, 1, 1))

    second_scale = lax.rsqrt(row_total(jnp.sum(middle * middle, -1, keepdims=True)) / D + 1e-06)
    ffn_in = (middle * second_scale * gain_two).astype(LOW)
    ffn_in_parts = by_part(gather_width(ffn_in))
    gate, upward = (
        sum(jnp.dot(ffn_in_parts[k], ffn_parts[half][k], preferred_element_type=WIDE) for k in range(parts))
        for half in (0, 1)
    )
    sigma = sigmoid(gate)
    active = (gate * sigma * upward).astype(LOW)
    down_slots = sum(
        (
            by_slot([contract(active, down_parts[half][k], 1, 1) for k in range(parts)])
            for half in (0, 1)
        ),
        [],
    )
    result = middle + sum_pair(scatter_width(down_slots))
    out = ring.order(result).astype(LOW).reshape(block_input.shape)

    down_grads = [
        ring.scatter(
            lambda k: contract(
                direction_parts[k][:, 2 * half * block : 2 * (half + 1) * block], active, 0, 0
            ).reshape(2, block, hidden)
        )
        for half in (0, 1)
    ]
    active_grad = sum(
        jnp.dot(
            direction_parts[k][:, 2 * half * block : 2 * (half + 1) * block],
            down_parts[half][k],
            preferred_element_type=WIDE,
        )
        for k in range(parts)
        for half in (0, 1)
    )
    gate_grad = (active_grad * upward * sigma * (1.0 + gate * (1.0 - sigma))).astype(LOW)
    upward_grad = (active_grad * gate * sigma).astype(LOW)
    ffn_slots = by_slot(
        [
            contract(gate_grad, ffn_parts[0][k], 1, 1) + contract(upward_grad, ffn_parts[1][k], 1, 1)
            for k in range(parts)
        ]
    )
    ffn_grads = [
        ring.scatter(lambda k: contract(ffn_in_parts[k], grad, 0, 0).reshape(4, block, hidden))
        for grad in (gate_grad, upward_grad)
    ]
    ffn_in_grad = sum_pair(scatter_width(ffn_slots))
    weighted_two = ffn_in_grad * gain_two
    norm_two_grad = jnp.sum(ffn_in_grad * middle * second_scale, 0)
    inner_two = row_total(jnp.sum(weighted_two * middle, -1, keepdims=True))
    middle_grad = (
        direction + second_scale * weighted_two - middle * (second_scale**3 * inner_two / D)
    )

    branch_low = middle_grad.astype(LOW)
    out_grads = [
        ring.scatter(
            lambda k: contract(
                branch_low[:, k * block : (k + 1) * block],
                gated_all[:, 2 * half * span : 2 * (half + 1) * span],
                0,
                0,
            )[None]
        )
        for half in (0, 1)
    ]
    gated_slots = jnp.split(jnp.dot(branch_low, out_weights, preferred_element_type=WIDE), 4, axis=1)
    gated_grad = scatter_width(gated_slots)
    projected_grad, beta_grad, conv_grad, head_grad = mixer_backward(
        *mixer_args, saved, gated_grad
    )
    projected_slots = gather_width(projected_grad)
    mix_grads = [
        ring.scatter(
            lambda k: contract(
                mixer_in[:, k * block : (k + 1) * block],
                jnp.concatenate(projected_slots[2 * half : 2 * half + 2], 1),
                0,
                0,
            )[None]
        )
        for half in (0, 1)
    ]
    beta_slots = jnp.concatenate(
        exclusive_order(gather_width(beta_grad.T.astype(LOW))), 0
    )
    beta_weight_grad = contract(beta_slots, mixer_in, 1, 0)
    mixer_slots = by_slot(
        [
            contract(projected_grad[:, : 2 * span], mix_parts[0][k], 1, 1)
            + contract(projected_grad[:, 2 * span :], mix_parts[1][k], 1, 1)
            for k in range(parts)
        ]
    )
    mixer_grad = sum_pair(scatter_width(mixer_slots) + contract(beta_slots, beta_weights, 0, 0))
    weighted_one = mixer_grad * gain_one
    norm_one_grad = jnp.sum(mixer_grad * rows * first_scale, 0)
    inner_one = row_total(jnp.sum(weighted_one * rows, -1, keepdims=True))
    grad_input = ring.order(
        middle_grad + first_scale * weighted_one - rows * (first_scale**3 * inner_one / D)
    ).reshape(block_input.shape)

    head_total = lax.psum(jnp.sum(head_grad, (0, 1)), ("dp", "mp", "dmod"))
    head_out = lax.dynamic_slice_in_dim(head_total, place * head_norm.size, head_norm.size, 0)
    small = jnp.concatenate(
        [
            jnp.sum(conv_grad, 0),
            ring.order(jnp.stack([norm_one_grad, norm_two_grad]))
            .reshape(2, data_size, -1)
            .transpose(1, 0, 2)
            .reshape(data_size, -1)
            .reshape(-1)
            .reshape(-1, span),
            ring.order(beta_weight_grad)
            .reshape(-1, data_size, strip)
            .transpose(1, 0, 2)
            .reshape(-1, span),
        ],
        0,
    )
    conv_part = (
        small[:lines].reshape(lines, data_size, -1).transpose(1, 0, 2).reshape(data_size, -1)
    )
    norm_part = small[lines : lines + 2 * width // span].reshape(data_size, -1)
    beta_part = small[lines + 2 * width // span :].reshape(data_size, -1)
    small_own = lax.psum_scatter(
        jnp.concatenate([conv_part, norm_part, beta_part], 1), "dp", scatter_dimension=0
    )
    conv_out = small_own[: conv_kernel.size].reshape(conv_kernel.shape)
    norm_one_out = small_own[conv_kernel.size : conv_kernel.size + strip]
    norm_two_out = small_own[conv_kernel.size + strip : conv_kernel.size + 2 * strip]
    beta_out = small_own[conv_kernel.size + 2 * strip :].reshape(-1, strip).T

    def placed(blocks):
        return exclusive_order(trade([values.astype(LOW) for values in blocks]))

    ffn_out = jnp.stack(
        [
            jnp.concatenate([values.astype(WIDE) for values in placed(list(grad))], 1)
            for grad in ffn_grads
        ],
        1,
    )
    down_out = jnp.concatenate(
        [
            values.astype(WIDE).T
            for values in placed(list(down_grads[0]) + list(down_grads[1]))
        ],
        0,
    )
    out_out = jnp.concatenate(
        exclusive_order(jnp.split(jnp.concatenate([grad[0] for grad in out_grads], 1).T, 4, axis=0)),
        0,
    )
    mix_blocks = sum((jnp.split(grad[0], 2, axis=1) for grad in mix_grads), [])
    mix_out = jnp.concatenate(
        [values.reshape(strip, 4, span) for values in exclusive_order(mix_blocks)], 2
    )
    return (
        out,
        grad_input,
        norm_one_out,
        mix_out,
        beta_out,
        conv_out,
        head_out,
        out_out,
        norm_two_out,
        ffn_out,
        down_out,
    )


def solution(mesh):
    wide = P(("dmod", "dp"))
    tokens = P(None, "dp", None, "dmod")
    weights = (
        wide,
        P(("dmod", "dp"), None, "mp"),
        P(("dmod", "dp"), "mp"),
        P(None, None, ("mp", "dmod", "dp")),
        P("dp"),
        P("mp", ("dmod", "dp")),
        wide,
        P(("dmod", "dp"), None, "mp"),
        P("mp", ("dmod", "dp")),
    )
    ids = P(None, "dp", None)
    return jax.shard_map(
        body,
        mesh=mesh,
        in_specs=(tokens, ids, ids, P()) + weights + (tokens,),
        out_specs=(tokens, tokens) + weights,
        check_vma=False,
    )
```

```python
import jax
import jax.numpy as jnp
from jax import lax
from jax.experimental import pallas as pl
from jax.experimental.pallas import tpu as pltpu
from jax.sharding import PartitionSpec as P

D = 2048
HEAD = 128
LOW = jnp.bfloat16
WIDE = jnp.float32
LONGEST_RING = 1
CORE = [(i, i ^ 1) for i in range(4)]
ACROSS = [(i, i ^ 2) for i in range(4)]
SWAP = [(0, 1), (1, 0)]


def halves(values):
    high = values.astype(LOW)
    return high, (values - high.astype(WIDE)).astype(LOW)


def product(left, right, left_dim, right_dim):
    def one(a, b):
        return lax.dot_general(
            a, b, (((left_dim,), (right_dim,)), ((), ())), preferred_element_type=WIDE
        )

    return one(left[0], right[0]) + (one(left[0], right[1]) + one(left[1], right[0]))


def sigmoid(values):
    return 1.0 / (1.0 + jnp.exp(-values))


def masks_of(seg_col, seg_row):
    length = seg_col.shape[0]
    rows = lax.broadcasted_iota(jnp.int32, (length, length), 0)
    cols = lax.broadcasted_iota(jnp.int32, (length, length), 1)
    same = seg_col == seg_row
    return rows, cols, same & (cols < rows), same & (cols <= rows)


def kept_of(seg_col, taps):
    length = seg_col.shape[0]
    wide = jnp.broadcast_to(seg_col, (length, HEAD))
    place = lax.broadcasted_iota(jnp.int32, (length, HEAD), 0)
    return [
        ((pltpu.roll(wide, shift, 0) == wide) & (place >= shift)).astype(WIDE)
        for shift in range(1, taps)
    ]


def convolve(signal, kernel, kept):
    taps = kernel.shape[0]
    total = signal * kernel[taps - 1 : taps]
    for shift in range(1, taps):
        moved = pltpu.roll(signal, shift, 0) * kept[shift - 1]
        total = total + moved * kernel[taps - 1 - shift : taps - shift]
    return total


def blocks_of(order_ref, length):
    count = order_ref.shape[0]
    share = length // count
    return [pl.ds(pl.multiple_of(order_ref[j] * share, share), share) for j in range(count)]


def single(left, right):
    return lax.dot_general(
        left.astype(LOW),
        right.astype(LOW),
        (((1,), (0,)), ((), ())),
        preferred_element_type=WIDE,
    )


def invert(lower, rows, cols):
    length = lower.shape[0]
    eye = (rows == cols).astype(WIDE)
    inverse = eye - jnp.where((rows // 2) == (cols // 2), lower, 0.0)
    size = 2
    while size < length:
        cross = ((rows // (2 * size)) == (cols // (2 * size))) & ((rows // size) != (cols // size))
        inverse = inverse - single(single(inverse, jnp.where(cross, lower, 0.0)), inverse)
        size *= 2
    rest = eye - inverse - product(halves(lower), halves(inverse), 1, 0)
    return inverse + single(inverse, rest)


def forward_head(signals, beta_in, conv, kept, masks, gain):
    rows, cols, strict, inclusive = masks
    taps = conv.shape[0] // 3
    convolved = []
    for part in range(3):
        pre = convolve(signals[part], conv[part * taps : (part + 1) * taps], kept)
        convolved.append(pre * sigmoid(pre))
    query = convolved[0] * (
        lax.rsqrt(jnp.sum(convolved[0] * convolved[0], 1, keepdims=True) + 1e-06) * HEAD**-0.5
    )
    key = convolved[1] * lax.rsqrt(
        jnp.sum(convolved[1] * convolved[1], 1, keepdims=True) + 1e-06
    )
    beta = sigmoid(beta_in)
    key_parts = halves(key)
    gram = product(key_parts, key_parts, 1, 1)
    inverse = invert(jnp.where(strict, gram * beta, 0.0), rows, cols)
    update = product(halves(inverse), halves(convolved[2] * beta), 1, 0)
    scores = jnp.where(inclusive, product(halves(query), key_parts, 1, 1), 0.0)
    mixed = product(halves(scores), halves(update), 1, 0)
    scale = lax.rsqrt(jnp.sum(mixed * mixed, 1, keepdims=True) * (1.0 / HEAD) + 1e-05)
    gate = signals[3]
    gated = (mixed * scale * gain * (gate * sigmoid(gate))).astype(LOW)
    return gated, inverse, update, mixed


def backward_head(signals, beta_in, conv, kept, masks, gain, inverse, update, mixed, grad):
    rows, cols, strict, inclusive = masks
    length = grad.shape[0]
    taps = conv.shape[0] // 3
    before, gates, convolved = [], [], []
    for part in range(3):
        pre = convolve(signals[part], conv[part * taps : (part + 1) * taps], kept)
        before.append(pre)
        gates.append(sigmoid(pre))
        convolved.append(pre * gates[part])
    query_unit = lax.rsqrt(jnp.sum(convolved[0] * convolved[0], 1, keepdims=True) + 1e-06)
    key_unit = lax.rsqrt(jnp.sum(convolved[1] * convolved[1], 1, keepdims=True) + 1e-06)
    query = convolved[0] * (query_unit * HEAD**-0.5)
    key = convolved[1] * key_unit
    beta = sigmoid(beta_in)
    gate = signals[3]
    gate_sigma = sigmoid(gate)
    opened = gate * gate_sigma
    scale = lax.rsqrt(jnp.sum(mixed * mixed, 1, keepdims=True) * (1.0 / HEAD) + 1e-05)
    normed = mixed * scale
    head_grad = jnp.sum(grad * opened * normed, 0, keepdims=True)
    inner = grad * opened * gain
    mixed_grad = scale * inner - mixed * (
        scale * scale * scale * (jnp.sum(inner * mixed, 1, keepdims=True) * (1.0 / HEAD))
    )
    gate_grad = grad * normed * gain * gate_sigma * (1.0 + gate * (1.0 - gate_sigma))
    key_parts = halves(key)
    query_parts = halves(query)
    update_parts = halves(update)
    mixed_parts = halves(mixed_grad)
    gram = product(key_parts, key_parts, 1, 1)
    scores = jnp.where(inclusive, product(query_parts, key_parts, 1, 1), 0.0)
    scores_grad = halves(jnp.where(inclusive, product(mixed_parts, update_parts, 1, 1), 0.0))
    update_grad = product(halves(scores), mixed_parts, 0, 0)
    solved = product(halves(inverse), halves(update_grad), 0, 0)
    system_grad = jnp.where(strict, -product(halves(solved), update_parts, 1, 1), 0.0)
    gram_grad = halves(system_grad * beta)
    query_grad = product(scores_grad, key_parts, 1, 0)
    key_grad = (
        product(scores_grad, query_parts, 0, 0)
        + product(gram_grad, key_parts, 1, 0)
        + product(gram_grad, key_parts, 0, 0)
    )
    beta_grad = jnp.sum(system_grad * gram, 1, keepdims=True) + jnp.sum(
        solved * convolved[2], 1, keepdims=True
    )
    beta_grad = beta_grad * beta * (1.0 - beta)
    conv_grads = [
        HEAD**-0.5
        * (
            query_grad * query_unit
            - convolved[0]
            * (
                query_unit
                * query_unit
                * query_unit
                * jnp.sum(convolved[0] * query_grad, 1, keepdims=True)
            )
        ),
        key_grad * key_unit
        - convolved[1]
        * (key_unit * key_unit * key_unit * jnp.sum(convolved[1] * key_grad, 1, keepdims=True)),
        solved * beta,
    ]
    lines = [None] * (3 * taps)
    signal_grads = []
    for part in range(3):
        sigma = gates[part]
        error = conv_grads[part] * sigma * (1.0 + before[part] * (1.0 - sigma))
        kernel = conv[part * taps : (part + 1) * taps]
        total = error * kernel[taps - 1 : taps]
        last = part * taps + taps - 1
        lines[last] = jnp.sum(error * signals[part], 0, keepdims=True)
        for shift in range(1, taps):
            held = error * kept[shift - 1]
            lines[last - shift] = jnp.sum(
                held * pltpu.roll(signals[part], shift, 0), 0, keepdims=True
            )
            total = total + pltpu.roll(held, length - shift, 0) * (
                kernel[taps - 1 - shift : taps - shift]
            )
        signal_grads.append(total.astype(LOW))
    signal_grads.append(gate_grad.astype(LOW))
    return signal_grads, beta_grad, lines, head_grad


def head_lanes(head):
    return slice(head * HEAD, (head + 1) * HEAD)


def mixer_forward_kernel(*refs):
    parts = refs[:2]
    beta_ref, col_ref, row_ref, conv_ref, head_ref = refs[2:7]
    gated_ref, inverse_ref, update_ref, mixed_ref = refs[7:]
    masks = masks_of(col_ref[...], row_ref[0])
    kept = kept_of(col_ref[...], conv_ref.shape[0] // 3)
    for head in range(2):
        own = head_lanes(head)
        gated_ref[:, own], inverse_ref[0, head], update_ref[:, own], mixed_ref[:, own] = (
            forward_head(
                [parts[head][:, head_lanes(part)] for part in range(4)],
                beta_ref[:, head : head + 1],
                conv_ref[:, own],
                kept,
                masks,
                head_ref[...],
            )
        )


def mixer_backward_kernel(*refs):
    parts = refs[:2]
    beta_ref, col_ref, row_ref, conv_ref, head_ref = refs[2:7]
    inverse_ref, update_ref, mixed_ref, grad_ref = refs[7:11]
    out_ref, beta_grad_ref, conv_grad_ref, head_grad_ref = refs[11:]
    masks = masks_of(col_ref[...], row_ref[0])
    kept = kept_of(col_ref[...], conv_ref.shape[0] // 3)
    head_grad = jnp.zeros((1, HEAD), WIDE)
    for head in range(2):
        own = head_lanes(head)
        grads, beta_grad, lines, gain_grad = backward_head(
            [parts[head][:, head_lanes(part)] for part in range(4)],
            beta_ref[:, head : head + 1],
            conv_ref[:, own],
            kept,
            masks,
            head_ref[...],
            inverse_ref[0, head],
            update_ref[:, own],
            mixed_ref[:, own],
            grad_ref[:, own],
        )
        head_grad = head_grad + gain_grad
        beta_grad_ref[:, head : head + 1] = beta_grad
        for line, values in enumerate(lines):
            conv_grad_ref[0, line : line + 1, own] = values
        for part in range(4):
            out_ref[:, head_lanes(4 * head + part)] = grads[part]
    head_grad_ref[0] = head_grad


def mixer_specs(length, lines):
    part = pl.BlockSpec((length, 4 * HEAD), lambda i: (i, 0))
    return [
        part,
        part,
        pl.BlockSpec((length, 2), lambda i: (i, 0)),
        pl.BlockSpec((length, 1), lambda i: (i, 0)),
        pl.BlockSpec((1, 1, length), lambda i: (i, 0, 0)),
        pl.BlockSpec((lines, 2 * HEAD), lambda i: (0, 0)),
        pl.BlockSpec((1, HEAD), lambda i: (0, 0)),
    ]


def saved_specs(length):
    return [
        pl.BlockSpec((1, 2, length, length), lambda i: (i, 0, 0, 0)),
        pl.BlockSpec((length, 2 * HEAD), lambda i: (i, 0)),
        pl.BlockSpec((length, 2 * HEAD), lambda i: (i, 0)),
    ]


def saved_shapes(count, length):
    return [
        jax.ShapeDtypeStruct((count, 2, length, length), WIDE),
        jax.ShapeDtypeStruct((count * length, 2 * HEAD), WIDE),
        jax.ShapeDtypeStruct((count * length, 2 * HEAD), WIDE),
    ]


def grad_specs(length, lines):
    return [
        pl.BlockSpec((length, 8 * HEAD), lambda i: (i, 0)),
        pl.BlockSpec((length, 2), lambda i: (i, 0)),
        pl.BlockSpec((1, lines, 2 * HEAD), lambda i: (i, 0, 0)),
        pl.BlockSpec((1, 1, HEAD), lambda i: (i, 0, 0)),
    ]


def grad_shapes(count, length, lines):
    return [
        jax.ShapeDtypeStruct((count * length, 8 * HEAD), LOW),
        jax.ShapeDtypeStruct((count * length, 2), WIDE),
        jax.ShapeDtypeStruct((count, lines, 2 * HEAD), WIDE),
        jax.ShapeDtypeStruct((count, 1, HEAD), WIDE),
    ]


def mixer_forward(inputs):
    count, _, length = inputs[4].shape
    return pl.pallas_call(
        mixer_forward_kernel,
        grid=(count,),
        in_specs=mixer_specs(length, inputs[5].shape[0]),
        out_specs=[pl.BlockSpec((length, 2 * HEAD), lambda i: (i, 0))] + saved_specs(length),
        out_shape=[jax.ShapeDtypeStruct((count * length, 2 * HEAD), LOW)]
        + saved_shapes(count, length),
        compiler_params=pltpu.CompilerParams(vmem_limit_bytes=32 << 20),
        name="mixer_forward",
    )(*inputs)


def mixer_backward(inputs, saved, grad):
    count, _, length = inputs[4].shape
    lines = inputs[5].shape[0]
    return pl.pallas_call(
        mixer_backward_kernel,
        grid=(count,),
        in_specs=mixer_specs(length, lines)
        + saved_specs(length)
        + [pl.BlockSpec((length, 2 * HEAD), lambda i: (i, 0))],
        out_specs=grad_specs(length, lines),
        out_shape=grad_shapes(count, length, lines),
        compiler_params=pltpu.CompilerParams(vmem_limit_bytes=32 << 20),
        name="mixer_backward",
    )(*inputs, *saved, grad)


def across(refs, rows):
    return jnp.concatenate(
        [ref[z, c, rows] for ref in refs for z in range(ref.shape[0]) for c in range(2)], 1
    )


def down_list(refs):
    return jnp.concatenate([ref[...] for ref in refs], 0)


def turned(left, right):
    return lax.dot_general(
        left, right, (((0,), (0,)), ((), ())), preferred_element_type=WIDE
    )


def straight(left, right):
    return lax.dot_general(
        left, right, (((1,), (0,)), ((), ())), preferred_element_type=WIDE
    )


def crossed(left, right):
    return lax.dot_general(
        left, right, (((1,), (1,)), ((), ())), preferred_element_type=WIDE
    )


def collect(token_refs, hold_ref, place_refs):
    half = len(token_refs) // 2
    for step in range(2):

        @pl.when(pl.program_id(0) == step)
        def _():
            for k in range(half):
                hold_ref[place_refs[k], :] = token_refs[step * half + k][...]


def deal(near_ref, far_ref, values, places, lanes):
    share = values.shape[0] // len(places)
    for step, ref in enumerate((near_ref, far_ref)):

        @pl.when(pl.program_id(0) == step)
        def _():
            for j, place in enumerate(places):
                ref[place, lanes] = values[j * share : (j + 1) * share].astype(LOW)


def whole(values):
    rank = len(values.shape)
    return pl.BlockSpec(values.shape, lambda i: (0,) * rank)


def split_refs(refs, sizes):
    out, start = [], 0
    for size in sizes:
        out.append(refs[start : start + size])
        start += size
    return out


def flat(grid):
    return [item for pair in grid for items in pair for item in items]


def nested(refs, lengths):
    flat_lists = split_refs(refs, [n for pair in lengths for n in pair])
    return [flat_lists[:2], flat_lists[2:]]


def lengths_of(grid):
    return [[len(items) for items in pair] for pair in grid]


def call(kernel, inputs, in_specs, out_specs, out_shape, scratch, name, grid=2, work=20):
    return pl.pallas_call(
        kernel,
        grid=(grid,),
        in_specs=in_specs,
        out_specs=out_specs,
        out_shape=out_shape,
        scratch_shapes=scratch,
        compiler_params=pltpu.CompilerParams(vmem_limit_bytes=48 << 20),
        cost_estimate=pl.CostEstimate(
            flops=work * 10**9, bytes_accessed=8 << 20, transcendentals=0
        ),
        name=name,
    )(*inputs)


def column_forward(tokens, weights, gain, beta_weights, seg_col, seg_row, conv, head_gain, order):
    count, _, length = seg_row.shape
    width = tokens[0].shape[1]
    lengths = lengths_of(weights)
    pieces = flat(weights)

    def kernel(*refs):
        token_refs, weight_refs, rest = split_refs(refs, [len(tokens), len(pieces), 18])
        gain_ref, beta_ref, col_ref, row_ref, conv_ref, head_ref, order_ref = rest[:7]
        gated_ref, inverse_ref, update_ref, mixed_ref = rest[7:11]
        mixer_ref, first_ref, second_ref, beta_in_ref, hold_ref = rest[11:]
        weight_refs = nested(weight_refs, lengths)
        collect(token_refs, hold_ref, blocks_of(order_ref, length))
        values = hold_ref[...].astype(WIDE)
        scale = lax.rsqrt(jnp.sum(values * values, 1, keepdims=True) * (1.0 / D) + 1e-06)
        mixer_ref[...] = (values * scale * gain_ref[...]).astype(LOW)
        masks = masks_of(col_ref[...], row_ref[0])
        kept = kept_of(col_ref[...], conv_ref.shape[0] // 3)
        mixer_in = mixer_ref[...].astype(WIDE)
        half = width // 2
        for head, projected_ref in enumerate((first_ref, second_ref)):
            own = head_lanes(head)
            projected_ref[...] = straight(
                mixer_ref[:, :half], down_list(weight_refs[head][0])
            ) + straight(mixer_ref[:, half:], down_list(weight_refs[head][1]))
            beta_in = jnp.sum(
                mixer_in * beta_ref[head : head + 1, :].astype(WIDE), 1, keepdims=True
            )
            beta_in_ref[:, head : head + 1] = beta_in
            gated_ref[:, own], inverse_ref[0, head], update_ref[:, own], mixed_ref[:, own] = (
                forward_head(
                    [projected_ref[:, head_lanes(part)] for part in range(4)],
                    beta_in,
                    conv_ref[:, own],
                    kept,
                    masks,
                    head_ref[...],
                )
            )

    inputs = list(tokens) + pieces + [
        gain, beta_weights, seg_col, seg_row, conv, head_gain, order
    ]
    in_specs = [whole(item) for item in inputs]
    in_specs[-5] = pl.BlockSpec((length, 1), lambda i: (i, 0))
    in_specs[-4] = pl.BlockSpec((1, 1, length), lambda i: (i, 0, 0))
    in_specs[-1] = pl.BlockSpec(memory_space=pltpu.SMEM)
    step = lambda lanes: pl.BlockSpec((length, lanes), lambda i: (i, 0))
    shape = lambda lanes, kind: jax.ShapeDtypeStruct((count * length, lanes), kind)
    return call(
        kernel,
        inputs,
        in_specs,
        [step(2 * HEAD)]
        + saved_specs(length)
        + [step(width), step(4 * HEAD), step(4 * HEAD), step(2)],
        [shape(2 * HEAD, LOW)]
        + saved_shapes(count, length)
        + [shape(width, LOW), shape(4 * HEAD, WIDE), shape(4 * HEAD, WIDE), shape(2, WIDE)],
        [pltpu.VMEM((length, width), LOW)],
        "column_forward",
    )


def column_branch(gated, weights, order, length):
    lengths = lengths_of(weights)
    pieces = flat(weights)
    width = 2 * sum(item.shape[0] * 2 * item.shape[3] for item in weights[0][0])

    def kernel(*refs):
        gated_ref, weight_refs, rest = refs[0], nested(refs[1 : 1 + len(pieces)], lengths), refs[-3:]
        order_ref, near_ref, far_ref = rest
        places = blocks_of(order_ref, length)
        half = width // 2
        for far in range(2):
            values = straight(
                gated_ref[:, :HEAD], across(weight_refs[0][far], slice(None))
            ) + straight(gated_ref[:, HEAD:], across(weight_refs[1][far], slice(None)))
            deal(near_ref, far_ref, values, places, slice(far * half, (far + 1) * half))

    inputs = [gated] + pieces + [order]
    in_specs = [whole(item) for item in inputs]
    in_specs[0] = pl.BlockSpec((length, 2 * HEAD), lambda i: (i, 0))
    in_specs[-1] = pl.BlockSpec(memory_space=pltpu.SMEM)
    out = jax.ShapeDtypeStruct((length, width), LOW)
    return call(kernel, inputs, in_specs, [whole(out)] * 2, [out] * 2, [], "column_branch", work=2)


def column_ffn(tokens, directions, first, down, hidden):
    share, width = tokens[0].shape
    length = share * len(tokens) // 2
    lengths = [lengths_of(first), lengths_of(down)]
    pieces = [flat(first), flat(down)]
    gate_rows, up_rows = slice(0, hidden), slice(hidden, 2 * hidden)

    def kernel(*refs):
        token_refs, way_refs, first_refs, down_refs, rest = split_refs(
            refs, [len(tokens), len(tokens), len(pieces[0]), len(pieces[1]), 10]
        )
        first_refs, down_refs = nested(first_refs, lengths[0]), nested(down_refs, lengths[1])
        near_ref, far_ref, token_ref, way_ref = rest[:4]
        active_refs, gate_refs, up_refs = rest[4:6], rest[6:8], rest[8:10]
        half = width // 2
        order = [pl.ds(k * share, share) for k in range(len(tokens) // 2)]
        collect(token_refs, token_ref, order)
        collect(way_refs, way_ref, order)
        lanes = [slice(0, half), slice(half, width)]
        for i in range(2):
            gate, upward = (
                sum(
                    crossed(token_ref[:, lanes[far]], across(first_refs[i][far], rows))
                    for far in range(2)
                )
                for rows in (gate_rows, up_rows)
            )
            sigma = sigmoid(gate)
            opened = gate * sigma
            active_refs[i][...] = (opened * upward).astype(LOW)
            grad = sum(
                crossed(way_ref[:, lanes[far]], across(down_refs[i][far], slice(None)))
                for far in range(2)
            )
            gate_refs[i][...] = (grad * upward * sigma * (1.0 + gate * (1.0 - sigma))).astype(LOW)
            up_refs[i][...] = (grad * opened).astype(LOW)
        for far in range(2):
            values = sum(
                straight(gate_refs[i][...], across(first_refs[i][far], gate_rows))
                + straight(up_refs[i][...], across(first_refs[i][far], up_rows))
                for i in range(2)
            )
            deal(near_ref, far_ref, values, order, lanes[far])

    inputs = list(tokens) + list(directions) + pieces[0] + pieces[1]
    out = jax.ShapeDtypeStruct((length, width), LOW)
    step = lambda lanes: pl.BlockSpec((length, lanes), lambda i: (i, 0))
    shape = lambda lanes: jax.ShapeDtypeStruct((2 * length, lanes), LOW)
    near, far, all_tokens, all_ways, *rest = call(
        kernel,
        inputs,
        [whole(item) for item in inputs],
        [whole(out)] * 2 + [step(width)] * 2 + [step(hidden)] * 6,
        [out] * 2 + [shape(width)] * 2 + [shape(hidden)] * 6,
        [],
        "column_ffn",
    )
    return near, far, all_tokens, all_ways, rest[:2], rest[2:4], rest[4:6]


def write_across(ref, rows, values):
    size, _, _, strip = ref.shape
    for z in range(size):
        for c in range(2):
            start = (2 * z + c) * strip
            ref[z, c, rows] = values[:, start : start + strip].astype(LOW)


def column_down(actives, ways, down, size, strip):
    hidden = actives[0].shape[1]
    tokens, width = ways.shape
    length = tokens // 2
    lengths = lengths_of(down)
    pieces = flat(down)

    def kernel(*refs):
        active_refs, way_ref = refs[:2], refs[2]
        down_refs = nested(refs[3 : 3 + len(pieces)], lengths)
        near_ref, far_ref = refs[3 + len(pieces) : 5 + len(pieces)]
        grad_refs = refs[5 + len(pieces) :]
        half = width // 2
        for far in range(2):
            lanes = slice(far * half, (far + 1) * half)
            values = sum(
                straight(active_refs[i][...], across(down_refs[i][far], slice(None)))
                for i in range(2)
            ).astype(LOW)
            near_ref[:, lanes] = values[:length]
            far_ref[:, lanes] = values[length:]
            for i in range(2):
                write_across(
                    grad_refs[2 * i + far],
                    slice(None),
                    turned(active_refs[i][...], way_ref[:, lanes]),
                )

    inputs = list(actives) + [ways] + pieces
    out = jax.ShapeDtypeStruct((length, width), LOW)
    grad = jax.ShapeDtypeStruct((size, 2, hidden, strip), LOW)
    near, far, *grads = call(
        kernel,
        inputs,
        [whole(item) for item in inputs],
        [whole(out)] * 2 + [whole(grad)] * 4,
        [out] * 2 + [grad] * 4,
        [],
        "column_down",
        grid=1,
    )
    return near, far, [grads[:2], grads[2:]]


def column_rows(chunks, rights, size, strip):
    rows = [lefts[0].shape[1] for lefts in chunks]
    width = rights.shape[1]

    def kernel(*refs):
        left_refs = refs[: 2 * len(chunks)]
        right_ref = refs[2 * len(chunks)]
        grad_refs = refs[2 * len(chunks) + 1 :]
        half = width // 2
        for i in range(2):
            for far in range(2):
                for n in range(len(chunks)):
                    start = sum(rows[:n])
                    write_across(
                        grad_refs[2 * i + far],
                        slice(start, start + rows[n]),
                        turned(
                            left_refs[2 * n + i][...], right_ref[:, far * half : (far + 1) * half]
                        ),
                    )

    inputs = [left for lefts in chunks for left in lefts] + [rights]
    grad = jax.ShapeDtypeStruct((size, 2, sum(rows), strip), LOW)
    grads = call(
        kernel,
        inputs,
        [whole(item) for item in inputs],
        [whole(grad)] * 4,
        [grad] * 4,
        [],
        "column_rows",
        grid=1,
    )
    return [grads[:2], grads[2:]]


def column_backward(
    grads, out_weights, mix_weights, beta_weights, seg_col, seg_row, conv, head_gain, order,
    saved, projected, beta_in,
):
    count, _, length = seg_row.shape
    lines = conv.shape[0]
    width = grads[0].shape[1]
    lengths = [lengths_of(out_weights), lengths_of(mix_weights)]
    pieces = [flat(out_weights), flat(mix_weights)]

    def kernel(*refs):
        token_refs, out_refs, mix_refs, rest = split_refs(
            refs, [len(grads), len(pieces[0]), len(pieces[1]), 20]
        )
        out_refs, mix_refs = nested(out_refs, lengths[0]), nested(mix_refs, lengths[1])
        beta_ref, col_ref, row_ref, conv_ref, head_ref, order_ref = rest[:6]
        inverse_ref, update_ref, mixed_ref, first_ref, second_ref, beta_in_ref = rest[6:12]
        signal_ref, beta_grad_ref, conv_grad_ref, head_grad_ref = rest[12:16]
        near_ref, far_ref, hold_ref = rest[16:]
        places = blocks_of(order_ref, length)
        collect(token_refs, hold_ref, places)
        half = width // 2
        lanes = [slice(0, half), slice(half, width)]
        masks = masks_of(col_ref[...], row_ref[0])
        kept = kept_of(col_ref[...], conv_ref.shape[0] // 3)
        head_grad = jnp.zeros((1, HEAD), WIDE)
        beta_grads = []
        for head, projected_ref in enumerate((first_ref, second_ref)):
            own = head_lanes(head)
            grad = sum(
                crossed(hold_ref[:, lanes[far]], across(out_refs[head][far], slice(None)))
                for far in range(2)
            )
            signal_grads, beta_grad, conv_lines, gain_grad = backward_head(
                [projected_ref[:, head_lanes(part)] for part in range(4)],
                beta_in_ref[:, head : head + 1],
                conv_ref[:, own],
                kept,
                masks,
                head_ref[...],
                inverse_ref[0, head],
                update_ref[:, own],
                mixed_ref[:, own],
                grad,
            )
            head_grad = head_grad + gain_grad
            beta_grads.append(beta_grad.astype(LOW).astype(WIDE))
            beta_grad_ref[:, head : head + 1] = beta_grad
            for line, values in enumerate(conv_lines):
                conv_grad_ref[0, line : line + 1, own] = values
            for part in range(4):
                signal_ref[:, head_lanes(4 * head + part)] = signal_grads[part]
        head_grad_ref[0] = head_grad
        for far in range(2):
            values = sum(
                crossed(
                    signal_ref[:, 4 * HEAD * head : 4 * HEAD * (head + 1)],
                    down_list(mix_refs[head][far]),
                )
                + beta_grads[head] * beta_ref[head : head + 1, lanes[far]].astype(WIDE)
                for head in range(2)
            )
            deal(near_ref, far_ref, values, places, lanes[far])

    inputs = (
        list(grads)
        + pieces[0]
        + pieces[1]
        + [beta_weights, seg_col, seg_row, conv, head_gain, order]
        + list(saved)
        + list(projected)
        + [beta_in]
    )
    in_specs = [whole(item) for item in inputs]
    step = lambda lanes: pl.BlockSpec((length, lanes), lambda i: (i, 0))
    in_specs[-11] = step(1)
    in_specs[-10] = pl.BlockSpec((1, 1, length), lambda i: (i, 0, 0))
    in_specs[-7] = pl.BlockSpec(memory_space=pltpu.SMEM)
    in_specs[-6:] = saved_specs(length) + [step(4 * HEAD), step(4 * HEAD), step(2)]
    out = jax.ShapeDtypeStruct((length, width), LOW)
    return call(
        kernel,
        inputs,
        in_specs,
        grad_specs(length, lines) + [whole(out)] * 2 + [step(width)],
        grad_shapes(count, length, lines)
        + [out] * 2
        + [jax.ShapeDtypeStruct((count * length, width), LOW)],
        [],
        "column_backward",
    )


def column_mix(mixer_in, signal_grads):
    width = mixer_in.shape[1]

    def kernel(mixer_ref, signal_ref, *grad_refs):
        half = width // 2
        for far in range(2):
            for head in range(2):
                grad_refs[2 * head + far][...] = turned(
                    mixer_ref[:, far * half : (far + 1) * half],
                    signal_ref[:, 4 * HEAD * head : 4 * HEAD * (head + 1)],
                ).astype(LOW)

    inputs = [mixer_in, signal_grads]
    grad = jax.ShapeDtypeStruct((width // 2, 4 * HEAD), LOW)
    grads = call(
        kernel,
        inputs,
        [whole(item) for item in inputs],
        [whole(grad)] * 4,
        [grad] * 4,
        [],
        "column_mix",
        grid=1,
    )
    return [grads[:2], grads[2:]]


def contract(left, right, left_dim, right_dim):
    return lax.dot_general(
        left, right, (((left_dim,), (right_dim,)), ((), ())), preferred_element_type=WIDE
    )


def after(values, earlier):
    return lax.optimization_barrier((values, earlier))[0]


def exclusive_order(blocks):
    place = lax.axis_index("dmod")
    for bit in (1, 2):
        flip = (place & bit) != 0
        blocks = [jnp.where(flip, blocks[i ^ bit], blocks[i]) for i in range(4)]
    return blocks


def trade(blocks):
    return [blocks[0]] + [
        lax.ppermute(blocks[m], "dmod", [(i, i ^ m) for i in range(4)]) for m in (1, 2, 3)
    ]


def gather_width(values):
    far = lax.ppermute(values, "dmod", ACROSS)
    near = lax.ppermute(values, "dmod", CORE)
    return [values, near, far, lax.ppermute(far, "dmod", CORE)]


def scatter_width(blocks):
    near = lax.ppermute(blocks[1].astype(LOW), "dmod", CORE)
    cross = lax.ppermute(blocks[3].astype(LOW), "dmod", CORE)
    far = lax.ppermute((blocks[2] + cross.astype(WIDE)).astype(LOW), "dmod", ACROSS)
    return blocks[0] + near.astype(WIDE) + far.astype(WIDE)


def sum_pair(values):
    low = values.astype(LOW)
    return low.astype(WIDE) + lax.ppermute(low, "mp", SWAP).astype(WIDE)


def row_total(values):
    return lax.psum(values, "dmod")


class Ring:
    def __init__(self):
        self.size = lax.axis_size("dp")
        self.parts = 1

    def order(self, values):
        return values

    def gather(self, values):
        return [lax.all_gather(values, "dp", axis=1, tiled=True)]

    def scatter(self, make):
        return lax.psum_scatter(
            make(0).astype(LOW), "dp", scatter_dimension=1, tiled=True
        ).astype(WIDE)


def plane_body(
    block_input,
    segment_ids,
    group_ids,
    group_weight,
    mixer_norm,
    w_mix,
    w_beta,
    conv_kernel,
    head_norm,
    w_out,
    ffn_norm,
    w_ffn_in,
    w_ffn_down,
    cotangent,
):
    ring = Ring()
    parts = ring.parts
    micro, seqs, length, width = block_input.shape
    tokens = micro * seqs * length
    block = width // parts
    strip = w_mix.shape[0]
    span = w_mix.shape[2] // 4
    hidden = w_ffn_in.shape[2] // 4
    dmod = lax.axis_index("dmod")
    data_size = ring.size
    place = lax.axis_index("dp")

    lines = conv_kernel.shape[0] * conv_kernel.shape[1]
    pack = jnp.concatenate(
        [
            conv_kernel.reshape(-1),
            head_norm,
            mixer_norm,
            ffn_norm,
            w_beta.T.reshape(-1),
        ]
    )
    packs = lax.all_gather(pack, "dp", axis=0)
    sizes = [conv_kernel.size, head_norm.size, strip, strip, w_beta.size]
    cuts = [sum(sizes[:i]) for i in range(6)]
    conv = (
        packs[:, cuts[0] : cuts[1]]
        .reshape(data_size, lines, -1)
        .transpose(1, 0, 2)
        .reshape(lines, span)
        .astype(WIDE)
    )
    head_gain = packs[:, cuts[1] : cuts[2]].reshape(1, -1).astype(WIDE)
    gain_one = ring.order(packs[:, cuts[2] : cuts[3]].reshape(1, -1).astype(WIDE))
    gain_two = ring.order(packs[:, cuts[3] : cuts[4]].reshape(1, -1).astype(WIDE))
    beta_weights = ring.order(
        packs[:, cuts[4] : cuts[5]]
        .reshape(data_size, -1, strip)
        .transpose(1, 0, 2)
        .reshape(-1, width)
    )

    out_rows = jnp.concatenate(exclusive_order(jnp.split(w_out, 4, axis=0)), 0)
    out_halves = jnp.split(out_rows.T, 2, axis=1)
    mix_own = jnp.stack(trade(exclusive_order(jnp.split(w_mix, 4, axis=2))))
    mix_halves = [
        mix_own[:, :, :, head * HEAD : (head + 1) * HEAD].reshape(4, strip, 4 * HEAD)
        for head in (0, 1)
    ]
    ffn_own = jnp.stack(trade(exclusive_order(jnp.split(w_ffn_in, 4, axis=2))))
    ffn_halves = [ffn_own[:, :, 0], ffn_own[:, :, 1]]
    down_own = trade(exclusive_order(jnp.split(w_ffn_down, 4, axis=0)))
    down_halves = [
        jnp.stack([down_own[0].T, down_own[1].T]),
        jnp.stack([down_own[2].T, down_own[3].T]),
    ]

    def chain(half):
        first = ring.gather(out_halves[half][None])
        second = ring.gather(after(mix_halves[half], first[-1]))
        third = ring.gather(after(ffn_halves[half], second[-1]))
        fourth = ring.gather(after(down_halves[half], third[-1]))
        return first, second, third, fourth

    chains = [chain(0), chain(1)]
    out_weights = jnp.concatenate(
        [
            jnp.concatenate([part[0] for part in chains[0][0]], 0),
            jnp.concatenate([part[0] for part in chains[1][0]], 0),
        ],
        1,
    )
    mix_parts = [[part.reshape(4 * block, -1) for part in each[1]] for each in chains]
    ffn_parts = [[part.reshape(4 * block, -1) for part in each[2]] for each in chains]
    down_parts = [[part.reshape(2 * block, -1) for part in each[3]] for each in chains]

    marks = (group_ids.reshape(tokens, 1) == jnp.arange(group_weight.shape[0])[None]).astype(WIDE)
    counts = lax.psum(jnp.sum(marks, 0), "dp")
    table = group_weight * (tokens * data_size / group_weight.shape[0]) / counts
    scales = jnp.sum(marks * table, -1, keepdims=True)
    direction = ring.order(cotangent.reshape(tokens, width).astype(WIDE)) * scales
    direction_low = direction.astype(LOW)

    def by_part(slots):
        return [
            jnp.concatenate([slot[:, k * block : (k + 1) * block] for slot in slots], 1)
            for k in range(parts)
        ]

    def by_slot(pieces):
        return [
            jnp.concatenate([piece[:, m * block : (m + 1) * block] for piece in pieces], 1)
            for m in range(pieces[0].shape[1] // block)
        ]

    direction_parts = by_part(gather_width(direction_low))

    rows = ring.order(block_input.reshape(tokens, width).astype(WIDE))
    first_scale = lax.rsqrt(row_total(jnp.sum(rows * rows, -1, keepdims=True)) / D + 1e-06)
    mixer_in = (rows * first_scale * gain_one).astype(LOW)
    mixer_parts = by_part(gather_width(mixer_in))
    projected = [
        sum(jnp.dot(mixer_parts[k], mix_parts[half][k], preferred_element_type=WIDE) for k in range(parts))
        for half in (0, 1)
    ]
    beta_all = row_total(contract(beta_weights, mixer_in, 1, 1))
    heads = span // HEAD
    beta_in = lax.dynamic_slice_in_dim(beta_all, dmod * heads, heads, 0).T
    seg_col = segment_ids.reshape(tokens, 1)
    seg_row = segment_ids.reshape(micro * seqs, 1, length)
    mixer_args = list(projected) + [
        beta_in, seg_col, seg_row, conv, head_gain
    ]
    gated, *saved = mixer_forward(mixer_args)
    gated_all = jnp.concatenate(gather_width(gated), 1)
    middle = rows + sum_pair(contract(gated_all, out_weights, 1, 1))

    second_scale = lax.rsqrt(row_total(jnp.sum(middle * middle, -1, keepdims=True)) / D + 1e-06)
    ffn_in = (middle * second_scale * gain_two).astype(LOW)
    ffn_in_parts = by_part(gather_width(ffn_in))
    gate, upward = (
        sum(jnp.dot(ffn_in_parts[k], ffn_parts[half][k], preferred_element_type=WIDE) for k in range(parts))
        for half in (0, 1)
    )
    sigma = sigmoid(gate)
    active = (gate * sigma * upward).astype(LOW)
    down_slots = sum(
        (
            by_slot([contract(active, down_parts[half][k], 1, 1) for k in range(parts)])
            for half in (0, 1)
        ),
        [],
    )
    result = middle + sum_pair(scatter_width(down_slots))
    out = ring.order(result).astype(LOW).reshape(block_input.shape)

    down_grads = [
        ring.scatter(
            lambda k: contract(
                direction_parts[k][:, 2 * half * block : 2 * (half + 1) * block], active, 0, 0
            ).reshape(2, block, hidden)
        )
        for half in (0, 1)
    ]
    active_grad = sum(
        jnp.dot(
            direction_parts[k][:, 2 * half * block : 2 * (half + 1) * block],
            down_parts[half][k],
            preferred_element_type=WIDE,
        )
        for k in range(parts)
        for half in (0, 1)
    )
    gate_grad = (active_grad * upward * sigma * (1.0 + gate * (1.0 - sigma))).astype(LOW)
    upward_grad = (active_grad * gate * sigma).astype(LOW)
    ffn_slots = by_slot(
        [
            contract(gate_grad, ffn_parts[0][k], 1, 1) + contract(upward_grad, ffn_parts[1][k], 1, 1)
            for k in range(parts)
        ]
    )
    ffn_grads = [
        ring.scatter(lambda k: contract(ffn_in_parts[k], grad, 0, 0).reshape(4, block, hidden))
        for grad in (gate_grad, upward_grad)
    ]
    ffn_in_grad = sum_pair(scatter_width(ffn_slots))
    weighted_two = ffn_in_grad * gain_two
    norm_two_grad = jnp.sum(ffn_in_grad * middle * second_scale, 0)
    inner_two = row_total(jnp.sum(weighted_two * middle, -1, keepdims=True))
    middle_grad = (
        direction + second_scale * weighted_two - middle * (second_scale**3 * inner_two / D)
    )

    branch_low = middle_grad.astype(LOW)
    out_grads = [
        ring.scatter(
            lambda k: contract(
                branch_low[:, k * block : (k + 1) * block],
                gated_all[:, 2 * half * span : 2 * (half + 1) * span],
                0,
                0,
            )[None]
        )
        for half in (0, 1)
    ]
    gated_slots = jnp.split(jnp.dot(branch_low, out_weights, preferred_element_type=WIDE), 4, axis=1)
    gated_grad = scatter_width(gated_slots)
    projected_grad, beta_grad, conv_grad, head_grad = mixer_backward(
        mixer_args, saved, gated_grad
    )
    projected_slots = gather_width(projected_grad)
    mix_grads = [
        ring.scatter(
            lambda k: contract(
                mixer_in[:, k * block : (k + 1) * block],
                jnp.concatenate(projected_slots[2 * half : 2 * half + 2], 1),
                0,
                0,
            )[None]
        )
        for half in (0, 1)
    ]
    beta_slots = jnp.concatenate(
        exclusive_order(gather_width(beta_grad.T.astype(LOW))), 0
    )
    beta_weight_grad = contract(beta_slots, mixer_in, 1, 0)
    mixer_slots = by_slot(
        [
            contract(projected_grad[:, : 2 * span], mix_parts[0][k], 1, 1)
            + contract(projected_grad[:, 2 * span :], mix_parts[1][k], 1, 1)
            for k in range(parts)
        ]
    )
    mixer_grad = sum_pair(scatter_width(mixer_slots) + contract(beta_slots, beta_weights, 0, 0))
    weighted_one = mixer_grad * gain_one
    norm_one_grad = jnp.sum(mixer_grad * rows * first_scale, 0)
    inner_one = row_total(jnp.sum(weighted_one * rows, -1, keepdims=True))
    grad_input = ring.order(
        middle_grad + first_scale * weighted_one - rows * (first_scale**3 * inner_one / D)
    ).reshape(block_input.shape)

    head_total = lax.psum(jnp.sum(head_grad, (0, 1)), ("dp", "mp", "dmod"))
    head_out = lax.dynamic_slice_in_dim(head_total, place * head_norm.size, head_norm.size, 0)
    small = jnp.concatenate(
        [
            jnp.sum(conv_grad, 0),
            ring.order(jnp.stack([norm_one_grad, norm_two_grad]))
            .reshape(2, data_size, -1)
            .transpose(1, 0, 2)
            .reshape(data_size, -1)
            .reshape(-1)
            .reshape(-1, span),
            ring.order(beta_weight_grad)
            .reshape(-1, data_size, strip)
            .transpose(1, 0, 2)
            .reshape(-1, span),
        ],
        0,
    )
    conv_part = (
        small[:lines].reshape(lines, data_size, -1).transpose(1, 0, 2).reshape(data_size, -1)
    )
    norm_part = small[lines : lines + 2 * width // span].reshape(data_size, -1)
    beta_part = small[lines + 2 * width // span :].reshape(data_size, -1)
    small_own = lax.psum_scatter(
        jnp.concatenate([conv_part, norm_part, beta_part], 1), "dp", scatter_dimension=0
    )
    conv_out = small_own[: conv_kernel.size].reshape(conv_kernel.shape)
    norm_one_out = small_own[conv_kernel.size : conv_kernel.size + strip]
    norm_two_out = small_own[conv_kernel.size + strip : conv_kernel.size + 2 * strip]
    beta_out = small_own[conv_kernel.size + 2 * strip :].reshape(-1, strip).T

    def placed(blocks):
        return exclusive_order(trade([values.astype(LOW) for values in blocks]))

    ffn_out = jnp.stack(
        [
            jnp.concatenate([values.astype(WIDE) for values in placed(list(grad))], 1)
            for grad in ffn_grads
        ],
        1,
    )
    down_out = jnp.concatenate(
        [
            values.astype(WIDE).T
            for values in placed(list(down_grads[0]) + list(down_grads[1]))
        ],
        0,
    )
    out_out = jnp.concatenate(
        exclusive_order(jnp.split(jnp.concatenate([grad[0] for grad in out_grads], 1).T, 4, axis=0)),
        0,
    )
    mix_blocks = sum((jnp.split(grad[0], 2, axis=1) for grad in mix_grads), [])
    mix_out = jnp.concatenate(
        [
            values.reshape(strip, 2, 4, HEAD).transpose(0, 2, 1, 3).reshape(strip, 4, span)
            for values in exclusive_order(mix_blocks)
        ],
        2,
    )
    return (
        out,
        grad_input,
        norm_one_out,
        mix_out,
        beta_out,
        conv_out,
        head_out,
        out_out,
        norm_two_out,
        ffn_out,
        down_out,
    )


def exchange(values, axis):
    return lax.all_to_all(values, axis, 0, 0, tiled=True)


def swap_mp(values):
    return lax.ppermute(values, "mp", SWAP)


def swap_core(values):
    return lax.ppermute(values, "dmod", CORE)


def swap_across(values):
    return lax.ppermute(values, "dmod", ACROSS)


def swap_dp(values, k):
    return lax.ppermute(values, "dp", [(i, i ^ k) for i in range(lax.axis_size("dp"))])


def trade_blocks(blocks, axis, place):
    size = len(blocks)
    blocks = by_difference(blocks, place)
    moved = [blocks[0]] + [
        lax.ppermute(blocks[k], axis, [(i, i ^ k) for i in range(size)]) for k in range(1, size)
    ]
    return by_difference(moved, place)


def by_difference(blocks, place):
    bit = 1
    while bit < len(blocks):
        flip = (place & bit) != 0
        blocks = [jnp.where(flip, blocks[i ^ bit], blocks[i]) for i in range(len(blocks))]
        bit *= 2
    return blocks


def everyone(values, place):
    size = lax.axis_size("dp")
    values = values[None]
    bit = 1
    while bit < size:
        values = jnp.concatenate(turn((place & bit) != 0, (values, swap_dp(values, bit))), 0)
        bit *= 2
    return values


def turn(flag, pair):
    return jnp.where(flag, pair[1], pair[0]), jnp.where(flag, pair[0], pair[1])


def chip_blocks(core, pair):
    keep, send = turn(core, pair)
    return jnp.stack(turn(core, (keep, swap_core(send))), 1)


def along_column(core, pair, earlier=None):
    both = chip_blocks(core, pair)
    if earlier is not None:
        both = after(both, earlier)
    return exchange(both, "dp")


def gather_columns(values, earlier=None, later=None):
    if earlier is not None:
        values = after(values, earlier)
    half = values.shape[0] // 2
    over = swap_mp(values)
    far = swap_across(values)
    corner = (over[:half], far[half:])
    if later is not None:
        corner = after(corner, later)
    both = [swap_across(corner[0]), swap_mp(corner[1])]
    return [[[values], [far]], [[over], both]]


def wide(values):
    return values.astype(WIDE)


def scatter_columns(grid):
    half = grid[0][0].shape[0] // 2
    sent = swap_mp(jnp.concatenate([grid[1][0][:half], grid[1][1][:half]], 0))
    top = wide(grid[0][1][:half]) + wide(sent[half:])
    top = wide(grid[0][0][:half]) + wide(sent[:half]) + wide(swap_across(top.astype(LOW)))
    rest = grid[0][0].shape[0] - half
    sent = swap_across(jnp.concatenate([grid[0][1][half:], grid[1][1][half:]], 0))
    low = wide(grid[1][0][half:]) + wide(sent[rest:])
    low = wide(grid[0][0][half:]) + wide(sent[:rest]) + wide(swap_mp(low.astype(LOW)))
    return jnp.concatenate([top, low], 0).astype(LOW)


def column_blocks(values):
    mine = [values] + [swap_dp(values, k) for k in range(1, lax.axis_size("dp"))]
    return mine + [swap_core(block) for block in mine]


def column_total(near, far):
    size = lax.axis_size("dp")
    share = near.shape[0] // size
    chip = wide(near) + wide(swap_core(far))
    total = chip[:share]
    low = [chip[k * share : (k + 1) * share].astype(LOW) for k in range(1, size)]
    for k in range(1, size):
        total = total + wide(swap_dp(low[k - 1], k))
    return total, low[0]


def column_body(
    block_input,
    segment_ids,
    group_ids,
    group_weight,
    mixer_norm,
    w_mix,
    w_beta,
    conv_kernel,
    head_norm,
    w_out,
    ffn_norm,
    w_ffn_in,
    w_ffn_down,
    cotangent,
):
    place = lax.axis_index("dp")
    size = lax.axis_size("dp")
    side = lax.axis_index("mp")
    dmod = lax.axis_index("dmod")
    row, core = dmod // 2, dmod % 2
    at_far_side, at_far_row, at_core = side == 1, row == 1, core == 1
    micro, _, length, width = block_input.shape
    share = length // size
    strip = w_mix.shape[0]
    groups = group_weight.shape[0]
    group_heads = w_beta.shape[1]
    hidden = w_ffn_down.shape[0] // (2 * size)
    span = 2 * width

    def to_column(values):
        lead = values.shape[:-1]
        values = values.reshape(lead + (2, 2, size, strip))
        values = jnp.swapaxes(values, -2, -3).reshape(lead + (2, span))
        return jnp.concatenate(turn(at_far_row, (values[..., 0, :], values[..., 1, :])), -1)

    def from_column(values):
        lead = values.shape[:-1]
        halves_of = turn(at_far_row, (values[..., :span], values[..., span:]))
        values = jnp.stack(halves_of, -2).reshape(lead + (2, size, 2, strip))
        return jnp.swapaxes(values, -2, -3).reshape(lead + (2 * span,))

    def tokens_in(values):
        values = values.reshape(micro, size, share, width)
        moved = trade_blocks([values[:, z] for z in range(size)], "dp", place)
        moved = jnp.where(at_far_side, jnp.stack(moved[2:]), jnp.stack(moved[:2]))
        moved = moved.reshape(4, share, width)
        moved = trade_blocks([moved[j] for j in range(4)], "dmod", dmod)
        return to_column(jnp.concatenate(moved, 1))

    def tokens_out(values):
        blocks = jnp.split(from_column(values), 4, axis=1)
        moved = jnp.stack(trade_blocks(blocks, "dmod", dmod)).reshape(2, micro, share, width)
        moved = jnp.concatenate(turn(at_far_side, (moved, swap_mp(moved))), 0)
        moved = trade_blocks([moved[z] for z in range(size)], "dp", place)
        return jnp.stack(moved, 1).reshape(block_input.shape)

    blocks = w_mix.reshape(strip, 4, 2, size, HEAD).transpose(2, 3, 0, 1, 4)
    blocks = blocks.reshape(2, size, strip, 4 * HEAD)
    mix_blocks = chip_blocks(at_core, (blocks[0], blocks[1]))
    block_input, w_out, w_ffn_in, w_ffn_down, conv_kernel = after(
        (block_input, w_out, w_ffn_in, w_ffn_down, conv_kernel), mix_blocks
    )
    mix_pieces = exchange(mix_blocks, "dp")
    tokens_low = tokens_in(block_input)
    rows = wide(tokens_low)
    mix_weights = gather_columns(mix_pieces)
    mix_weights = [
        [[item.reshape(-1, 4 * HEAD) for item in items] for items in pair] for pair in mix_weights
    ]
    token_blocks = column_blocks(tokens_low)
    out_pieces = along_column(
        at_core, tuple(w_out.reshape(2, size, HEAD, strip)), (mix_pieces, token_blocks[3])
    )
    ffn_rows = w_ffn_in.transpose(1, 2, 0).reshape(2, 2, size, hidden, strip)
    blocks = jnp.concatenate([ffn_rows[0], ffn_rows[1]], 2)
    first_pieces = along_column(at_core, (blocks[0], blocks[1]), out_pieces)
    out_weights = gather_columns(out_pieces, mix_weights[1][1])

    small = [
        conv_kernel.reshape(-1),
        head_norm,
        mixer_norm,
        ffn_norm,
        w_beta.T.reshape(-1),
        segment_ids.reshape(-1).astype(LOW),
        group_ids.reshape(-1).astype(LOW),
    ]
    count = sum(item.size for item in small)
    pack = jnp.concatenate(small + [jnp.zeros((-count % HEAD,), LOW)]).reshape(-1, HEAD)
    packs = everyone(pack, place)
    packs = jnp.stack(turn(at_far_side, (packs, swap_mp(packs))))
    packs = jnp.stack(turn(at_core, (packs, swap_core(packs))))
    packs = jnp.stack(turn(at_far_row, (packs, swap_across(packs))))
    packs = packs.reshape(2, 2, 2, size, -1)
    fields = []
    start = 0
    for item in small:
        fields.append(packs[..., start : start + item.size])
        start += item.size
    lines = conv_kernel.shape[0] * conv_kernel.shape[1]
    heads = 2 * group_heads
    local_head = size * core + place
    own_heads = [group_heads * side + local_head, group_heads * (1 - side) + local_head]
    conv_all = (
        fields[0]
        .reshape(2, 2, 2, size, lines, -1)
        .transpose(4, 2, 0, 1, 3, 5)
        .reshape(lines, heads * HEAD)
    )
    conv = wide(
        jnp.concatenate(
            [lax.dynamic_slice_in_dim(conv_all, head * HEAD, HEAD, 1) for head in own_heads], 1
        )
    )
    head_gain = wide(fields[1][0, 0, 0].reshape(1, HEAD))
    gain_one = to_column(wide(fields[2][:, :, 0].reshape(1, -1)))
    gain_two = to_column(wide(fields[3][:, :, 0].reshape(1, -1)))
    beta_rows = (
        fields[4]
        .reshape(2, 2, 2, size, group_heads, strip)
        .transpose(2, 4, 0, 1, 3, 5)
        .reshape(heads, -1)
    )
    beta_weights = to_column(
        jnp.concatenate([lax.dynamic_slice_in_dim(beta_rows, head, 1, 0) for head in own_heads], 0)
    )
    sequence = 2 * side + row
    segments = lax.dynamic_index_in_dim(fields[5][0, 0, 0], sequence, 0, keepdims=False)
    segments = segments.reshape(micro, length).astype(jnp.int32)
    segments = jnp.concatenate(turn(at_core, (segments[:1], segments[1:])), 0)
    seg_col = segments.reshape(-1, 1)
    seg_row = segments.reshape(micro, 1, length)
    all_groups = fields[6][0, 0, 0].reshape(-1).astype(jnp.int32)
    names = jnp.arange(groups, dtype=jnp.int32)
    counts = jnp.sum((all_groups[:, None] == names[None]).astype(WIDE), 0)
    table = group_weight * (all_groups.shape[0] / groups) / counts
    own_groups = lax.dynamic_slice_in_dim(
        all_groups, (sequence * micro + core) * length + place * share, share, 0
    )
    scales = jnp.sum((own_groups[:, None] == names[None]).astype(WIDE) * table, -1, keepdims=True)

    order = jnp.arange(size, dtype=jnp.int32) ^ place
    constants = [beta_weights, seg_col, seg_row, conv, head_gain, order]
    gated, inverse, update, mixed, mixer_in, *projected, beta_in = column_forward(
        token_blocks, mix_weights, gain_one, *constants
    )
    branch, mark = column_total(*column_branch(gated, out_weights, order, length))
    first_weights = gather_columns(first_pieces, mix_weights[1][1], gated)
    middle = rows + branch

    second_scale = lax.rsqrt(jnp.mean(middle * middle, -1, keepdims=True) + 1e-06)
    ffn_low = (middle * second_scale * gain_two).astype(LOW)
    ffn_blocks = column_blocks(ffn_low)
    down_pieces = along_column(
        at_core, tuple(w_ffn_down.reshape(2, size, hidden, strip)), (first_pieces, ffn_low)
    )
    down_weights = gather_columns(down_pieces, first_weights[1][1])
    direction = wide(tokens_in(after(cotangent, token_blocks[3]))) * scales
    direction_blocks = column_blocks(after(direction.astype(LOW), ffn_blocks[3]))
    near, far, ffn_in, directions, actives, gate_grads, up_grads = column_ffn(
        ffn_blocks, direction_blocks, first_weights, down_weights, hidden
    )
    ffn_in_grad, mark = column_total(near, far)
    near, far, down_grads = column_down(
        after(actives, mark), directions, down_weights, size, strip
    )
    ffn_grads = column_rows([after(gate_grads, mark), up_grads], ffn_in, size, strip)

    def placed(grid, earlier=None):
        total = scatter_columns(grid)
        return along_column(at_core, (total[:, 0], total[:, 1]), earlier)

    def stacked(pieces):
        return pieces.transpose(1, 0, 2, 3).reshape(2 * size, -1, strip)

    weighted_two = ffn_in_grad * gain_two
    norm_two_grad = jnp.sum(ffn_in_grad * middle * second_scale, 0, keepdims=True)
    inner_two = jnp.mean(weighted_two * middle, -1, keepdims=True)
    middle_grad = (
        direction + second_scale * weighted_two - middle * (second_scale**3 * inner_two)
    )
    branch_low = middle_grad.astype(LOW)
    branch_blocks = column_blocks(branch_low)
    down_pieces = placed(down_grads, branch_blocks[3])
    ffn_pieces = placed(ffn_grads, down_pieces)
    down_out = wide(stacked(down_pieces).reshape(-1, strip))
    ffn_out = stacked(ffn_pieces).reshape(2 * size, 2, hidden, strip)
    ffn_out = wide(ffn_out.transpose(1, 0, 2, 3).reshape(2, -1, strip).transpose(2, 0, 1))
    down_sum, _ = column_total(near, after(far, branch_blocks[3]))
    out = tokens_out((middle + down_sum).astype(LOW))

    signal_grads, beta_grad, conv_grad, head_grad, near, far, branch_all = column_backward(
        branch_blocks,
        out_weights,
        mix_weights,
        *constants,
        (inverse, update, mixed),
        projected,
        beta_in,
    )
    mix_grads = column_mix(mixer_in, signal_grads)
    mixer_grad, _ = column_total(near, far)
    gated_heads = [gated[:, :HEAD], gated[:, HEAD:]]
    out_grads = column_rows(
        [after(gated_heads, mix_grads[1][1])], branch_all, size, strip
    )
    out_pieces = placed(out_grads, ffn_pieces)
    out_out = wide(stacked(out_pieces).reshape(-1, strip))
    mix_total = scatter_columns(mix_grads).reshape(size, 2, strip, 4 * HEAD)
    mix_pieces = along_column(
        at_core, (mix_total[:, 0], mix_total[:, 1]), out_pieces
    )
    mix_out = wide(
        mix_pieces.reshape(size, 2, strip, 4, HEAD).transpose(2, 3, 1, 0, 4).reshape(strip, 4, -1)
    )
    beta_weight_grad = contract(beta_grad.astype(LOW), mixer_in, 0, 0)
    weighted_one = mixer_grad * gain_one
    first_scale = lax.rsqrt(jnp.mean(rows * rows, -1, keepdims=True) + 1e-06)
    norm_one_grad = jnp.sum(mixer_grad * rows * first_scale, 0, keepdims=True)
    inner_one = jnp.mean(weighted_one * rows, -1, keepdims=True)
    grad_input = wide(
        tokens_out(
            (
                middle_grad + first_scale * weighted_one - rows * (first_scale**3 * inner_one)
            ).astype(LOW)
        )
    )

    def over_columns(values):
        values = values + swap_mp(values)
        return values + swap_across(values)

    conv_sides = jnp.stack(turn(at_far_side, jnp.split(jnp.sum(conv_grad, 0), 2, axis=1)))
    beta_sides = from_column(
        jnp.concatenate(turn(at_far_side, (beta_weight_grad[:1], beta_weight_grad[1:])), 0)
    )
    vector = jnp.concatenate(
        [
            conv_sides.reshape(-1, HEAD),
            beta_sides.reshape(-1, HEAD),
            from_column(norm_two_grad).reshape(-1, HEAD),
            jnp.sum(head_grad, 0),
        ]
    )
    vector = over_columns(vector)
    vectors = jnp.stack(turn(at_core, (vector, swap_core(vector))))
    vectors = everyone(vectors, place)
    ends = [2 * lines, 2 * lines + 4 * span // HEAD]
    ends.append(ends[1] + 2 * span // HEAD)
    own_width = dmod * width + place * strip
    taps_own = conv_kernel.shape[2]
    at = (dmod * size + place) * taps_own
    conv_head = at // HEAD
    conv_out = lax.dynamic_slice(
        vectors,
        (conv_head % size, conv_head // size, side * lines, at % HEAD),
        (1, 1, lines, taps_own),
    ).reshape(conv_kernel.shape)
    beta_out = (
        lax.dynamic_slice(
            vectors[:, :, ends[0] : ends[1]].reshape(size, 2, 2, 2 * span),
            (0, 0, side, own_width),
            (size, 2, 1, strip),
        )
        .reshape(size, 2, strip)
        .transpose(2, 1, 0)
        .reshape(strip, group_heads)
    )
    sums = jnp.sum(vectors[:, :, ends[1] :], (0, 1))
    norm_two_out = lax.dynamic_slice_in_dim(sums[:-1].reshape(-1), own_width, strip, 0)
    head_out = lax.dynamic_slice_in_dim(sums[-1], place * head_norm.size, head_norm.size, 0)
    last = over_columns(from_column(norm_one_grad).reshape(-1, HEAD))
    last = last + swap_core(last)
    bit = 1
    while bit < size:
        last = last + swap_dp(last, bit)
        bit *= 2
    last = last.reshape(-1)
    norm_one_out = lax.dynamic_slice_in_dim(last, own_width, strip, 0)
    return (
        out,
        grad_input,
        norm_one_out,
        mix_out,
        beta_out,
        conv_out,
        head_out,
        out_out,
        norm_two_out,
        ffn_out,
        down_out,
    )


def solution(mesh):
    sizes = dict(mesh.shape)
    columns = sizes["mp"] * sizes["dmod"] // 2
    body = column_body if columns == sizes["dp"] else plane_body
    wide = P(("dmod", "dp"))
    tokens = P(None, "dp", None, "dmod")
    weights = (
        wide,
        P(("dmod", "dp"), None, "mp"),
        P(("dmod", "dp"), "mp"),
        P(None, None, ("mp", "dmod", "dp")),
        P("dp"),
        P("mp", ("dmod", "dp")),
        wide,
        P(("dmod", "dp"), None, "mp"),
        P("mp", ("dmod", "dp")),
    )
    ids = P(None, "dp", None)
    return jax.shard_map(
        body,
        mesh=mesh,
        in_specs=(tokens, ids, ids, P()) + weights + (tokens,),
        out_specs=(tokens, tokens) + weights,
        check_vma=False,
    )
```

```python
import jax
import jax.numpy as jnp
from jax import lax
from jax.experimental import pallas as pl
from jax.experimental.pallas import tpu as pltpu
from jax.sharding import PartitionSpec as P

D = 2048
HEAD = 128
LOW = jnp.bfloat16
WIDE = jnp.float32
LONGEST_RING = 1
CORE = [(i, i ^ 1) for i in range(4)]
ACROSS = [(i, i ^ 2) for i in range(4)]
SWAP = [(0, 1), (1, 0)]


def halves(values):
    high = values.astype(LOW)
    return high, (values - high.astype(WIDE)).astype(LOW)


def product(left, right, left_dim, right_dim):
    def one(a, b):
        return lax.dot_general(
            a, b, (((left_dim,), (right_dim,)), ((), ())), preferred_element_type=WIDE
        )

    return one(left[0], right[0]) + (one(left[0], right[1]) + one(left[1], right[0]))


def sigmoid(values):
    return 1.0 / (1.0 + jnp.exp(-values))


def masks_of(seg_col, seg_row):
    length = seg_col.shape[0]
    rows = lax.broadcasted_iota(jnp.int32, (length, length), 0)
    cols = lax.broadcasted_iota(jnp.int32, (length, length), 1)
    same = seg_col == seg_row
    return rows, cols, same & (cols < rows), same & (cols <= rows)


def kept_of(seg_col, taps):
    length = seg_col.shape[0]
    wide = jnp.broadcast_to(seg_col, (length, HEAD))
    place = lax.broadcasted_iota(jnp.int32, (length, HEAD), 0)
    return [
        ((pltpu.roll(wide, shift, 0) == wide) & (place >= shift)).astype(WIDE)
        for shift in range(1, taps)
    ]


def convolve(signal, kernel, kept):
    taps = kernel.shape[0]
    total = signal * kernel[taps - 1 : taps]
    for shift in range(1, taps):
        moved = pltpu.roll(signal, shift, 0) * kept[shift - 1]
        total = total + moved * kernel[taps - 1 - shift : taps - shift]
    return total


def single(left, right):
    return lax.dot_general(
        left.astype(LOW),
        right.astype(LOW),
        (((1,), (0,)), ((), ())),
        preferred_element_type=WIDE,
    )


def invert(lowers, rows, cols):
    length = lowers[0].shape[0]
    eye = (rows == cols).astype(WIDE)
    pair = (rows // 2) == (cols // 2)
    inverses = [eye - jnp.where(pair, lower, 0.0) for lower in lowers]
    size = 2
    while size < length:
        cross = ((rows // (2 * size)) == (cols // (2 * size))) & ((rows // size) != (cols // size))
        steps = [
            single(inverse, jnp.where(cross, lower, 0.0))
            for inverse, lower in zip(inverses, lowers)
        ]
        inverses = [
            inverse - single(step, inverse) for step, inverse in zip(steps, inverses)
        ]
        size *= 2
    rests = [
        eye - inverse - product(halves(lower), halves(inverse), 1, 0)
        for inverse, lower in zip(inverses, lowers)
    ]
    return [inverse + single(inverse, rest) for inverse, rest in zip(inverses, rests)]


def forward_heads(signals, beta_in, conv, kept, masks, gain):
    rows, cols, strict, inclusive = masks
    taps = conv[0].shape[0] // 3
    lowers, held = [], []
    for head in range(len(signals)):
        convolved = []
        for part in range(3):
            kernel = conv[head][part * taps : (part + 1) * taps]
            pre = convolve(signals[head][part], kernel, kept)
            convolved.append(pre * sigmoid(pre))
        query = convolved[0] * (
            lax.rsqrt(jnp.sum(convolved[0] * convolved[0], 1, keepdims=True) + 1e-06) * HEAD**-0.5
        )
        key = convolved[1] * lax.rsqrt(
            jnp.sum(convolved[1] * convolved[1], 1, keepdims=True) + 1e-06
        )
        beta = sigmoid(beta_in[head])
        key_parts = halves(key)
        gram = product(key_parts, key_parts, 1, 1)
        lowers.append(jnp.where(strict, gram * beta, 0.0))
        scores = jnp.where(inclusive, product(halves(query), key_parts, 1, 1), 0.0)
        held.append((halves(scores), halves(convolved[2] * beta)))
    out = []
    for head, inverse in enumerate(invert(lowers, rows, cols)):
        scores, target = held[head]
        update = product(halves(inverse), target, 1, 0)
        mixed = product(scores, halves(update), 1, 0)
        scale = lax.rsqrt(jnp.sum(mixed * mixed, 1, keepdims=True) * (1.0 / HEAD) + 1e-05)
        gate = signals[head][3]
        gated = (mixed * scale * gain * (gate * sigmoid(gate))).astype(LOW)
        out.append((gated, inverse, update, mixed))
    return out


def backward_head(signals, beta_in, conv, kept, masks, gain, inverse, update, mixed, grad):
    rows, cols, strict, inclusive = masks
    length = grad.shape[0]
    taps = conv.shape[0] // 3
    before, gates, convolved = [], [], []
    for part in range(3):
        pre = convolve(signals[part], conv[part * taps : (part + 1) * taps], kept)
        before.append(pre)
        gates.append(sigmoid(pre))
        convolved.append(pre * gates[part])
    query_unit = lax.rsqrt(jnp.sum(convolved[0] * convolved[0], 1, keepdims=True) + 1e-06)
    key_unit = lax.rsqrt(jnp.sum(convolved[1] * convolved[1], 1, keepdims=True) + 1e-06)
    query = convolved[0] * (query_unit * HEAD**-0.5)
    key = convolved[1] * key_unit
    beta = sigmoid(beta_in)
    gate = signals[3]
    gate_sigma = sigmoid(gate)
    opened = gate * gate_sigma
    scale = lax.rsqrt(jnp.sum(mixed * mixed, 1, keepdims=True) * (1.0 / HEAD) + 1e-05)
    normed = mixed * scale
    head_grad = jnp.sum(grad * opened * normed, 0, keepdims=True)
    inner = grad * opened * gain
    mixed_grad = scale * inner - mixed * (
        scale * scale * scale * (jnp.sum(inner * mixed, 1, keepdims=True) * (1.0 / HEAD))
    )
    gate_grad = grad * normed * gain * gate_sigma * (1.0 + gate * (1.0 - gate_sigma))
    key_parts = halves(key)
    query_parts = halves(query)
    update_parts = halves(update)
    mixed_parts = halves(mixed_grad)
    gram = product(key_parts, key_parts, 1, 1)
    scores = jnp.where(inclusive, product(query_parts, key_parts, 1, 1), 0.0)
    scores_grad = halves(jnp.where(inclusive, product(mixed_parts, update_parts, 1, 1), 0.0))
    update_grad = product(halves(scores), mixed_parts, 0, 0)
    solved = product(halves(inverse), halves(update_grad), 0, 0)
    system_grad = jnp.where(strict, -product(halves(solved), update_parts, 1, 1), 0.0)
    gram_grad = halves(system_grad * beta)
    query_grad = product(scores_grad, key_parts, 1, 0)
    key_grad = (
        product(scores_grad, query_parts, 0, 0)
        + product(gram_grad, key_parts, 1, 0)
        + product(gram_grad, key_parts, 0, 0)
    )
    beta_grad = jnp.sum(system_grad * gram, 1, keepdims=True) + jnp.sum(
        solved * convolved[2], 1, keepdims=True
    )
    beta_grad = beta_grad * beta * (1.0 - beta)
    conv_grads = [
        HEAD**-0.5
        * (
            query_grad * query_unit
            - convolved[0]
            * (
                query_unit
                * query_unit
                * query_unit
                * jnp.sum(convolved[0] * query_grad, 1, keepdims=True)
            )
        ),
        key_grad * key_unit
        - convolved[1]
        * (key_unit * key_unit * key_unit * jnp.sum(convolved[1] * key_grad, 1, keepdims=True)),
        solved * beta,
    ]
    lines = [None] * (3 * taps)
    signal_grads = []
    for part in range(3):
        sigma = gates[part]
        error = conv_grads[part] * sigma * (1.0 + before[part] * (1.0 - sigma))
        kernel = conv[part * taps : (part + 1) * taps]
        total = error * kernel[taps - 1 : taps]
        last = part * taps + taps - 1
        lines[last] = jnp.sum(error * signals[part], 0, keepdims=True)
        for shift in range(1, taps):
            held = error * kept[shift - 1]
            lines[last - shift] = jnp.sum(
                held * pltpu.roll(signals[part], shift, 0), 0, keepdims=True
            )
            total = total + pltpu.roll(held, length - shift, 0) * (
                kernel[taps - 1 - shift : taps - shift]
            )
        signal_grads.append(total.astype(LOW))
    signal_grads.append(gate_grad.astype(LOW))
    return signal_grads, beta_grad, lines, head_grad


def head_lanes(head):
    return slice(head * HEAD, (head + 1) * HEAD)


def mixer_forward_kernel(*refs):
    parts = refs[:2]
    beta_ref, col_ref, row_ref, conv_ref, head_ref = refs[2:7]
    gated_ref, inverse_ref, update_ref, mixed_ref = refs[7:]
    masks = masks_of(col_ref[...], row_ref[0])
    kept = kept_of(col_ref[...], conv_ref.shape[0] // 3)
    results = forward_heads(
        [[parts[head][:, head_lanes(part)] for part in range(4)] for head in range(2)],
        [beta_ref[:, head : head + 1] for head in range(2)],
        [conv_ref[:, head_lanes(head)] for head in range(2)],
        kept,
        masks,
        head_ref[...],
    )
    for head, result in enumerate(results):
        own = head_lanes(head)
        gated_ref[:, own], inverse_ref[0, head], update_ref[:, own], mixed_ref[:, own] = result


def mixer_backward_kernel(*refs):
    parts = refs[:2]
    beta_ref, col_ref, row_ref, conv_ref, head_ref = refs[2:7]
    inverse_ref, update_ref, mixed_ref, grad_ref = refs[7:11]
    out_ref, beta_grad_ref, conv_grad_ref, head_grad_ref = refs[11:]
    masks = masks_of(col_ref[...], row_ref[0])
    kept = kept_of(col_ref[...], conv_ref.shape[0] // 3)
    head_grad = jnp.zeros((1, HEAD), WIDE)
    for head in range(2):
        own = head_lanes(head)
        grads, beta_grad, lines, gain_grad = backward_head(
            [parts[head][:, head_lanes(part)] for part in range(4)],
            beta_ref[:, head : head + 1],
            conv_ref[:, own],
            kept,
            masks,
            head_ref[...],
            inverse_ref[0, head],
            update_ref[:, own],
            mixed_ref[:, own],
            grad_ref[:, own],
        )
        head_grad = head_grad + gain_grad
        beta_grad_ref[:, head : head + 1] = beta_grad
        for line, values in enumerate(lines):
            conv_grad_ref[0, line : line + 1, own] = values
        for part in range(4):
            out_ref[:, head_lanes(4 * head + part)] = grads[part]
    head_grad_ref[0] = head_grad


def mixer_specs(length, lines):
    part = pl.BlockSpec((length, 4 * HEAD), lambda i: (i, 0))
    return [
        part,
        part,
        pl.BlockSpec((length, 2), lambda i: (i, 0)),
        pl.BlockSpec((length, 1), lambda i: (i, 0)),
        pl.BlockSpec((1, 1, length), lambda i: (i, 0, 0)),
        pl.BlockSpec((lines, 2 * HEAD), lambda i: (0, 0)),
        pl.BlockSpec((1, HEAD), lambda i: (0, 0)),
    ]


def saved_specs(length):
    return [
        pl.BlockSpec((1, 2, length, length), lambda i: (i, 0, 0, 0)),
        pl.BlockSpec((length, 2 * HEAD), lambda i: (i, 0)),
        pl.BlockSpec((length, 2 * HEAD), lambda i: (i, 0)),
    ]


def saved_shapes(count, length):
    return [
        jax.ShapeDtypeStruct((count, 2, length, length), WIDE),
        jax.ShapeDtypeStruct((count * length, 2 * HEAD), WIDE),
        jax.ShapeDtypeStruct((count * length, 2 * HEAD), WIDE),
    ]


def grad_specs(length, lines):
    return [
        pl.BlockSpec((length, 8 * HEAD), lambda i: (i, 0)),
        pl.BlockSpec((length, 2), lambda i: (i, 0)),
        pl.BlockSpec((1, lines, 2 * HEAD), lambda i: (i, 0, 0)),
        pl.BlockSpec((1, 1, HEAD), lambda i: (i, 0, 0)),
    ]


def grad_shapes(count, length, lines):
    return [
        jax.ShapeDtypeStruct((count * length, 8 * HEAD), LOW),
        jax.ShapeDtypeStruct((count * length, 2), WIDE),
        jax.ShapeDtypeStruct((count, lines, 2 * HEAD), WIDE),
        jax.ShapeDtypeStruct((count, 1, HEAD), WIDE),
    ]


def mixer_forward(inputs):
    count, _, length = inputs[4].shape
    return pl.pallas_call(
        mixer_forward_kernel,
        grid=(count,),
        in_specs=mixer_specs(length, inputs[5].shape[0]),
        out_specs=[pl.BlockSpec((length, 2 * HEAD), lambda i: (i, 0))] + saved_specs(length),
        out_shape=[jax.ShapeDtypeStruct((count * length, 2 * HEAD), LOW)]
        + saved_shapes(count, length),
        compiler_params=pltpu.CompilerParams(vmem_limit_bytes=32 << 20),
        name="mixer_forward",
    )(*inputs)


def mixer_backward(inputs, saved, grad):
    count, _, length = inputs[4].shape
    lines = inputs[5].shape[0]
    return pl.pallas_call(
        mixer_backward_kernel,
        grid=(count,),
        in_specs=mixer_specs(length, lines)
        + saved_specs(length)
        + [pl.BlockSpec((length, 2 * HEAD), lambda i: (i, 0))],
        out_specs=grad_specs(length, lines),
        out_shape=grad_shapes(count, length, lines),
        compiler_params=pltpu.CompilerParams(vmem_limit_bytes=32 << 20),
        name="mixer_backward",
    )(*inputs, *saved, grad)


def beside(refs, rows, lanes=slice(None)):
    return jnp.concatenate(
        [ref[z, c, rows, lanes] for ref in refs for z in range(ref.shape[0]) for c in range(2)], 1
    )


def atop(refs, lanes):
    return jnp.concatenate(
        [ref[z, c, :, lanes] for ref in refs for z in range(ref.shape[0]) for c in range(2)], 0
    )


def both(weight_refs, far, rows, lanes=slice(None)):
    return jnp.concatenate([beside(weight_refs[i][far], rows, lanes) for i in range(2)], 0)


def turned(left, right):
    return lax.dot_general(
        left, right, (((0,), (0,)), ((), ())), preferred_element_type=WIDE
    )


def straight(left, right):
    return lax.dot_general(
        left, right, (((1,), (0,)), ((), ())), preferred_element_type=WIDE
    )


def crossed(left, right):
    return lax.dot_general(
        left, right, (((1,), (1,)), ((), ())), preferred_element_type=WIDE
    )


def collect(token_refs, hold_ref):
    for step in range(2):

        @pl.when(pl.program_id(0) == step)
        def _():
            hold_ref[...] = token_refs[step][...]


def deal(pair_refs, values, lanes):
    for step in range(2):

        @pl.when(pl.program_id(0) == step)
        def _():
            pair_refs[step][:, lanes] = values.astype(LOW)


def whole(values):
    rank = len(values.shape)
    return pl.BlockSpec(values.shape, lambda i: (0,) * rank)


def split_refs(refs, sizes):
    out, start = [], 0
    for size in sizes:
        out.append(refs[start : start + size])
        start += size
    return out


def flat(grid):
    return [item for pair in grid for items in pair for item in items]


def nested(refs, grid):
    lists = split_refs(refs, [len(items) for pair in grid for items in pair])
    return [lists[:2], lists[2:]]


def call(kernel, inputs, in_specs, out_specs, out_shape, scratch, name, grid=2):
    return pl.pallas_call(
        kernel,
        grid=(grid,),
        in_specs=in_specs,
        out_specs=out_specs,
        out_shape=out_shape,
        scratch_shapes=scratch,
        compiler_params=pltpu.CompilerParams(vmem_limit_bytes=48 << 20),
        cost_estimate=pl.CostEstimate(
            flops=10 * 10**9, bytes_accessed=8 << 20, transcendentals=0
        ),
        name=name,
    )(*inputs)


QKVG = slice(0, 4 * HEAD)
OUT = slice(4 * HEAD, 5 * HEAD)


def column_forward(tokens, weights, gain, beta_weights, seg_col, seg_row, conv, head_gain):
    count, _, length = seg_row.shape
    width = tokens[0].shape[1]
    half = width // 2
    span = [slice(0, half), slice(half, width)]
    pieces = flat(weights)

    def kernel(*refs):
        token_refs, weight_refs, rest = split_refs(refs, [2, len(pieces), 17])
        gain_ref, beta_ref, col_ref, row_ref, conv_ref, head_ref = rest[:6]
        gated_ref, inverse_ref, update_ref, mixed_ref = rest[6:10]
        mixer_ref, first_ref, second_ref, beta_in_ref = rest[10:14]
        pair_refs, hold_ref = rest[14:16], rest[16]
        weight_refs = nested(weight_refs, weights)
        collect(token_refs, hold_ref)
        values = hold_ref[...].astype(WIDE)
        scale = lax.rsqrt(jnp.sum(values * values, 1, keepdims=True) * (1.0 / D) + 1e-06)
        mixer_ref[...] = (values * scale * gain_ref[...]).astype(LOW)
        masks = masks_of(col_ref[...], row_ref[0])
        kept = kept_of(col_ref[...], conv_ref.shape[0] // 3)
        mixer_in = mixer_ref[...].astype(WIDE)
        beta_in = []
        for head, projected_ref in enumerate((first_ref, second_ref)):
            projected_ref[...] = sum(
                straight(mixer_ref[:, span[far]], atop(weight_refs[head][far], QKVG))
                for far in range(2)
            )
            beta_in.append(
                jnp.sum(mixer_in * beta_ref[head : head + 1, :].astype(WIDE), 1, keepdims=True)
            )
            beta_in_ref[:, head : head + 1] = beta_in[head]
        results = forward_heads(
            [
                [ref[:, head_lanes(part)] for part in range(4)]
                for ref in (first_ref, second_ref)
            ],
            beta_in,
            [conv_ref[:, head_lanes(head)] for head in range(2)],
            kept,
            masks,
            head_ref[...],
        )
        for head, result in enumerate(results):
            own = head_lanes(head)
            gated_ref[:, own], inverse_ref[0, head], update_ref[:, own], mixed_ref[:, own] = result
        for far in range(2):
            branch = straight(gated_ref[...], both(weight_refs, far, slice(None), OUT))
            deal(pair_refs, branch, span[far])

    inputs = list(tokens) + pieces + [gain, beta_weights, seg_col, seg_row, conv, head_gain]
    in_specs = [whole(item) for item in inputs]
    in_specs[-4] = pl.BlockSpec((length, 1), lambda i: (i, 0))
    in_specs[-3] = pl.BlockSpec((1, 1, length), lambda i: (i, 0, 0))
    step = lambda lanes: pl.BlockSpec((length, lanes), lambda i: (i, 0))
    shape = lambda lanes, kind: jax.ShapeDtypeStruct((count * length, lanes), kind)
    out = jax.ShapeDtypeStruct((length, width), LOW)
    return call(
        kernel,
        inputs,
        in_specs,
        [step(2 * HEAD)]
        + saved_specs(length)
        + [step(width), step(4 * HEAD), step(4 * HEAD), step(2)]
        + [whole(out)] * 2,
        [shape(2 * HEAD, LOW)]
        + saved_shapes(count, length)
        + [shape(width, LOW), shape(4 * HEAD, WIDE), shape(4 * HEAD, WIDE), shape(2, WIDE)]
        + [out] * 2,
        [pltpu.VMEM((length, width), LOW)],
        "column_forward",
    )


def ffn_rows_of(hidden):
    return [slice(n * hidden, (n + 1) * hidden) for n in range(3)]


def column_ffn(tokens, ways, scales, weights, hidden):
    length, width = tokens[0].shape
    half = width // 2
    span = [slice(0, half), slice(half, width)]
    pieces = flat(weights)
    gate_rows, up_rows, down_rows = ffn_rows_of(hidden)

    def kernel(*refs):
        token_refs, way_refs, (scale_ref,), weight_refs, rest = split_refs(
            refs, [2, 2, 1, len(pieces), 7]
        )
        weight_refs = nested(weight_refs, weights)
        pair_refs, token_ref, way_ref = rest[:2], rest[2], rest[3]
        active_ref, gate_ref, up_ref = rest[4:]
        collect(token_refs, token_ref)
        collect(way_refs, way_ref)
        way_ref[...] = (way_ref[...].astype(WIDE) * scale_ref[...]).astype(LOW)
        gate, upward = (
            sum(crossed(token_ref[:, span[far]], both(weight_refs, far, rows)) for far in range(2))
            for rows in (gate_rows, up_rows)
        )
        sigma = sigmoid(gate)
        opened = gate * sigma
        active_ref[...] = (opened * upward).astype(LOW)
        grad = sum(
            crossed(way_ref[:, span[far]], both(weight_refs, far, down_rows)) for far in range(2)
        )
        gate_ref[...] = (grad * upward * sigma * (1.0 + gate * (1.0 - sigma))).astype(LOW)
        up_ref[...] = (grad * opened).astype(LOW)
        for far in range(2):
            values = straight(gate_ref[...], both(weight_refs, far, gate_rows)) + straight(
                up_ref[...], both(weight_refs, far, up_rows)
            )
            deal(pair_refs, values, span[far])

    inputs = list(tokens) + list(ways) + [scales] + pieces
    in_specs = [whole(item) for item in inputs]
    in_specs[4] = pl.BlockSpec((length, 1), lambda i: (i, 0))
    out = jax.ShapeDtypeStruct((length, width), LOW)
    step = lambda lanes: pl.BlockSpec((length, lanes), lambda i: (i, 0))
    shape = lambda lanes: jax.ShapeDtypeStruct((2 * length, lanes), LOW)
    return call(
        kernel,
        inputs,
        in_specs,
        [whole(out)] * 2 + [step(width)] * 2 + [step(2 * hidden)] * 3,
        [out] * 2 + [shape(width)] * 2 + [shape(2 * hidden)] * 3,
        [],
        "column_ffn",
    )


def write_beside(ref, rows, lanes, values):
    size = ref.shape[0]
    strip = values.shape[1] // (2 * size)
    for z in range(size):
        for c in range(2):
            start = (2 * z + c) * strip
            ref[z, c, rows, lanes] = values[:, start : start + strip].astype(LOW)


def column_ffn_grads(active, gate_grad, up_grad, tokens, ways, weights, grad):
    hidden = active.shape[1] // 2
    count, width = ways.shape
    length, half = count // 2, width // 2
    pieces = flat(weights)
    rows = ffn_rows_of(hidden)

    def kernel(active_ref, gate_ref, up_ref, token_ref, way_ref, *refs):
        weight_refs = nested(refs[: len(pieces)], weights)
        near_ref, far_ref, *out = refs[len(pieces) :]
        for far in range(2):
            lanes = slice(far * half, (far + 1) * half)
            values = straight(active_ref[...], both(weight_refs, far, rows[2])).astype(LOW)
            near_ref[:, lanes] = values[:length]
            far_ref[:, lanes] = values[length:]
            for n, left_ref, right_ref in (
                (0, gate_ref, token_ref), (1, up_ref, token_ref), (2, active_ref, way_ref)
            ):
                values = turned(left_ref[...], right_ref[:, lanes])
                for i in range(2):
                    write_beside(
                        out[2 * i + far],
                        rows[n],
                        slice(None),
                        values[i * hidden : (i + 1) * hidden],
                    )

    inputs = [active, gate_grad, up_grad, tokens, ways] + pieces
    out = jax.ShapeDtypeStruct((length, width), LOW)
    near, far, *grads = call(
        kernel,
        inputs,
        [whole(item) for item in inputs],
        [whole(out)] * 2 + [whole(grad)] * 4,
        [out] * 2 + [grad] * 4,
        [],
        "column_ffn_grads",
        grid=1,
    )
    return near, far, [grads[:2], grads[2:]]


def column_backward(
    grads, weights, beta_weights, seg_col, seg_row, conv, head_gain, saved, projected, beta_in
):
    count, _, length = seg_row.shape
    lines = conv.shape[0]
    width = grads[0].shape[1]
    half = width // 2
    span = [slice(0, half), slice(half, width)]
    pieces = flat(weights)

    def kernel(*refs):
        token_refs, weight_refs, rest = split_refs(refs, [2, len(pieces), 18])
        weight_refs = nested(weight_refs, weights)
        beta_ref, col_ref, row_ref, conv_ref, head_ref = rest[:5]
        inverse_ref, update_ref, mixed_ref, first_ref, second_ref, beta_in_ref = rest[5:11]
        signal_ref, beta_grad_ref, conv_grad_ref, head_grad_ref = rest[11:15]
        pair_refs, hold_ref = rest[15:17], rest[17]
        collect(token_refs, hold_ref)
        masks = masks_of(col_ref[...], row_ref[0])
        kept = kept_of(col_ref[...], conv_ref.shape[0] // 3)
        head_grad = jnp.zeros((1, HEAD), WIDE)
        beta_grads = []
        grad = sum(
            crossed(hold_ref[:, span[far]], both(weight_refs, far, slice(None), OUT))
            for far in range(2)
        )
        for head, projected_ref in enumerate((first_ref, second_ref)):
            own = head_lanes(head)
            signal_grads, beta_grad, conv_lines, gain_grad = backward_head(
                [projected_ref[:, head_lanes(part)] for part in range(4)],
                beta_in_ref[:, head : head + 1],
                conv_ref[:, own],
                kept,
                masks,
                head_ref[...],
                inverse_ref[0, head],
                update_ref[:, own],
                mixed_ref[:, own],
                grad[:, own],
            )
            head_grad = head_grad + gain_grad
            beta_grads.append(beta_grad.astype(LOW).astype(WIDE))
            beta_grad_ref[:, head : head + 1] = beta_grad
            for line, values in enumerate(conv_lines):
                conv_grad_ref[0, line : line + 1, own] = values
            for part in range(4):
                signal_ref[:, head_lanes(4 * head + part)] = signal_grads[part]
        head_grad_ref[0] = head_grad
        for far in range(2):
            values = sum(
                crossed(
                    signal_ref[:, 4 * HEAD * head : 4 * HEAD * (head + 1)],
                    atop(weight_refs[head][far], QKVG),
                )
                + beta_grads[head] * beta_ref[head : head + 1, span[far]].astype(WIDE)
                for head in range(2)
            )
            deal(pair_refs, values, span[far])

    inputs = (
        list(grads)
        + pieces
        + [beta_weights, seg_col, seg_row, conv, head_gain]
        + list(saved)
        + list(projected)
        + [beta_in]
    )
    in_specs = [whole(item) for item in inputs]
    step = lambda lanes: pl.BlockSpec((length, lanes), lambda i: (i, 0))
    in_specs[-10] = step(1)
    in_specs[-9] = pl.BlockSpec((1, 1, length), lambda i: (i, 0, 0))
    in_specs[-6:] = saved_specs(length) + [step(4 * HEAD), step(4 * HEAD), step(2)]
    out = jax.ShapeDtypeStruct((length, width), LOW)
    return call(
        kernel,
        inputs,
        in_specs,
        grad_specs(length, lines) + [whole(out)] * 2 + [step(width)],
        grad_shapes(count, length, lines)
        + [out] * 2
        + [jax.ShapeDtypeStruct((count * length, width), LOW)],
        [],
        "column_backward",
    )


def column_mixer_grads(mixer_in, signal_grads, gated, ways, grad):
    half = mixer_in.shape[1] // 2
    strip = grad.shape[2]

    def kernel(mixer_ref, signal_ref, gated_ref, way_ref, *grad_refs):
        for far in range(2):
            lanes = slice(far * half, (far + 1) * half)
            outs = turned(gated_ref[...], way_ref[:, lanes])
            for head in range(2):
                ref = grad_refs[2 * head + far]
                values = turned(
                    mixer_ref[:, lanes], signal_ref[:, 4 * HEAD * head : 4 * HEAD * (head + 1)]
                ).astype(LOW)
                for z in range(ref.shape[0]):
                    for c in range(2):
                        start = (2 * z + c) * strip
                        ref[z, c, :, QKVG] = values[start : start + strip]
                write_beside(ref, slice(None), OUT, outs[head_lanes(head)])

    inputs = [mixer_in, signal_grads, gated, ways]
    grads = call(
        kernel,
        inputs,
        [whole(item) for item in inputs],
        [whole(grad)] * 4,
        [grad] * 4,
        [],
        "column_mixer_grads",
        grid=1,
    )
    return [grads[:2], grads[2:]]


def contract(left, right, left_dim, right_dim):
    return lax.dot_general(
        left, right, (((left_dim,), (right_dim,)), ((), ())), preferred_element_type=WIDE
    )


def after(values, earlier):
    return lax.optimization_barrier((values, earlier))[0]


def exclusive_order(blocks):
    place = lax.axis_index("dmod")
    for bit in (1, 2):
        flip = (place & bit) != 0
        blocks = [jnp.where(flip, blocks[i ^ bit], blocks[i]) for i in range(4)]
    return blocks


def trade(blocks):
    return [blocks[0]] + [
        lax.ppermute(blocks[m], "dmod", [(i, i ^ m) for i in range(4)]) for m in (1, 2, 3)
    ]


def gather_width(values):
    far = lax.ppermute(values, "dmod", ACROSS)
    near = lax.ppermute(values, "dmod", CORE)
    return [values, near, far, lax.ppermute(far, "dmod", CORE)]


def scatter_width(blocks):
    near = lax.ppermute(blocks[1].astype(LOW), "dmod", CORE)
    cross = lax.ppermute(blocks[3].astype(LOW), "dmod", CORE)
    far = lax.ppermute((blocks[2] + cross.astype(WIDE)).astype(LOW), "dmod", ACROSS)
    return blocks[0] + near.astype(WIDE) + far.astype(WIDE)


def sum_pair(values):
    low = values.astype(LOW)
    return low.astype(WIDE) + lax.ppermute(low, "mp", SWAP).astype(WIDE)


def row_total(values):
    return lax.psum(values, "dmod")


class Ring:
    def __init__(self):
        self.size = lax.axis_size("dp")
        self.parts = 1

    def order(self, values):
        return values

    def gather(self, values):
        return [lax.all_gather(values, "dp", axis=1, tiled=True)]

    def scatter(self, make):
        return lax.psum_scatter(
            make(0).astype(LOW), "dp", scatter_dimension=1, tiled=True
        ).astype(WIDE)


def plane_body(
    block_input,
    segment_ids,
    group_ids,
    group_weight,
    mixer_norm,
    w_mix,
    w_beta,
    conv_kernel,
    head_norm,
    w_out,
    ffn_norm,
    w_ffn_in,
    w_ffn_down,
    cotangent,
):
    ring = Ring()
    parts = ring.parts
    micro, seqs, length, width = block_input.shape
    tokens = micro * seqs * length
    block = width // parts
    strip = w_mix.shape[0]
    span = w_mix.shape[2] // 4
    hidden = w_ffn_in.shape[2] // 4
    dmod = lax.axis_index("dmod")
    data_size = ring.size
    place = lax.axis_index("dp")

    lines = conv_kernel.shape[0] * conv_kernel.shape[1]
    pack = jnp.concatenate(
        [
            conv_kernel.reshape(-1),
            head_norm,
            mixer_norm,
            ffn_norm,
            w_beta.T.reshape(-1),
        ]
    )
    packs = lax.all_gather(pack, "dp", axis=0)
    sizes = [conv_kernel.size, head_norm.size, strip, strip, w_beta.size]
    cuts = [sum(sizes[:i]) for i in range(6)]
    conv = (
        packs[:, cuts[0] : cuts[1]]
        .reshape(data_size, lines, -1)
        .transpose(1, 0, 2)
        .reshape(lines, span)
        .astype(WIDE)
    )
    head_gain = packs[:, cuts[1] : cuts[2]].reshape(1, -1).astype(WIDE)
    gain_one = ring.order(packs[:, cuts[2] : cuts[3]].reshape(1, -1).astype(WIDE))
    gain_two = ring.order(packs[:, cuts[3] : cuts[4]].reshape(1, -1).astype(WIDE))
    beta_weights = ring.order(
        packs[:, cuts[4] : cuts[5]]
        .reshape(data_size, -1, strip)
        .transpose(1, 0, 2)
        .reshape(-1, width)
    )

    out_rows = jnp.concatenate(exclusive_order(jnp.split(w_out, 4, axis=0)), 0)
    out_halves = jnp.split(out_rows.T, 2, axis=1)
    mix_own = jnp.stack(trade(exclusive_order(jnp.split(w_mix, 4, axis=2))))
    mix_halves = [
        mix_own[:, :, :, head * HEAD : (head + 1) * HEAD].reshape(4, strip, 4 * HEAD)
        for head in (0, 1)
    ]
    ffn_own = jnp.stack(trade(exclusive_order(jnp.split(w_ffn_in, 4, axis=2))))
    ffn_halves = [ffn_own[:, :, 0], ffn_own[:, :, 1]]
    down_own = trade(exclusive_order(jnp.split(w_ffn_down, 4, axis=0)))
    down_halves = [
        jnp.stack([down_own[0].T, down_own[1].T]),
        jnp.stack([down_own[2].T, down_own[3].T]),
    ]

    def chain(half):
        first = ring.gather(out_halves[half][None])
        second = ring.gather(after(mix_halves[half], first[-1]))
        third = ring.gather(after(ffn_halves[half], second[-1]))
        fourth = ring.gather(after(down_halves[half], third[-1]))
        return first, second, third, fourth

    chains = [chain(0), chain(1)]
    out_weights = jnp.concatenate(
        [
            jnp.concatenate([part[0] for part in chains[0][0]], 0),
            jnp.concatenate([part[0] for part in chains[1][0]], 0),
        ],
        1,
    )
    mix_parts = [[part.reshape(4 * block, -1) for part in each[1]] for each in chains]
    ffn_parts = [[part.reshape(4 * block, -1) for part in each[2]] for each in chains]
    down_parts = [[part.reshape(2 * block, -1) for part in each[3]] for each in chains]

    marks = (group_ids.reshape(tokens, 1) == jnp.arange(group_weight.shape[0])[None]).astype(WIDE)
    counts = lax.psum(jnp.sum(marks, 0), "dp")
    table = group_weight * (tokens * data_size / group_weight.shape[0]) / counts
    scales = jnp.sum(marks * table, -1, keepdims=True)
    direction = ring.order(cotangent.reshape(tokens, width).astype(WIDE)) * scales
    direction_low = direction.astype(LOW)

    def by_part(slots):
        return [
            jnp.concatenate([slot[:, k * block : (k + 1) * block] for slot in slots], 1)
            for k in range(parts)
        ]

    def by_slot(pieces):
        return [
            jnp.concatenate([piece[:, m * block : (m + 1) * block] for piece in pieces], 1)
            for m in range(pieces[0].shape[1] // block)
        ]

    direction_parts = by_part(gather_width(direction_low))

    rows = ring.order(block_input.reshape(tokens, width).astype(WIDE))
    first_scale = lax.rsqrt(row_total(jnp.sum(rows * rows, -1, keepdims=True)) / D + 1e-06)
    mixer_in = (rows * first_scale * gain_one).astype(LOW)
    mixer_parts = by_part(gather_width(mixer_in))
    projected = [
        sum(jnp.dot(mixer_parts[k], mix_parts[half][k], preferred_element_type=WIDE) for k in range(parts))
        for half in (0, 1)
    ]
    beta_all = row_total(contract(beta_weights, mixer_in, 1, 1))
    heads = span // HEAD
    beta_in = lax.dynamic_slice_in_dim(beta_all, dmod * heads, heads, 0).T
    seg_col = segment_ids.reshape(tokens, 1)
    seg_row = segment_ids.reshape(micro * seqs, 1, length)
    mixer_args = list(projected) + [
        beta_in, seg_col, seg_row, conv, head_gain
    ]
    gated, *saved = mixer_forward(mixer_args)
    gated_all = jnp.concatenate(gather_width(gated), 1)
    middle = rows + sum_pair(contract(gated_all, out_weights, 1, 1))

    second_scale = lax.rsqrt(row_total(jnp.sum(middle * middle, -1, keepdims=True)) / D + 1e-06)
    ffn_in = (middle * second_scale * gain_two).astype(LOW)
    ffn_in_parts = by_part(gather_width(ffn_in))
    gate, upward = (
        sum(jnp.dot(ffn_in_parts[k], ffn_parts[half][k], preferred_element_type=WIDE) for k in range(parts))
        for half in (0, 1)
    )
    sigma = sigmoid(gate)
    active = (gate * sigma * upward).astype(LOW)
    down_slots = sum(
        (
            by_slot([contract(active, down_parts[half][k], 1, 1) for k in range(parts)])
            for half in (0, 1)
        ),
        [],
    )
    result = middle + sum_pair(scatter_width(down_slots))
    out = ring.order(result).astype(LOW).reshape(block_input.shape)

    down_grads = [
        ring.scatter(
            lambda k: contract(
                direction_parts[k][:, 2 * half * block : 2 * (half + 1) * block], active, 0, 0
            ).reshape(2, block, hidden)
        )
        for half in (0, 1)
    ]
    active_grad = sum(
        jnp.dot(
            direction_parts[k][:, 2 * half * block : 2 * (half + 1) * block],
            down_parts[half][k],
            preferred_element_type=WIDE,
        )
        for k in range(parts)
        for half in (0, 1)
    )
    gate_grad = (active_grad * upward * sigma * (1.0 + gate * (1.0 - sigma))).astype(LOW)
    upward_grad = (active_grad * gate * sigma).astype(LOW)
    ffn_slots = by_slot(
        [
            contract(gate_grad, ffn_parts[0][k], 1, 1) + contract(upward_grad, ffn_parts[1][k], 1, 1)
            for k in range(parts)
        ]
    )
    ffn_grads = [
        ring.scatter(lambda k: contract(ffn_in_parts[k], grad, 0, 0).reshape(4, block, hidden))
        for grad in (gate_grad, upward_grad)
    ]
    ffn_in_grad = sum_pair(scatter_width(ffn_slots))
    weighted_two = ffn_in_grad * gain_two
    norm_two_grad = jnp.sum(ffn_in_grad * middle * second_scale, 0)
    inner_two = row_total(jnp.sum(weighted_two * middle, -1, keepdims=True))
    middle_grad = (
        direction + second_scale * weighted_two - middle * (second_scale**3 * inner_two / D)
    )

    branch_low = middle_grad.astype(LOW)
    out_grads = [
        ring.scatter(
            lambda k: contract(
                branch_low[:, k * block : (k + 1) * block],
                gated_all[:, 2 * half * span : 2 * (half + 1) * span],
                0,
                0,
            )[None]
        )
        for half in (0, 1)
    ]
    gated_slots = jnp.split(jnp.dot(branch_low, out_weights, preferred_element_type=WIDE), 4, axis=1)
    gated_grad = scatter_width(gated_slots)
    projected_grad, beta_grad, conv_grad, head_grad = mixer_backward(
        mixer_args, saved, gated_grad
    )
    projected_slots = gather_width(projected_grad)
    mix_grads = [
        ring.scatter(
            lambda k: contract(
                mixer_in[:, k * block : (k + 1) * block],
                jnp.concatenate(projected_slots[2 * half : 2 * half + 2], 1),
                0,
                0,
            )[None]
        )
        for half in (0, 1)
    ]
    beta_slots = jnp.concatenate(
        exclusive_order(gather_width(beta_grad.T.astype(LOW))), 0
    )
    beta_weight_grad = contract(beta_slots, mixer_in, 1, 0)
    mixer_slots = by_slot(
        [
            contract(projected_grad[:, : 2 * span], mix_parts[0][k], 1, 1)
            + contract(projected_grad[:, 2 * span :], mix_parts[1][k], 1, 1)
            for k in range(parts)
        ]
    )
    mixer_grad = sum_pair(scatter_width(mixer_slots) + contract(beta_slots, beta_weights, 0, 0))
    weighted_one = mixer_grad * gain_one
    norm_one_grad = jnp.sum(mixer_grad * rows * first_scale, 0)
    inner_one = row_total(jnp.sum(weighted_one * rows, -1, keepdims=True))
    grad_input = ring.order(
        middle_grad + first_scale * weighted_one - rows * (first_scale**3 * inner_one / D)
    ).reshape(block_input.shape)

    head_total = lax.psum(jnp.sum(head_grad, (0, 1)), ("dp", "mp", "dmod"))
    head_out = lax.dynamic_slice_in_dim(head_total, place * head_norm.size, head_norm.size, 0)
    small = jnp.concatenate(
        [
            jnp.sum(conv_grad, 0),
            ring.order(jnp.stack([norm_one_grad, norm_two_grad]))
            .reshape(2, data_size, -1)
            .transpose(1, 0, 2)
            .reshape(data_size, -1)
            .reshape(-1)
            .reshape(-1, span),
            ring.order(beta_weight_grad)
            .reshape(-1, data_size, strip)
            .transpose(1, 0, 2)
            .reshape(-1, span),
        ],
        0,
    )
    conv_part = (
        small[:lines].reshape(lines, data_size, -1).transpose(1, 0, 2).reshape(data_size, -1)
    )
    norm_part = small[lines : lines + 2 * width // span].reshape(data_size, -1)
    beta_part = small[lines + 2 * width // span :].reshape(data_size, -1)
    small_own = lax.psum_scatter(
        jnp.concatenate([conv_part, norm_part, beta_part], 1), "dp", scatter_dimension=0
    )
    conv_out = small_own[: conv_kernel.size].reshape(conv_kernel.shape)
    norm_one_out = small_own[conv_kernel.size : conv_kernel.size + strip]
    norm_two_out = small_own[conv_kernel.size + strip : conv_kernel.size + 2 * strip]
    beta_out = small_own[conv_kernel.size + 2 * strip :].reshape(-1, strip).T

    def placed(blocks):
        return exclusive_order(trade([values.astype(LOW) for values in blocks]))

    ffn_out = jnp.stack(
        [
            jnp.concatenate([values.astype(WIDE) for values in placed(list(grad))], 1)
            for grad in ffn_grads
        ],
        1,
    )
    down_out = jnp.concatenate(
        [
            values.astype(WIDE).T
            for values in placed(list(down_grads[0]) + list(down_grads[1]))
        ],
        0,
    )
    out_out = jnp.concatenate(
        exclusive_order(jnp.split(jnp.concatenate([grad[0] for grad in out_grads], 1).T, 4, axis=0)),
        0,
    )
    mix_blocks = sum((jnp.split(grad[0], 2, axis=1) for grad in mix_grads), [])
    mix_out = jnp.concatenate(
        [
            values.reshape(strip, 2, 4, HEAD).transpose(0, 2, 1, 3).reshape(strip, 4, span)
            for values in exclusive_order(mix_blocks)
        ],
        2,
    )
    return (
        out,
        grad_input,
        norm_one_out,
        mix_out,
        beta_out,
        conv_out,
        head_out,
        out_out,
        norm_two_out,
        ffn_out,
        down_out,
    )


def exchange(values, axis):
    return lax.all_to_all(values, axis, 0, 0, tiled=True)


def swap_mp(values):
    return lax.ppermute(values, "mp", SWAP)


def swap_core(values):
    return lax.ppermute(values, "dmod", CORE)


def swap_across(values):
    return lax.ppermute(values, "dmod", ACROSS)


def swap_dp(values, k):
    return lax.ppermute(values, "dp", [(i, i ^ k) for i in range(lax.axis_size("dp"))])


def trade_blocks(blocks, axis, place):
    size = len(blocks)
    blocks = by_difference(blocks, place)
    moved = [blocks[0]] + [
        lax.ppermute(blocks[k], axis, [(i, i ^ k) for i in range(size)]) for k in range(1, size)
    ]
    return by_difference(moved, place)


def by_difference(blocks, place):
    bit = 1
    while bit < len(blocks):
        flip = (place & bit) != 0
        blocks = [jnp.where(flip, blocks[i ^ bit], blocks[i]) for i in range(len(blocks))]
        bit *= 2
    return blocks


def everyone(values, place):
    size = lax.axis_size("dp")
    values = values[None]
    bit = 1
    while bit < size:
        values = jnp.concatenate(turn((place & bit) != 0, (values, swap_dp(values, bit))), 0)
        bit *= 2
    return values


def turn(flag, pair):
    return jnp.where(flag, pair[1], pair[0]), jnp.where(flag, pair[0], pair[1])


def chip_blocks(core, pair):
    keep, send = turn(core, pair)
    return jnp.stack(turn(core, (keep, swap_core(send))), 1)


def along_column(core, pair, earlier=None):
    both = chip_blocks(core, pair)
    if earlier is not None:
        both = after(both, earlier)
    return exchange(both, "dp")


def gather_columns(values, earlier=None, later=None):
    if earlier is not None:
        values = after(values, earlier)
    half = values.shape[0] // 2
    over = swap_mp(values)
    far = swap_across(values)
    corner = (over[:half], far[half:])
    if later is not None:
        corner = after(corner, later)
    both = [swap_across(corner[0]), swap_mp(corner[1])]
    return [[[values], [far]], [[over], both]]


def wide(values):
    return values.astype(WIDE)


def scatter_send(grid):
    half = grid[0][0].shape[0] // 2
    return (
        jnp.concatenate([grid[1][0][:half], grid[1][1][:half]], 0),
        jnp.concatenate([grid[0][1][half:], grid[1][1][half:]], 0),
    )


def scatter_turn(grid, sent):
    half = grid[0][0].shape[0] // 2
    top = wide(grid[0][1][:half]) + wide(sent[0][half:])
    low = wide(grid[1][0][half:]) + wide(sent[1][half:])
    return top.astype(LOW), low.astype(LOW)


def scatter_end(grid, sent, back):
    half = grid[0][0].shape[0] // 2
    top = wide(grid[0][0][:half]) + wide(sent[0][:half]) + wide(swap_across(back[0]))
    low = wide(grid[0][0][half:]) + wide(sent[1][:half]) + wide(swap_mp(back[1]))
    return jnp.concatenate([top, low], 0).astype(LOW)


def column_tokens(values):
    size = lax.axis_size("dp")
    moved = [values] + [swap_dp(values, k) for k in range(1, size)]
    mine = jnp.concatenate(by_difference(moved, lax.axis_index("dp")), 0)
    return [mine, swap_core(mine)]


def column_chip(near, far):
    return (wide(near) + wide(swap_core(far))).astype(LOW)


def column_total(chip):
    size = lax.axis_size("dp")
    moved = exchange(chip, "dp").reshape(size, chip.shape[0] // size, -1)
    return jnp.sum(wide(moved), 0)


def column_body(
    block_input,
    segment_ids,
    group_ids,
    group_weight,
    mixer_norm,
    w_mix,
    w_beta,
    conv_kernel,
    head_norm,
    w_out,
    ffn_norm,
    w_ffn_in,
    w_ffn_down,
    cotangent,
):
    place = lax.axis_index("dp")
    size = lax.axis_size("dp")
    side = lax.axis_index("mp")
    dmod = lax.axis_index("dmod")
    row, core = dmod // 2, dmod % 2
    at_far_side, at_far_row, at_core = side == 1, row == 1, core == 1
    micro, _, length, width = block_input.shape
    share = length // size
    strip = w_mix.shape[0]
    groups = group_weight.shape[0]
    group_heads = w_beta.shape[1]
    hidden = w_ffn_down.shape[0] // (2 * size)
    span = 2 * width

    def to_column(values):
        lead = values.shape[:-1]
        values = values.reshape(lead + (2, 2, size, strip))
        values = jnp.swapaxes(values, -2, -3).reshape(lead + (2, span))
        return jnp.concatenate(turn(at_far_row, (values[..., 0, :], values[..., 1, :])), -1)

    def from_column(values):
        lead = values.shape[:-1]
        halves_of = turn(at_far_row, (values[..., :span], values[..., span:]))
        values = jnp.stack(halves_of, -2).reshape(lead + (2, size, 2, strip))
        return jnp.swapaxes(values, -2, -3).reshape(lead + (2 * span,))

    def over_dp(values):
        values = values.reshape(micro, size, share, width)
        moved = trade_blocks([values[:, z] for z in range(size)], "dp", place)
        moved = jnp.where(at_far_side, jnp.stack(moved[2:]), jnp.stack(moved[:2]))
        return moved.reshape(4, share, width)

    def over_dmod(moved):
        moved = trade_blocks([moved[j] for j in range(4)], "dmod", dmod)
        return to_column(jnp.concatenate(moved, 1))

    def tokens_out(values):
        blocks = jnp.split(from_column(values), 4, axis=1)
        moved = jnp.stack(trade_blocks(blocks, "dmod", dmod)).reshape(2, micro, share, width)
        moved = jnp.concatenate(turn(at_far_side, (moved, swap_mp(moved))), 0)
        moved = trade_blocks([moved[z] for z in range(size)], "dp", place)
        return jnp.stack(moved, 1).reshape(block_input.shape)

    blocks = w_mix.reshape(strip, 4, 2, size, HEAD).transpose(2, 3, 0, 1, 4)
    blocks = blocks.reshape(2, size, strip, 4 * HEAD)
    blocks = jnp.concatenate([blocks, w_out.reshape(2, size, HEAD, strip)], 3)
    mix_blocks = chip_blocks(at_core, (blocks[0], blocks[1]))
    mix_pieces = exchange(mix_blocks, "dp")
    block_input, cotangent, conv_kernel, w_ffn_in, w_ffn_down = after(
        (block_input, cotangent, conv_kernel, w_ffn_in, w_ffn_down), mix_blocks
    )
    blocks = jnp.concatenate(
        [
            w_ffn_in.transpose(1, 2, 0).reshape(2, 2 * size, hidden, strip),
            w_ffn_down.reshape(1, 2 * size, hidden, strip),
        ],
        0,
    )
    blocks = blocks.transpose(1, 0, 2, 3).reshape(2, size, 3 * hidden, strip)
    ffn_blocks = chip_blocks(at_core, (blocks[0], blocks[1]))

    small = [
        conv_kernel.reshape(-1),
        head_norm,
        mixer_norm,
        ffn_norm,
        w_beta.T.reshape(-1),
        segment_ids.reshape(-1).astype(LOW),
        group_ids.reshape(-1).astype(LOW),
    ]
    count = sum(item.size for item in small)
    pack = jnp.concatenate(small + [jnp.zeros((-count % HEAD,), LOW)]).reshape(-1, HEAD)
    packs = everyone(pack, place)
    packs = jnp.stack(turn(at_far_side, (packs, swap_mp(packs))))
    packs = jnp.stack(turn(at_core, (packs, swap_core(packs))))
    packs = jnp.stack(turn(at_far_row, (packs, swap_across(packs))))
    packs = packs.reshape(2, 2, 2, size, -1)

    tokens_low, way_moved = over_dp(block_input), over_dp(cotangent)
    tokens_low = over_dmod(after(tokens_low, (mix_pieces, packs, ffn_blocks)))
    rows = wide(tokens_low)
    tokens_pair = column_tokens(tokens_low)
    mix_weights = gather_columns(mix_pieces)
    ffn_pieces = exchange(ffn_blocks, "dp")
    way_low = over_dmod(after(way_moved, tokens_pair[0]))

    fields = []
    start = 0
    for item in small:
        fields.append(packs[..., start : start + item.size])
        start += item.size
    lines = conv_kernel.shape[0] * conv_kernel.shape[1]
    heads = 2 * group_heads
    local_head = size * core + place
    own_heads = [group_heads * side + local_head, group_heads * (1 - side) + local_head]
    conv_all = (
        fields[0]
        .reshape(2, 2, 2, size, lines, -1)
        .transpose(4, 2, 0, 1, 3, 5)
        .reshape(lines, heads * HEAD)
    )
    conv = wide(
        jnp.concatenate(
            [lax.dynamic_slice_in_dim(conv_all, head * HEAD, HEAD, 1) for head in own_heads], 1
        )
    )
    head_gain = wide(fields[1][0, 0, 0].reshape(1, HEAD))
    gain_one = to_column(wide(fields[2][:, :, 0].reshape(1, -1)))
    gain_two = to_column(wide(fields[3][:, :, 0].reshape(1, -1)))
    beta_rows = (
        fields[4]
        .reshape(2, 2, 2, size, group_heads, strip)
        .transpose(2, 4, 0, 1, 3, 5)
        .reshape(heads, -1)
    )
    beta_weights = to_column(
        jnp.concatenate([lax.dynamic_slice_in_dim(beta_rows, head, 1, 0) for head in own_heads], 0)
    )
    sequence = 2 * side + row
    segments = lax.dynamic_index_in_dim(fields[5][0, 0, 0], sequence, 0, keepdims=False)
    segments = segments.reshape(micro, length).astype(jnp.int32)
    segments = jnp.concatenate(turn(at_core, (segments[:1], segments[1:])), 0)
    seg_col = segments.reshape(-1, 1)
    seg_row = segments.reshape(micro, 1, length)
    all_groups = fields[6][0, 0, 0].reshape(-1).astype(jnp.int32)
    names = jnp.arange(groups, dtype=jnp.int32)
    counts = jnp.sum((all_groups[:, None] == names[None]).astype(WIDE), 0)
    table = group_weight * (all_groups.shape[0] / groups) / counts
    own_groups = lax.dynamic_slice_in_dim(all_groups, sequence * micro * length, micro * length, 0)
    scales = jnp.sum((own_groups[:, None] == names[None]).astype(WIDE) * table, -1, keepdims=True)
    scales = jnp.concatenate(turn(at_core, (scales[:length], scales[length:])), 0)

    constants = [beta_weights, seg_col, seg_row, conv, head_gain]
    gated, inverse, update, mixed, mixer_in, *projected, beta_in, near, far = column_forward(
        tokens_pair, mix_weights, gain_one, *constants
    )
    middle = rows + column_total(after(column_chip(near, far), ffn_pieces))

    second_scale = lax.rsqrt(jnp.mean(middle * middle, -1, keepdims=True) + 1e-06)
    ffn_low = (middle * second_scale * gain_two).astype(LOW)
    way_pair = column_tokens(after(way_low, middle))
    direction = wide(way_low) * lax.dynamic_slice_in_dim(scales, place * share, share, 0)
    ffn_pair = column_tokens(ffn_low)
    ffn_weights = gather_columns(ffn_pieces, mix_weights[1][1])
    near, far, ffn_in, directions, active, gate_grad, up_grad = column_ffn(
        ffn_pair, way_pair, scales, ffn_weights, hidden
    )
    chip = column_chip(near, far)
    ffn_in_grad = column_total(chip)
    near, far, ffn_grads = column_ffn_grads(
        after(active, chip),
        gate_grad,
        up_grad,
        ffn_in,
        directions,
        ffn_weights,
        jax.ShapeDtypeStruct((size, 2, 3 * hidden, strip), LOW),
    )
    out_chip = column_chip(near, far)
    ffn_sent = scatter_send(ffn_grads)
    ffn_in_grad = after(ffn_in_grad, out_chip)
    ffn_sent = swap_mp(ffn_sent[0]), swap_across(ffn_sent[1])

    weighted_two = ffn_in_grad * gain_two
    norm_two_grad = jnp.sum(ffn_in_grad * middle * second_scale, 0, keepdims=True)
    inner_two = jnp.mean(weighted_two * middle, -1, keepdims=True)
    middle_grad = (
        direction + second_scale * weighted_two - middle * (second_scale**3 * inner_two)
    )
    branch_pair = column_tokens(middle_grad.astype(LOW))
    down_sum = column_total(after(out_chip, branch_pair[0]))
    ffn_back = scatter_turn(ffn_grads, ffn_sent)

    signal_grads, beta_grad, conv_grad, head_grad, near, far, branch_all = column_backward(
        branch_pair,
        mix_weights,
        *constants,
        (inverse, update, mixed),
        projected,
        beta_in,
    )
    mix_grads = column_mixer_grads(
        mixer_in,
        signal_grads,
        gated,
        branch_all,
        jax.ShapeDtypeStruct((size, 2, strip, 5 * HEAD), LOW),
    )
    chip = column_chip(near, far)
    mixer_grad = column_total(chip)
    ffn_total = scatter_end(ffn_grads, ffn_sent, ffn_back)
    mix_sent = scatter_send(mix_grads)
    mix_sent = after((swap_mp(mix_sent[0]), swap_across(mix_sent[1])), mixer_grad)
    mix_total = scatter_end(mix_grads, mix_sent, scatter_turn(mix_grads, mix_sent))
    out_low = (middle + after(down_sum, mixer_grad)).astype(LOW)

    def placed(total, earlier=None):
        return along_column(at_core, (total[:, 0], total[:, 1]), earlier).transpose(1, 0, 2, 3)

    ffn_pieces = placed(ffn_total)
    ffn_out = wide(
        ffn_pieces[:, :, : 2 * hidden]
        .reshape(2 * size, 2, hidden, strip)
        .transpose(1, 0, 2, 3)
        .reshape(2, -1, strip)
        .transpose(2, 0, 1)
    )
    down_out = wide(ffn_pieces[:, :, 2 * hidden :].reshape(-1, strip))
    mix_pieces = placed(mix_total, ffn_pieces).reshape(2 * size, strip, 5, HEAD)
    mix_out = wide(mix_pieces[:, :, :4].transpose(1, 2, 0, 3).reshape(strip, 4, -1))
    out_out = wide(mix_pieces[:, :, 4].reshape(-1, strip))
    beta_weight_grad = contract(beta_grad.astype(LOW), mixer_in, 0, 0)
    weighted_one = mixer_grad * gain_one
    first_scale = lax.rsqrt(jnp.mean(rows * rows, -1, keepdims=True) + 1e-06)
    norm_one_grad = jnp.sum(mixer_grad * rows * first_scale, 0, keepdims=True)
    inner_one = jnp.mean(weighted_one * rows, -1, keepdims=True)
    grad_low = (
        middle_grad + first_scale * weighted_one - rows * (first_scale**3 * inner_one)
    ).astype(LOW)
    out = tokens_out(out_low)
    grad_input = wide(tokens_out(grad_low))

    conv_sides = jnp.stack(turn(at_far_side, jnp.split(jnp.sum(conv_grad, 0), 2, axis=1)))
    beta_sides = from_column(
        jnp.concatenate(turn(at_far_side, (beta_weight_grad[:1], beta_weight_grad[1:])), 0)
    )
    vector = jnp.concatenate(
        [
            conv_sides.reshape(-1, HEAD),
            beta_sides.reshape(-1, HEAD),
            from_column(norm_one_grad).reshape(-1, HEAD),
            from_column(norm_two_grad).reshape(-1, HEAD),
            jnp.sum(head_grad, 0),
        ]
    )
    vector = vector + swap_mp(vector)
    vector = vector + swap_across(vector)
    vectors = jnp.stack(turn(at_core, (vector, swap_core(vector))))
    vectors = everyone(vectors, place)
    ends = [2 * lines, 2 * lines + 4 * span // HEAD]
    own_width = dmod * width + place * strip
    taps_own = conv_kernel.shape[2]
    at = (dmod * size + place) * taps_own
    conv_head = at // HEAD
    conv_out = lax.dynamic_slice(
        vectors,
        (conv_head % size, conv_head // size, side * lines, at % HEAD),
        (1, 1, lines, taps_own),
    ).reshape(conv_kernel.shape)
    beta_out = (
        lax.dynamic_slice(
            vectors[:, :, ends[0] : ends[1]].reshape(size, 2, 2, 2 * span),
            (0, 0, side, own_width),
            (size, 2, 1, strip),
        )
        .reshape(size, 2, strip)
        .transpose(2, 1, 0)
        .reshape(strip, group_heads)
    )
    sums = jnp.sum(vectors[:, :, ends[1] :], (0, 1))
    norms = sums[:-1].reshape(2, -1)
    norm_one_out, norm_two_out = (
        lax.dynamic_slice_in_dim(norms[i], own_width, strip, 0) for i in (0, 1)
    )
    head_out = lax.dynamic_slice_in_dim(sums[-1], place * head_norm.size, head_norm.size, 0)
    return (
        out,
        grad_input,
        norm_one_out,
        mix_out,
        beta_out,
        conv_out,
        head_out,
        out_out,
        norm_two_out,
        ffn_out,
        down_out,
    )


def solution(mesh):
    sizes = dict(mesh.shape)
    columns = sizes["mp"] * sizes["dmod"] // 2
    body = column_body if columns == sizes["dp"] else plane_body
    wide = P(("dmod", "dp"))
    tokens = P(None, "dp", None, "dmod")
    weights = (
        wide,
        P(("dmod", "dp"), None, "mp"),
        P(("dmod", "dp"), "mp"),
        P(None, None, ("mp", "dmod", "dp")),
        P("dp"),
        P("mp", ("dmod", "dp")),
        wide,
        P(("dmod", "dp"), None, "mp"),
        P("mp", ("dmod", "dp")),
    )
    ids = P(None, "dp", None)
    return jax.shard_map(
        body,
        mesh=mesh,
        in_specs=(tokens, ids, ids, P()) + weights + (tokens,),
        out_specs=(tokens, tokens) + weights,
        check_vma=False,
    )
```

```python
import jax
import jax.numpy as jnp
from jax import lax
from jax.experimental import pallas as pl
from jax.experimental.pallas import tpu as pltpu
from jax.sharding import PartitionSpec as P

D = 2048
HEAD = 128
LOW = jnp.bfloat16
WIDE = jnp.float32
LONGEST_RING = 1
CORE = [(i, i ^ 1) for i in range(4)]
ACROSS = [(i, i ^ 2) for i in range(4)]
SWAP = [(0, 1), (1, 0)]


def halves(values):
    high = values.astype(LOW)
    return high, (values - high.astype(WIDE)).astype(LOW)


def product(left, right, left_dim, right_dim):
    def one(a, b):
        return lax.dot_general(
            a, b, (((left_dim,), (right_dim,)), ((), ())), preferred_element_type=WIDE
        )

    return one(left[0], right[0]) + (one(left[0], right[1]) + one(left[1], right[0]))


def sigmoid(values):
    return 1.0 / (1.0 + jnp.exp(-values))


def masks_of(seg_col, seg_row):
    length = seg_col.shape[0]
    rows = lax.broadcasted_iota(jnp.int32, (length, length), 0)
    cols = lax.broadcasted_iota(jnp.int32, (length, length), 1)
    same = seg_col == seg_row
    return rows, cols, same & (cols < rows), same & (cols <= rows)


def kept_of(seg_col, taps):
    length = seg_col.shape[0]
    wide = jnp.broadcast_to(seg_col, (length, HEAD))
    place = lax.broadcasted_iota(jnp.int32, (length, HEAD), 0)
    return [
        ((pltpu.roll(wide, shift, 0) == wide) & (place >= shift)).astype(WIDE)
        for shift in range(1, taps)
    ]


def convolve(signal, kernel, kept):
    taps = kernel.shape[0]
    total = signal * kernel[taps - 1 : taps]
    for shift in range(1, taps):
        moved = pltpu.roll(signal, shift, 0) * kept[shift - 1]
        total = total + moved * kernel[taps - 1 - shift : taps - shift]
    return total


def single(left, right):
    return lax.dot_general(
        left.astype(LOW),
        right.astype(LOW),
        (((1,), (0,)), ((), ())),
        preferred_element_type=WIDE,
    )


def invert(lowers, rows, cols):
    length = lowers[0].shape[0]
    eye = (rows == cols).astype(WIDE)
    pair = (rows // 2) == (cols // 2)
    inverses = [eye - jnp.where(pair, lower, 0.0) for lower in lowers]
    size = 2
    while size < length:
        cross = ((rows // (2 * size)) == (cols // (2 * size))) & ((rows // size) != (cols // size))
        steps = [
            single(inverse, jnp.where(cross, lower, 0.0))
            for inverse, lower in zip(inverses, lowers)
        ]
        inverses = [
            inverse - single(step, inverse) for step, inverse in zip(steps, inverses)
        ]
        size *= 2
    rests = [
        eye - inverse - product(halves(lower), halves(inverse), 1, 0)
        for inverse, lower in zip(inverses, lowers)
    ]
    return [inverse + single(inverse, rest) for inverse, rest in zip(inverses, rests)]


def forward_heads(signals, beta_in, conv, kept, masks, gain):
    rows, cols, strict, inclusive = masks
    taps = conv[0].shape[0] // 3
    lowers, held = [], []
    for head in range(len(signals)):
        convolved = []
        for part in range(3):
            kernel = conv[head][part * taps : (part + 1) * taps]
            pre = convolve(signals[head][part], kernel, kept)
            convolved.append(pre * sigmoid(pre))
        query = convolved[0] * (
            lax.rsqrt(jnp.sum(convolved[0] * convolved[0], 1, keepdims=True) + 1e-06) * HEAD**-0.5
        )
        key = convolved[1] * lax.rsqrt(
            jnp.sum(convolved[1] * convolved[1], 1, keepdims=True) + 1e-06
        )
        beta = sigmoid(beta_in[head])
        key_parts = halves(key)
        gram = product(key_parts, key_parts, 1, 1)
        lowers.append(jnp.where(strict, gram * beta, 0.0))
        scores = jnp.where(inclusive, product(halves(query), key_parts, 1, 1), 0.0)
        held.append((halves(scores), halves(convolved[2] * beta)))
    out = []
    for head, inverse in enumerate(invert(lowers, rows, cols)):
        scores, target = held[head]
        update = product(halves(inverse), target, 1, 0)
        mixed = product(scores, halves(update), 1, 0)
        scale = lax.rsqrt(jnp.sum(mixed * mixed, 1, keepdims=True) * (1.0 / HEAD) + 1e-05)
        gate = signals[head][3]
        gated = (mixed * scale * gain * (gate * sigmoid(gate))).astype(LOW)
        out.append((gated, inverse, update, mixed))
    return out


def backward_head(signals, beta_in, conv, kept, masks, gain, inverse, update, mixed, grad):
    rows, cols, strict, inclusive = masks
    length = grad.shape[0]
    taps = conv.shape[0] // 3
    before, gates, convolved = [], [], []
    for part in range(3):
        pre = convolve(signals[part], conv[part * taps : (part + 1) * taps], kept)
        before.append(pre)
        gates.append(sigmoid(pre))
        convolved.append(pre * gates[part])
    query_unit = lax.rsqrt(jnp.sum(convolved[0] * convolved[0], 1, keepdims=True) + 1e-06)
    key_unit = lax.rsqrt(jnp.sum(convolved[1] * convolved[1], 1, keepdims=True) + 1e-06)
    query = convolved[0] * (query_unit * HEAD**-0.5)
    key = convolved[1] * key_unit
    beta = sigmoid(beta_in)
    gate = signals[3]
    gate_sigma = sigmoid(gate)
    opened = gate * gate_sigma
    scale = lax.rsqrt(jnp.sum(mixed * mixed, 1, keepdims=True) * (1.0 / HEAD) + 1e-05)
    normed = mixed * scale
    head_grad = jnp.sum(grad * opened * normed, 0, keepdims=True)
    inner = grad * opened * gain
    mixed_grad = scale * inner - mixed * (
        scale * scale * scale * (jnp.sum(inner * mixed, 1, keepdims=True) * (1.0 / HEAD))
    )
    gate_grad = grad * normed * gain * gate_sigma * (1.0 + gate * (1.0 - gate_sigma))
    key_parts = halves(key)
    query_parts = halves(query)
    update_parts = halves(update)
    mixed_parts = halves(mixed_grad)
    gram = product(key_parts, key_parts, 1, 1)
    scores = jnp.where(inclusive, product(query_parts, key_parts, 1, 1), 0.0)
    scores_grad = halves(jnp.where(inclusive, product(mixed_parts, update_parts, 1, 1), 0.0))
    update_grad = product(halves(scores), mixed_parts, 0, 0)
    solved = product(halves(inverse), halves(update_grad), 0, 0)
    system_grad = jnp.where(strict, -product(halves(solved), update_parts, 1, 1), 0.0)
    gram_grad = halves(system_grad * beta)
    query_grad = product(scores_grad, key_parts, 1, 0)
    key_grad = (
        product(scores_grad, query_parts, 0, 0)
        + product(gram_grad, key_parts, 1, 0)
        + product(gram_grad, key_parts, 0, 0)
    )
    beta_grad = jnp.sum(system_grad * gram, 1, keepdims=True) + jnp.sum(
        solved * convolved[2], 1, keepdims=True
    )
    beta_grad = beta_grad * beta * (1.0 - beta)
    conv_grads = [
        HEAD**-0.5
        * (
            query_grad * query_unit
            - convolved[0]
            * (
                query_unit
                * query_unit
                * query_unit
                * jnp.sum(convolved[0] * query_grad, 1, keepdims=True)
            )
        ),
        key_grad * key_unit
        - convolved[1]
        * (key_unit * key_unit * key_unit * jnp.sum(convolved[1] * key_grad, 1, keepdims=True)),
        solved * beta,
    ]
    lines = [None] * (3 * taps)
    signal_grads = []
    for part in range(3):
        sigma = gates[part]
        error = conv_grads[part] * sigma * (1.0 + before[part] * (1.0 - sigma))
        kernel = conv[part * taps : (part + 1) * taps]
        total = error * kernel[taps - 1 : taps]
        last = part * taps + taps - 1
        lines[last] = jnp.sum(error * signals[part], 0, keepdims=True)
        for shift in range(1, taps):
            held = error * kept[shift - 1]
            lines[last - shift] = jnp.sum(
                held * pltpu.roll(signals[part], shift, 0), 0, keepdims=True
            )
            total = total + pltpu.roll(held, length - shift, 0) * (
                kernel[taps - 1 - shift : taps - shift]
            )
        signal_grads.append(total.astype(LOW))
    signal_grads.append(gate_grad.astype(LOW))
    return signal_grads, beta_grad, lines, head_grad


def head_lanes(head):
    return slice(head * HEAD, (head + 1) * HEAD)


def mixer_forward_kernel(*refs):
    parts = refs[:2]
    beta_ref, col_ref, row_ref, conv_ref, head_ref = refs[2:7]
    gated_ref, inverse_ref, update_ref, mixed_ref = refs[7:]
    masks = masks_of(col_ref[...], row_ref[0])
    kept = kept_of(col_ref[...], conv_ref.shape[0] // 3)
    results = forward_heads(
        [[parts[head][:, head_lanes(part)] for part in range(4)] for head in range(2)],
        [beta_ref[:, head : head + 1] for head in range(2)],
        [conv_ref[:, head_lanes(head)] for head in range(2)],
        kept,
        masks,
        head_ref[...],
    )
    for head, result in enumerate(results):
        own = head_lanes(head)
        gated_ref[:, own], inverse_ref[0, head], update_ref[:, own], mixed_ref[:, own] = result


def mixer_backward_kernel(*refs):
    parts = refs[:2]
    beta_ref, col_ref, row_ref, conv_ref, head_ref = refs[2:7]
    inverse_ref, update_ref, mixed_ref, grad_ref = refs[7:11]
    out_ref, beta_grad_ref, conv_grad_ref, head_grad_ref = refs[11:]
    masks = masks_of(col_ref[...], row_ref[0])
    kept = kept_of(col_ref[...], conv_ref.shape[0] // 3)
    head_grad = jnp.zeros((1, HEAD), WIDE)
    for head in range(2):
        own = head_lanes(head)
        grads, beta_grad, lines, gain_grad = backward_head(
            [parts[head][:, head_lanes(part)] for part in range(4)],
            beta_ref[:, head : head + 1],
            conv_ref[:, own],
            kept,
            masks,
            head_ref[...],
            inverse_ref[0, head],
            update_ref[:, own],
            mixed_ref[:, own],
            grad_ref[:, own],
        )
        head_grad = head_grad + gain_grad
        beta_grad_ref[:, head : head + 1] = beta_grad
        for line, values in enumerate(lines):
            conv_grad_ref[0, line : line + 1, own] = values
        for part in range(4):
            out_ref[:, head_lanes(4 * head + part)] = grads[part]
    head_grad_ref[0] = head_grad


def mixer_specs(length, lines):
    part = pl.BlockSpec((length, 4 * HEAD), lambda i: (i, 0))
    return [
        part,
        part,
        pl.BlockSpec((length, 2), lambda i: (i, 0)),
        pl.BlockSpec((length, 1), lambda i: (i, 0)),
        pl.BlockSpec((1, 1, length), lambda i: (i, 0, 0)),
        pl.BlockSpec((lines, 2 * HEAD), lambda i: (0, 0)),
        pl.BlockSpec((1, HEAD), lambda i: (0, 0)),
    ]


def saved_specs(length):
    return [
        pl.BlockSpec((1, 2, length, length), lambda i: (i, 0, 0, 0)),
        pl.BlockSpec((length, 2 * HEAD), lambda i: (i, 0)),
        pl.BlockSpec((length, 2 * HEAD), lambda i: (i, 0)),
    ]


def saved_shapes(count, length):
    return [
        jax.ShapeDtypeStruct((count, 2, length, length), WIDE),
        jax.ShapeDtypeStruct((count * length, 2 * HEAD), WIDE),
        jax.ShapeDtypeStruct((count * length, 2 * HEAD), WIDE),
    ]


def grad_specs(length, lines):
    return [
        pl.BlockSpec((length, 8 * HEAD), lambda i: (i, 0)),
        pl.BlockSpec((length, 2), lambda i: (i, 0)),
        pl.BlockSpec((1, lines, 2 * HEAD), lambda i: (i, 0, 0)),
        pl.BlockSpec((1, 1, HEAD), lambda i: (i, 0, 0)),
    ]


def grad_shapes(count, length, lines):
    return [
        jax.ShapeDtypeStruct((count * length, 8 * HEAD), LOW),
        jax.ShapeDtypeStruct((count * length, 2), WIDE),
        jax.ShapeDtypeStruct((count, lines, 2 * HEAD), WIDE),
        jax.ShapeDtypeStruct((count, 1, HEAD), WIDE),
    ]


def mixer_forward(inputs):
    count, _, length = inputs[4].shape
    return pl.pallas_call(
        mixer_forward_kernel,
        grid=(count,),
        in_specs=mixer_specs(length, inputs[5].shape[0]),
        out_specs=[pl.BlockSpec((length, 2 * HEAD), lambda i: (i, 0))] + saved_specs(length),
        out_shape=[jax.ShapeDtypeStruct((count * length, 2 * HEAD), LOW)]
        + saved_shapes(count, length),
        compiler_params=pltpu.CompilerParams(vmem_limit_bytes=32 << 20),
        name="mixer_forward",
    )(*inputs)


def mixer_backward(inputs, saved, grad):
    count, _, length = inputs[4].shape
    lines = inputs[5].shape[0]
    return pl.pallas_call(
        mixer_backward_kernel,
        grid=(count,),
        in_specs=mixer_specs(length, lines)
        + saved_specs(length)
        + [pl.BlockSpec((length, 2 * HEAD), lambda i: (i, 0))],
        out_specs=grad_specs(length, lines),
        out_shape=grad_shapes(count, length, lines),
        compiler_params=pltpu.CompilerParams(vmem_limit_bytes=32 << 20),
        name="mixer_backward",
    )(*inputs, *saved, grad)


def beside(refs, rows, lanes=slice(None)):
    return jnp.concatenate(
        [ref[z, c, rows, lanes] for ref in refs for z in range(ref.shape[0]) for c in range(2)], 1
    )


def atop(refs, lanes):
    return jnp.concatenate(
        [ref[z, c, :, lanes] for ref in refs for z in range(ref.shape[0]) for c in range(2)], 0
    )


def both(weight_refs, far, rows, lanes=slice(None)):
    return jnp.concatenate([beside(weight_refs[i][far], rows, lanes) for i in range(2)], 0)


def turned(left, right):
    return lax.dot_general(
        left, right, (((0,), (0,)), ((), ())), preferred_element_type=WIDE
    )


def straight(left, right):
    return lax.dot_general(
        left, right, (((1,), (0,)), ((), ())), preferred_element_type=WIDE
    )


def crossed(left, right):
    return lax.dot_general(
        left, right, (((1,), (1,)), ((), ())), preferred_element_type=WIDE
    )


def collect(token_refs, hold_ref):
    for step in range(2):

        @pl.when(pl.program_id(0) == step)
        def _():
            hold_ref[...] = token_refs[step][...]


def deal(pair_refs, values, lanes):
    for step in range(2):

        @pl.when(pl.program_id(0) == step)
        def _():
            pair_refs[step][:, lanes] = values.astype(LOW)


def whole(values):
    rank = len(values.shape)
    return pl.BlockSpec(values.shape, lambda i: (0,) * rank)


def split_refs(refs, sizes):
    out, start = [], 0
    for size in sizes:
        out.append(refs[start : start + size])
        start += size
    return out


def flat(grid):
    return [item for pair in grid for items in pair for item in items]


def nested(refs, grid):
    lists = split_refs(refs, [len(items) for pair in grid for items in pair])
    return [lists[:2], lists[2:]]


def call(kernel, inputs, in_specs, out_specs, out_shape, scratch, name, grid=2):
    return pl.pallas_call(
        kernel,
        grid=(grid,),
        in_specs=in_specs,
        out_specs=out_specs,
        out_shape=out_shape,
        scratch_shapes=scratch,
        compiler_params=pltpu.CompilerParams(vmem_limit_bytes=48 << 20),
        cost_estimate=pl.CostEstimate(
            flops=10 * 10**9, bytes_accessed=8 << 20, transcendentals=0
        ),
        name=name,
    )(*inputs)


QKVG = slice(0, 4 * HEAD)
OUT = slice(4 * HEAD, 5 * HEAD)


def column_forward(tokens, weights, gain, beta_weights, seg_col, seg_row, conv, head_gain):
    count, _, length = seg_row.shape
    width = tokens[0].shape[1]
    half = width // 2
    span = [slice(0, half), slice(half, width)]
    pieces = flat(weights)

    def kernel(*refs):
        token_refs, weight_refs, rest = split_refs(refs, [2, len(pieces), 17])
        gain_ref, beta_ref, col_ref, row_ref, conv_ref, head_ref = rest[:6]
        gated_ref, inverse_ref, update_ref, mixed_ref = rest[6:10]
        mixer_ref, first_ref, second_ref, beta_in_ref = rest[10:14]
        pair_refs, hold_ref = rest[14:16], rest[16]
        weight_refs = nested(weight_refs, weights)
        collect(token_refs, hold_ref)
        values = hold_ref[...].astype(WIDE)
        scale = lax.rsqrt(jnp.sum(values * values, 1, keepdims=True) * (1.0 / D) + 1e-06)
        mixer_ref[...] = (values * scale * gain_ref[...]).astype(LOW)
        masks = masks_of(col_ref[...], row_ref[0])
        kept = kept_of(col_ref[...], conv_ref.shape[0] // 3)
        mixer_in = mixer_ref[...].astype(WIDE)
        beta_in = []
        for head, projected_ref in enumerate((first_ref, second_ref)):
            projected_ref[...] = sum(
                straight(mixer_ref[:, span[far]], atop(weight_refs[head][far], QKVG))
                for far in range(2)
            )
            beta_in.append(
                jnp.sum(mixer_in * beta_ref[head : head + 1, :].astype(WIDE), 1, keepdims=True)
            )
            beta_in_ref[:, head : head + 1] = beta_in[head]
        results = forward_heads(
            [
                [ref[:, head_lanes(part)] for part in range(4)]
                for ref in (first_ref, second_ref)
            ],
            beta_in,
            [conv_ref[:, head_lanes(head)] for head in range(2)],
            kept,
            masks,
            head_ref[...],
        )
        for head, result in enumerate(results):
            own = head_lanes(head)
            gated_ref[:, own], inverse_ref[0, head], update_ref[:, own], mixed_ref[:, own] = result
        for far in range(2):
            branch = straight(gated_ref[...], both(weight_refs, far, slice(None), OUT))
            deal(pair_refs, branch, span[far])

    inputs = list(tokens) + pieces + [gain, beta_weights, seg_col, seg_row, conv, head_gain]
    in_specs = [whole(item) for item in inputs]
    in_specs[-4] = pl.BlockSpec((length, 1), lambda i: (i, 0))
    in_specs[-3] = pl.BlockSpec((1, 1, length), lambda i: (i, 0, 0))
    step = lambda lanes: pl.BlockSpec((length, lanes), lambda i: (i, 0))
    shape = lambda lanes, kind: jax.ShapeDtypeStruct((count * length, lanes), kind)
    out = jax.ShapeDtypeStruct((length, width), LOW)
    return call(
        kernel,
        inputs,
        in_specs,
        [step(2 * HEAD)]
        + saved_specs(length)
        + [step(width), step(4 * HEAD), step(4 * HEAD), step(2)]
        + [whole(out)] * 2,
        [shape(2 * HEAD, LOW)]
        + saved_shapes(count, length)
        + [shape(width, LOW), shape(4 * HEAD, WIDE), shape(4 * HEAD, WIDE), shape(2, WIDE)]
        + [out] * 2,
        [pltpu.VMEM((length, width), LOW)],
        "column_forward",
    )


def ffn_rows_of(hidden):
    return [slice(n * hidden, (n + 1) * hidden) for n in range(3)]


def column_ffn(tokens, ways, scales, weights, hidden):
    length, width = tokens[0].shape
    half = width // 2
    span = [slice(0, half), slice(half, width)]
    pieces = flat(weights)
    gate_rows, up_rows, down_rows = ffn_rows_of(hidden)

    def kernel(*refs):
        token_refs, way_refs, (scale_ref,), weight_refs, rest = split_refs(
            refs, [2, 2, 1, len(pieces), 7]
        )
        weight_refs = nested(weight_refs, weights)
        pair_refs, token_ref, way_ref = rest[:2], rest[2], rest[3]
        active_ref, gate_ref, up_ref = rest[4:]
        collect(token_refs, token_ref)
        collect(way_refs, way_ref)
        way_ref[...] = (way_ref[...].astype(WIDE) * scale_ref[...]).astype(LOW)
        gate, upward = (
            sum(crossed(token_ref[:, span[far]], both(weight_refs, far, rows)) for far in range(2))
            for rows in (gate_rows, up_rows)
        )
        sigma = sigmoid(gate)
        opened = gate * sigma
        active_ref[...] = (opened * upward).astype(LOW)
        grad = sum(
            crossed(way_ref[:, span[far]], both(weight_refs, far, down_rows)) for far in range(2)
        )
        gate_ref[...] = (grad * upward * sigma * (1.0 + gate * (1.0 - sigma))).astype(LOW)
        up_ref[...] = (grad * opened).astype(LOW)
        for far in range(2):
            values = straight(gate_ref[...], both(weight_refs, far, gate_rows)) + straight(
                up_ref[...], both(weight_refs, far, up_rows)
            )
            deal(pair_refs, values, span[far])

    inputs = list(tokens) + list(ways) + [scales] + pieces
    in_specs = [whole(item) for item in inputs]
    in_specs[4] = pl.BlockSpec((length, 1), lambda i: (i, 0))
    out = jax.ShapeDtypeStruct((length, width), LOW)
    step = lambda lanes: pl.BlockSpec((length, lanes), lambda i: (i, 0))
    shape = lambda lanes: jax.ShapeDtypeStruct((2 * length, lanes), LOW)
    return call(
        kernel,
        inputs,
        in_specs,
        [whole(out)] * 2 + [step(width)] * 2 + [step(2 * hidden)] * 3,
        [out] * 2 + [shape(width)] * 2 + [shape(2 * hidden)] * 3,
        [],
        "column_ffn",
    )


def write_beside(ref, rows, lanes, values):
    size = ref.shape[0]
    strip = values.shape[1] // (2 * size)
    for z in range(size):
        for c in range(2):
            start = (2 * z + c) * strip
            ref[z, c, rows, lanes] = values[:, start : start + strip].astype(LOW)


def column_ffn_grads(active, gate_grad, up_grad, tokens, ways, weights, grad):
    hidden = active.shape[1] // 2
    count, width = ways.shape
    length, half = count // 2, width // 2
    pieces = flat(weights)
    rows = ffn_rows_of(hidden)

    def kernel(active_ref, gate_ref, up_ref, token_ref, way_ref, *refs):
        weight_refs = nested(refs[: len(pieces)], weights)
        near_ref, far_ref, *out = refs[len(pieces) :]
        for far in range(2):
            lanes = slice(far * half, (far + 1) * half)
            values = straight(active_ref[...], both(weight_refs, far, rows[2])).astype(LOW)
            near_ref[:, lanes] = values[:length]
            far_ref[:, lanes] = values[length:]
            for n, left_ref, right_ref in (
                (0, gate_ref, token_ref), (1, up_ref, token_ref), (2, active_ref, way_ref)
            ):
                values = turned(left_ref[...], right_ref[:, lanes])
                for i in range(2):
                    write_beside(
                        out[2 * i + far],
                        rows[n],
                        slice(None),
                        values[i * hidden : (i + 1) * hidden],
                    )

    inputs = [active, gate_grad, up_grad, tokens, ways] + pieces
    out = jax.ShapeDtypeStruct((length, width), LOW)
    near, far, *grads = call(
        kernel,
        inputs,
        [whole(item) for item in inputs],
        [whole(out)] * 2 + [whole(grad)] * 4,
        [out] * 2 + [grad] * 4,
        [],
        "column_ffn_grads",
        grid=1,
    )
    return near, far, [grads[:2], grads[2:]]


def column_backward(
    grads, weights, beta_weights, seg_col, seg_row, conv, head_gain, saved, projected, beta_in
):
    count, _, length = seg_row.shape
    lines = conv.shape[0]
    width = grads[0].shape[1]
    half = width // 2
    span = [slice(0, half), slice(half, width)]
    pieces = flat(weights)

    def kernel(*refs):
        token_refs, weight_refs, rest = split_refs(refs, [2, len(pieces), 18])
        weight_refs = nested(weight_refs, weights)
        beta_ref, col_ref, row_ref, conv_ref, head_ref = rest[:5]
        inverse_ref, update_ref, mixed_ref, first_ref, second_ref, beta_in_ref = rest[5:11]
        signal_ref, beta_grad_ref, conv_grad_ref, head_grad_ref = rest[11:15]
        pair_refs, hold_ref = rest[15:17], rest[17]
        collect(token_refs, hold_ref)
        masks = masks_of(col_ref[...], row_ref[0])
        kept = kept_of(col_ref[...], conv_ref.shape[0] // 3)
        head_grad = jnp.zeros((1, HEAD), WIDE)
        beta_grads = []
        grad = sum(
            crossed(hold_ref[:, span[far]], both(weight_refs, far, slice(None), OUT))
            for far in range(2)
        )
        for head, projected_ref in enumerate((first_ref, second_ref)):
            own = head_lanes(head)
            signal_grads, beta_grad, conv_lines, gain_grad = backward_head(
                [projected_ref[:, head_lanes(part)] for part in range(4)],
                beta_in_ref[:, head : head + 1],
                conv_ref[:, own],
                kept,
                masks,
                head_ref[...],
                inverse_ref[0, head],
                update_ref[:, own],
                mixed_ref[:, own],
                grad[:, own],
            )
            head_grad = head_grad + gain_grad
            beta_grads.append(beta_grad.astype(LOW).astype(WIDE))
            beta_grad_ref[:, head : head + 1] = beta_grad
            for line, values in enumerate(conv_lines):
                conv_grad_ref[0, line : line + 1, own] = values
            for part in range(4):
                signal_ref[:, head_lanes(4 * head + part)] = signal_grads[part]
        head_grad_ref[0] = head_grad
        for far in range(2):
            values = sum(
                crossed(
                    signal_ref[:, 4 * HEAD * head : 4 * HEAD * (head + 1)],
                    atop(weight_refs[head][far], QKVG),
                )
                + beta_grads[head] * beta_ref[head : head + 1, span[far]].astype(WIDE)
                for head in range(2)
            )
            deal(pair_refs, values, span[far])

    inputs = (
        list(grads)
        + pieces
        + [beta_weights, seg_col, seg_row, conv, head_gain]
        + list(saved)
        + list(projected)
        + [beta_in]
    )
    in_specs = [whole(item) for item in inputs]
    step = lambda lanes: pl.BlockSpec((length, lanes), lambda i: (i, 0))
    in_specs[-10] = step(1)
    in_specs[-9] = pl.BlockSpec((1, 1, length), lambda i: (i, 0, 0))
    in_specs[-6:] = saved_specs(length) + [step(4 * HEAD), step(4 * HEAD), step(2)]
    out = jax.ShapeDtypeStruct((length, width), LOW)
    return call(
        kernel,
        inputs,
        in_specs,
        grad_specs(length, lines) + [whole(out)] * 2 + [step(width)],
        grad_shapes(count, length, lines)
        + [out] * 2
        + [jax.ShapeDtypeStruct((count * length, width), LOW)],
        [],
        "column_backward",
    )


def column_mixer_grads(mixer_in, signal_grads, gated, ways, grad):
    half = mixer_in.shape[1] // 2
    strip = grad.shape[2]

    def kernel(mixer_ref, signal_ref, gated_ref, way_ref, *grad_refs):
        for far in range(2):
            lanes = slice(far * half, (far + 1) * half)
            outs = turned(gated_ref[...], way_ref[:, lanes])
            for head in range(2):
                ref = grad_refs[2 * head + far]
                values = turned(
                    mixer_ref[:, lanes], signal_ref[:, 4 * HEAD * head : 4 * HEAD * (head + 1)]
                ).astype(LOW)
                for z in range(ref.shape[0]):
                    for c in range(2):
                        start = (2 * z + c) * strip
                        ref[z, c, :, QKVG] = values[start : start + strip]
                write_beside(ref, slice(None), OUT, outs[head_lanes(head)])

    inputs = [mixer_in, signal_grads, gated, ways]
    grads = call(
        kernel,
        inputs,
        [whole(item) for item in inputs],
        [whole(grad)] * 4,
        [grad] * 4,
        [],
        "column_mixer_grads",
        grid=1,
    )
    return [grads[:2], grads[2:]]


def contract(left, right, left_dim, right_dim):
    return lax.dot_general(
        left, right, (((left_dim,), (right_dim,)), ((), ())), preferred_element_type=WIDE
    )


def after(values, earlier):
    return lax.optimization_barrier((values, earlier))[0]


def exclusive_order(blocks):
    place = lax.axis_index("dmod")
    for bit in (1, 2):
        flip = (place & bit) != 0
        blocks = [jnp.where(flip, blocks[i ^ bit], blocks[i]) for i in range(4)]
    return blocks


def trade(blocks):
    return [blocks[0]] + [
        lax.ppermute(blocks[m], "dmod", [(i, i ^ m) for i in range(4)]) for m in (1, 2, 3)
    ]


def gather_width(values):
    far = lax.ppermute(values, "dmod", ACROSS)
    near = lax.ppermute(values, "dmod", CORE)
    return [values, near, far, lax.ppermute(far, "dmod", CORE)]


def scatter_width(blocks):
    near = lax.ppermute(blocks[1].astype(LOW), "dmod", CORE)
    cross = lax.ppermute(blocks[3].astype(LOW), "dmod", CORE)
    far = lax.ppermute((blocks[2] + cross.astype(WIDE)).astype(LOW), "dmod", ACROSS)
    return blocks[0] + near.astype(WIDE) + far.astype(WIDE)


def sum_pair(values):
    low = values.astype(LOW)
    return low.astype(WIDE) + lax.ppermute(low, "mp", SWAP).astype(WIDE)


def row_total(values):
    return lax.psum(values, "dmod")


class Ring:
    def __init__(self):
        self.size = lax.axis_size("dp")
        self.parts = 1

    def order(self, values):
        return values

    def gather(self, values):
        return [lax.all_gather(values, "dp", axis=1, tiled=True)]

    def scatter(self, make):
        return lax.psum_scatter(
            make(0).astype(LOW), "dp", scatter_dimension=1, tiled=True
        ).astype(WIDE)


def plane_body(
    block_input,
    segment_ids,
    group_ids,
    group_weight,
    mixer_norm,
    w_mix,
    w_beta,
    conv_kernel,
    head_norm,
    w_out,
    ffn_norm,
    w_ffn_in,
    w_ffn_down,
    cotangent,
):
    ring = Ring()
    parts = ring.parts
    micro, seqs, length, width = block_input.shape
    tokens = micro * seqs * length
    block = width // parts
    strip = w_mix.shape[0]
    span = w_mix.shape[2] // 4
    hidden = w_ffn_in.shape[2] // 4
    dmod = lax.axis_index("dmod")
    data_size = ring.size
    place = lax.axis_index("dp")

    lines = conv_kernel.shape[0] * conv_kernel.shape[1]
    pack = jnp.concatenate(
        [
            conv_kernel.reshape(-1),
            head_norm,
            mixer_norm,
            ffn_norm,
            w_beta.T.reshape(-1),
        ]
    )
    packs = lax.all_gather(pack, "dp", axis=0)
    sizes = [conv_kernel.size, head_norm.size, strip, strip, w_beta.size]
    cuts = [sum(sizes[:i]) for i in range(6)]
    conv = (
        packs[:, cuts[0] : cuts[1]]
        .reshape(data_size, lines, -1)
        .transpose(1, 0, 2)
        .reshape(lines, span)
        .astype(WIDE)
    )
    head_gain = packs[:, cuts[1] : cuts[2]].reshape(1, -1).astype(WIDE)
    gain_one = ring.order(packs[:, cuts[2] : cuts[3]].reshape(1, -1).astype(WIDE))
    gain_two = ring.order(packs[:, cuts[3] : cuts[4]].reshape(1, -1).astype(WIDE))
    beta_weights = ring.order(
        packs[:, cuts[4] : cuts[5]]
        .reshape(data_size, -1, strip)
        .transpose(1, 0, 2)
        .reshape(-1, width)
    )

    out_rows = jnp.concatenate(exclusive_order(jnp.split(w_out, 4, axis=0)), 0)
    out_halves = jnp.split(out_rows.T, 2, axis=1)
    mix_own = jnp.stack(trade(exclusive_order(jnp.split(w_mix, 4, axis=2))))
    mix_halves = [
        mix_own[:, :, :, head * HEAD : (head + 1) * HEAD].reshape(4, strip, 4 * HEAD)
        for head in (0, 1)
    ]
    ffn_own = jnp.stack(trade(exclusive_order(jnp.split(w_ffn_in, 4, axis=2))))
    ffn_halves = [ffn_own[:, :, 0], ffn_own[:, :, 1]]
    down_own = trade(exclusive_order(jnp.split(w_ffn_down, 4, axis=0)))
    down_halves = [
        jnp.stack([down_own[0].T, down_own[1].T]),
        jnp.stack([down_own[2].T, down_own[3].T]),
    ]

    def chain(half):
        first = ring.gather(out_halves[half][None])
        second = ring.gather(after(mix_halves[half], first[-1]))
        third = ring.gather(after(ffn_halves[half], second[-1]))
        fourth = ring.gather(after(down_halves[half], third[-1]))
        return first, second, third, fourth

    chains = [chain(0), chain(1)]
    out_weights = jnp.concatenate(
        [
            jnp.concatenate([part[0] for part in chains[0][0]], 0),
            jnp.concatenate([part[0] for part in chains[1][0]], 0),
        ],
        1,
    )
    mix_parts = [[part.reshape(4 * block, -1) for part in each[1]] for each in chains]
    ffn_parts = [[part.reshape(4 * block, -1) for part in each[2]] for each in chains]
    down_parts = [[part.reshape(2 * block, -1) for part in each[3]] for each in chains]

    marks = (group_ids.reshape(tokens, 1) == jnp.arange(group_weight.shape[0])[None]).astype(WIDE)
    counts = lax.psum(jnp.sum(marks, 0), "dp")
    table = group_weight * (tokens * data_size / group_weight.shape[0]) / counts
    scales = jnp.sum(marks * table, -1, keepdims=True)
    direction = ring.order(cotangent.reshape(tokens, width).astype(WIDE)) * scales
    direction_low = direction.astype(LOW)

    def by_part(slots):
        return [
            jnp.concatenate([slot[:, k * block : (k + 1) * block] for slot in slots], 1)
            for k in range(parts)
        ]

    def by_slot(pieces):
        return [
            jnp.concatenate([piece[:, m * block : (m + 1) * block] for piece in pieces], 1)
            for m in range(pieces[0].shape[1] // block)
        ]

    direction_parts = by_part(gather_width(direction_low))

    rows = ring.order(block_input.reshape(tokens, width).astype(WIDE))
    first_scale = lax.rsqrt(row_total(jnp.sum(rows * rows, -1, keepdims=True)) / D + 1e-06)
    mixer_in = (rows * first_scale * gain_one).astype(LOW)
    mixer_parts = by_part(gather_width(mixer_in))
    projected = [
        sum(jnp.dot(mixer_parts[k], mix_parts[half][k], preferred_element_type=WIDE) for k in range(parts))
        for half in (0, 1)
    ]
    beta_all = row_total(contract(beta_weights, mixer_in, 1, 1))
    heads = span // HEAD
    beta_in = lax.dynamic_slice_in_dim(beta_all, dmod * heads, heads, 0).T
    seg_col = segment_ids.reshape(tokens, 1)
    seg_row = segment_ids.reshape(micro * seqs, 1, length)
    mixer_args = list(projected) + [
        beta_in, seg_col, seg_row, conv, head_gain
    ]
    gated, *saved = mixer_forward(mixer_args)
    gated_all = jnp.concatenate(gather_width(gated), 1)
    middle = rows + sum_pair(contract(gated_all, out_weights, 1, 1))

    second_scale = lax.rsqrt(row_total(jnp.sum(middle * middle, -1, keepdims=True)) / D + 1e-06)
    ffn_in = (middle * second_scale * gain_two).astype(LOW)
    ffn_in_parts = by_part(gather_width(ffn_in))
    gate, upward = (
        sum(jnp.dot(ffn_in_parts[k], ffn_parts[half][k], preferred_element_type=WIDE) for k in range(parts))
        for half in (0, 1)
    )
    sigma = sigmoid(gate)
    active = (gate * sigma * upward).astype(LOW)
    down_slots = sum(
        (
            by_slot([contract(active, down_parts[half][k], 1, 1) for k in range(parts)])
            for half in (0, 1)
        ),
        [],
    )
    result = middle + sum_pair(scatter_width(down_slots))
    out = ring.order(result).astype(LOW).reshape(block_input.shape)

    down_grads = [
        ring.scatter(
            lambda k: contract(
                direction_parts[k][:, 2 * half * block : 2 * (half + 1) * block], active, 0, 0
            ).reshape(2, block, hidden)
        )
        for half in (0, 1)
    ]
    active_grad = sum(
        jnp.dot(
            direction_parts[k][:, 2 * half * block : 2 * (half + 1) * block],
            down_parts[half][k],
            preferred_element_type=WIDE,
        )
        for k in range(parts)
        for half in (0, 1)
    )
    gate_grad = (active_grad * upward * sigma * (1.0 + gate * (1.0 - sigma))).astype(LOW)
    upward_grad = (active_grad * gate * sigma).astype(LOW)
    ffn_slots = by_slot(
        [
            contract(gate_grad, ffn_parts[0][k], 1, 1) + contract(upward_grad, ffn_parts[1][k], 1, 1)
            for k in range(parts)
        ]
    )
    ffn_grads = [
        ring.scatter(lambda k: contract(ffn_in_parts[k], grad, 0, 0).reshape(4, block, hidden))
        for grad in (gate_grad, upward_grad)
    ]
    ffn_in_grad = sum_pair(scatter_width(ffn_slots))
    weighted_two = ffn_in_grad * gain_two
    norm_two_grad = jnp.sum(ffn_in_grad * middle * second_scale, 0)
    inner_two = row_total(jnp.sum(weighted_two * middle, -1, keepdims=True))
    middle_grad = (
        direction + second_scale * weighted_two - middle * (second_scale**3 * inner_two / D)
    )

    branch_low = middle_grad.astype(LOW)
    out_grads = [
        ring.scatter(
            lambda k: contract(
                branch_low[:, k * block : (k + 1) * block],
                gated_all[:, 2 * half * span : 2 * (half + 1) * span],
                0,
                0,
            )[None]
        )
        for half in (0, 1)
    ]
    gated_slots = jnp.split(jnp.dot(branch_low, out_weights, preferred_element_type=WIDE), 4, axis=1)
    gated_grad = scatter_width(gated_slots)
    projected_grad, beta_grad, conv_grad, head_grad = mixer_backward(
        mixer_args, saved, gated_grad
    )
    projected_slots = gather_width(projected_grad)
    mix_grads = [
        ring.scatter(
            lambda k: contract(
                mixer_in[:, k * block : (k + 1) * block],
                jnp.concatenate(projected_slots[2 * half : 2 * half + 2], 1),
                0,
                0,
            )[None]
        )
        for half in (0, 1)
    ]
    beta_slots = jnp.concatenate(
        exclusive_order(gather_width(beta_grad.T.astype(LOW))), 0
    )
    beta_weight_grad = contract(beta_slots, mixer_in, 1, 0)
    mixer_slots = by_slot(
        [
            contract(projected_grad[:, : 2 * span], mix_parts[0][k], 1, 1)
            + contract(projected_grad[:, 2 * span :], mix_parts[1][k], 1, 1)
            for k in range(parts)
        ]
    )
    mixer_grad = sum_pair(scatter_width(mixer_slots) + contract(beta_slots, beta_weights, 0, 0))
    weighted_one = mixer_grad * gain_one
    norm_one_grad = jnp.sum(mixer_grad * rows * first_scale, 0)
    inner_one = row_total(jnp.sum(weighted_one * rows, -1, keepdims=True))
    grad_input = ring.order(
        middle_grad + first_scale * weighted_one - rows * (first_scale**3 * inner_one / D)
    ).reshape(block_input.shape)

    head_total = lax.psum(jnp.sum(head_grad, (0, 1)), ("dp", "mp", "dmod"))
    head_out = lax.dynamic_slice_in_dim(head_total, place * head_norm.size, head_norm.size, 0)
    small = jnp.concatenate(
        [
            jnp.sum(conv_grad, 0),
            ring.order(jnp.stack([norm_one_grad, norm_two_grad]))
            .reshape(2, data_size, -1)
            .transpose(1, 0, 2)
            .reshape(data_size, -1)
            .reshape(-1)
            .reshape(-1, span),
            ring.order(beta_weight_grad)
            .reshape(-1, data_size, strip)
            .transpose(1, 0, 2)
            .reshape(-1, span),
        ],
        0,
    )
    conv_part = (
        small[:lines].reshape(lines, data_size, -1).transpose(1, 0, 2).reshape(data_size, -1)
    )
    norm_part = small[lines : lines + 2 * width // span].reshape(data_size, -1)
    beta_part = small[lines + 2 * width // span :].reshape(data_size, -1)
    small_own = lax.psum_scatter(
        jnp.concatenate([conv_part, norm_part, beta_part], 1), "dp", scatter_dimension=0
    )
    conv_out = small_own[: conv_kernel.size].reshape(conv_kernel.shape)
    norm_one_out = small_own[conv_kernel.size : conv_kernel.size + strip]
    norm_two_out = small_own[conv_kernel.size + strip : conv_kernel.size + 2 * strip]
    beta_out = small_own[conv_kernel.size + 2 * strip :].reshape(-1, strip).T

    def placed(blocks):
        return exclusive_order(trade([values.astype(LOW) for values in blocks]))

    ffn_out = jnp.stack(
        [
            jnp.concatenate([values.astype(WIDE) for values in placed(list(grad))], 1)
            for grad in ffn_grads
        ],
        1,
    )
    down_out = jnp.concatenate(
        [
            values.astype(WIDE).T
            for values in placed(list(down_grads[0]) + list(down_grads[1]))
        ],
        0,
    )
    out_out = jnp.concatenate(
        exclusive_order(jnp.split(jnp.concatenate([grad[0] for grad in out_grads], 1).T, 4, axis=0)),
        0,
    )
    mix_blocks = sum((jnp.split(grad[0], 2, axis=1) for grad in mix_grads), [])
    mix_out = jnp.concatenate(
        [
            values.reshape(strip, 2, 4, HEAD).transpose(0, 2, 1, 3).reshape(strip, 4, span)
            for values in exclusive_order(mix_blocks)
        ],
        2,
    )
    return (
        out,
        grad_input,
        norm_one_out,
        mix_out,
        beta_out,
        conv_out,
        head_out,
        out_out,
        norm_two_out,
        ffn_out,
        down_out,
    )


def exchange(values, axis):
    return lax.all_to_all(values, axis, 0, 0, tiled=True)


def swap_mp(values):
    return lax.ppermute(values, "mp", SWAP)


def swap_core(values):
    return lax.ppermute(values, "dmod", CORE)


def swap_across(values):
    return lax.ppermute(values, "dmod", ACROSS)


def swap_dp(values, k):
    return lax.ppermute(values, "dp", [(i, i ^ k) for i in range(lax.axis_size("dp"))])


def trade_blocks(blocks, axis, place):
    size = len(blocks)
    blocks = by_difference(blocks, place)
    moved = [blocks[0]] + [
        lax.ppermute(blocks[k], axis, [(i, i ^ k) for i in range(size)]) for k in range(1, size)
    ]
    return by_difference(moved, place)


def by_difference(blocks, place):
    bit = 1
    while bit < len(blocks):
        flip = (place & bit) != 0
        blocks = [jnp.where(flip, blocks[i ^ bit], blocks[i]) for i in range(len(blocks))]
        bit *= 2
    return blocks


def everyone(values, place):
    size = lax.axis_size("dp")
    values = values[None]
    bit = 1
    while bit < size:
        values = jnp.concatenate(turn((place & bit) != 0, (values, swap_dp(values, bit))), 0)
        bit *= 2
    return values


def turn(flag, pair):
    return jnp.where(flag, pair[1], pair[0]), jnp.where(flag, pair[0], pair[1])


def chip_blocks(core, pair):
    keep, send = turn(core, pair)
    return jnp.stack(turn(core, (keep, swap_core(send))), 1)


def along_column(core, pair, earlier=None):
    both = chip_blocks(core, pair)
    if earlier is not None:
        both = after(both, earlier)
    return exchange(both, "dp")


def gather_columns(values, earlier=None, later=None):
    if earlier is not None:
        values = after(values, earlier)
    half = values.shape[0] // 2
    over = swap_mp(values)
    far = swap_across(values)
    corner = (over[:half], far[half:])
    if later is not None:
        corner = after(corner, later)
    both = [swap_across(corner[0]), swap_mp(corner[1])]
    return [[[values], [far]], [[over], both]]


def wide(values):
    return values.astype(WIDE)


def scatter_send(grid):
    half = grid[0][0].shape[0] // 2
    return (
        jnp.concatenate([grid[1][0][:half], grid[1][1][:half]], 0),
        jnp.concatenate([grid[0][1][half:], grid[1][1][half:]], 0),
    )


def scatter_turn(grid, sent):
    half = grid[0][0].shape[0] // 2
    top = wide(grid[0][1][:half]) + wide(sent[0][half:])
    low = wide(grid[1][0][half:]) + wide(sent[1][half:])
    return top.astype(LOW), low.astype(LOW)


def scatter_end(grid, sent, back):
    half = grid[0][0].shape[0] // 2
    top = wide(grid[0][0][:half]) + wide(sent[0][:half]) + wide(swap_across(back[0]))
    low = wide(grid[0][0][half:]) + wide(sent[1][:half]) + wide(swap_mp(back[1]))
    return jnp.concatenate([top, low], 0).astype(LOW)


def column_tokens(values):
    size = lax.axis_size("dp")
    moved = [values] + [swap_dp(values, k) for k in range(1, size)]
    mine = jnp.concatenate(by_difference(moved, lax.axis_index("dp")), 0)
    return [mine, swap_core(mine)]


def column_chip(near, far):
    return (wide(near) + wide(swap_core(far))).astype(LOW)


def column_total(chip):
    size = lax.axis_size("dp")
    moved = exchange(chip, "dp").reshape(size, chip.shape[0] // size, -1)
    return jnp.sum(wide(moved), 0)


def column_body(
    block_input,
    segment_ids,
    group_ids,
    group_weight,
    mixer_norm,
    w_mix,
    w_beta,
    conv_kernel,
    head_norm,
    w_out,
    ffn_norm,
    w_ffn_in,
    w_ffn_down,
    cotangent,
):
    place = lax.axis_index("dp")
    size = lax.axis_size("dp")
    side = lax.axis_index("mp")
    dmod = lax.axis_index("dmod")
    row, core = dmod // 2, dmod % 2
    at_far_side, at_far_row, at_core = side == 1, row == 1, core == 1
    micro, _, length, width = block_input.shape
    share = length // size
    strip = w_mix.shape[0]
    groups = group_weight.shape[0]
    group_heads = w_beta.shape[1]
    hidden = w_ffn_down.shape[0] // (2 * size)
    span = 2 * width

    def to_column(values):
        lead = values.shape[:-1]
        values = values.reshape(lead + (2, 2, size, strip))
        values = jnp.swapaxes(values, -2, -3).reshape(lead + (2, span))
        return jnp.concatenate(turn(at_far_row, (values[..., 0, :], values[..., 1, :])), -1)

    def from_column(values):
        lead = values.shape[:-1]
        halves_of = turn(at_far_row, (values[..., :span], values[..., span:]))
        values = jnp.stack(halves_of, -2).reshape(lead + (2, size, 2, strip))
        return jnp.swapaxes(values, -2, -3).reshape(lead + (2 * span,))

    def over_dp(values):
        values = values.reshape(micro, size, share, width)
        moved = trade_blocks([values[:, z] for z in range(size)], "dp", place)
        moved = jnp.where(at_far_side, jnp.stack(moved[2:]), jnp.stack(moved[:2]))
        return moved.reshape(4, share, width)

    def over_dmod(moved):
        moved = trade_blocks([moved[j] for j in range(4)], "dmod", dmod)
        return to_column(jnp.concatenate(moved, 1))

    def tokens_out(values):
        blocks = jnp.split(from_column(values), 4, axis=1)
        moved = jnp.stack(trade_blocks(blocks, "dmod", dmod)).reshape(2, micro, share, width)
        moved = jnp.concatenate(turn(at_far_side, (moved, swap_mp(moved))), 0)
        moved = trade_blocks([moved[z] for z in range(size)], "dp", place)
        return jnp.stack(moved, 1).reshape(block_input.shape)

    blocks = w_mix.reshape(strip, 4, 2, size, HEAD).transpose(2, 3, 0, 1, 4)
    blocks = blocks.reshape(2, size, strip, 4 * HEAD)
    blocks = jnp.concatenate([blocks, w_out.reshape(2, size, HEAD, strip)], 3)
    mix_blocks = chip_blocks(at_core, (blocks[0], blocks[1]))
    mix_pieces = exchange(mix_blocks, "dp")
    block_input, cotangent, conv_kernel, w_ffn_in, w_ffn_down = after(
        (block_input, cotangent, conv_kernel, w_ffn_in, w_ffn_down), mix_blocks
    )
    blocks = jnp.concatenate(
        [
            w_ffn_in.transpose(1, 2, 0).reshape(2, 2 * size, hidden, strip),
            w_ffn_down.reshape(1, 2 * size, hidden, strip),
        ],
        0,
    )
    blocks = blocks.transpose(1, 0, 2, 3).reshape(2, size, 3 * hidden, strip)
    ffn_blocks = chip_blocks(at_core, (blocks[0], blocks[1]))

    small = [
        conv_kernel.reshape(-1),
        head_norm,
        mixer_norm,
        ffn_norm,
        w_beta.T.reshape(-1),
        segment_ids.reshape(-1).astype(LOW),
        group_ids.reshape(-1).astype(LOW),
    ]
    count = sum(item.size for item in small)
    pack = jnp.concatenate(small + [jnp.zeros((-count % HEAD,), LOW)]).reshape(-1, HEAD)
    packs = everyone(pack, place)
    packs = jnp.stack(turn(at_far_side, (packs, swap_mp(packs))))
    packs = jnp.stack(turn(at_core, (packs, swap_core(packs))))
    packs = jnp.stack(turn(at_far_row, (packs, swap_across(packs))))
    packs = packs.reshape(2, 2, 2, size, -1)

    tokens_low, way_moved = over_dp(block_input), over_dp(cotangent)
    tokens_low = over_dmod(after(tokens_low, (mix_pieces, packs, ffn_blocks)))
    rows = wide(tokens_low)
    tokens_pair = column_tokens(tokens_low)
    mix_weights = gather_columns(mix_pieces)
    ffn_pieces = exchange(ffn_blocks, "dp")
    way_low = over_dmod(after(way_moved, tokens_pair[0]))

    fields = []
    start = 0
    for item in small:
        fields.append(packs[..., start : start + item.size])
        start += item.size
    lines = conv_kernel.shape[0] * conv_kernel.shape[1]
    heads = 2 * group_heads
    local_head = size * core + place
    own_heads = [group_heads * side + local_head, group_heads * (1 - side) + local_head]
    conv_all = (
        fields[0]
        .reshape(2, 2, 2, size, lines, -1)
        .transpose(4, 2, 0, 1, 3, 5)
        .reshape(lines, heads * HEAD)
    )
    conv = wide(
        jnp.concatenate(
            [lax.dynamic_slice_in_dim(conv_all, head * HEAD, HEAD, 1) for head in own_heads], 1
        )
    )
    head_gain = wide(fields[1][0, 0, 0].reshape(1, HEAD))
    gain_one = to_column(wide(fields[2][:, :, 0].reshape(1, -1)))
    gain_two = to_column(wide(fields[3][:, :, 0].reshape(1, -1)))
    beta_rows = (
        fields[4]
        .reshape(2, 2, 2, size, group_heads, strip)
        .transpose(2, 4, 0, 1, 3, 5)
        .reshape(heads, -1)
    )
    beta_weights = to_column(
        jnp.concatenate([lax.dynamic_slice_in_dim(beta_rows, head, 1, 0) for head in own_heads], 0)
    )
    sequence = 2 * side + row
    segments = lax.dynamic_index_in_dim(fields[5][0, 0, 0], sequence, 0, keepdims=False)
    segments = segments.reshape(micro, length).astype(jnp.int32)
    segments = jnp.concatenate(turn(at_core, (segments[:1], segments[1:])), 0)
    seg_col = segments.reshape(-1, 1)
    seg_row = segments.reshape(micro, 1, length)
    all_groups = fields[6][0, 0, 0].reshape(-1).astype(jnp.int32)
    names = jnp.arange(groups, dtype=jnp.int32)
    counts = jnp.sum((all_groups[:, None] == names[None]).astype(WIDE), 0)
    table = group_weight * (all_groups.shape[0] / groups) / counts
    own_groups = lax.dynamic_slice_in_dim(all_groups, sequence * micro * length, micro * length, 0)
    scales = jnp.sum((own_groups[:, None] == names[None]).astype(WIDE) * table, -1, keepdims=True)
    scales = jnp.concatenate(turn(at_core, (scales[:length], scales[length:])), 0)

    constants = [beta_weights, seg_col, seg_row, conv, head_gain]
    gated, inverse, update, mixed, mixer_in, *projected, beta_in, near, far = column_forward(
        tokens_pair, mix_weights, gain_one, *constants
    )
    middle = rows + column_total(after(column_chip(near, far), ffn_pieces))

    second_scale = lax.rsqrt(jnp.mean(middle * middle, -1, keepdims=True) + 1e-06)
    ffn_low = (middle * second_scale * gain_two).astype(LOW)
    way_pair = column_tokens(after(way_low, middle))
    direction = wide(way_low) * lax.dynamic_slice_in_dim(scales, place * share, share, 0)
    ffn_pair = column_tokens(ffn_low)
    ffn_weights = gather_columns(ffn_pieces, mix_weights[1][1])
    near, far, ffn_in, directions, active, gate_grad, up_grad = column_ffn(
        ffn_pair, way_pair, scales, ffn_weights, hidden
    )
    chip = column_chip(near, far)
    ffn_in_grad = column_total(chip)
    near, far, ffn_grads = column_ffn_grads(
        after(active, chip),
        gate_grad,
        up_grad,
        ffn_in,
        directions,
        ffn_weights,
        jax.ShapeDtypeStruct((size, 2, 3 * hidden, strip), LOW),
    )
    out_chip = column_chip(near, far)
    ffn_sent = scatter_send(ffn_grads)
    ffn_in_grad = after(ffn_in_grad, out_chip)
    ffn_sent = swap_mp(ffn_sent[0]), swap_across(ffn_sent[1])

    weighted_two = ffn_in_grad * gain_two
    norm_two_grad = jnp.sum(ffn_in_grad * middle * second_scale, 0, keepdims=True)
    inner_two = jnp.mean(weighted_two * middle, -1, keepdims=True)
    middle_grad = (
        direction + second_scale * weighted_two - middle * (second_scale**3 * inner_two)
    )
    branch_pair = column_tokens(middle_grad.astype(LOW))
    down_sum = column_total(after(out_chip, branch_pair[0]))
    ffn_back = scatter_turn(ffn_grads, ffn_sent)

    signal_grads, beta_grad, conv_grad, head_grad, near, far, branch_all = column_backward(
        branch_pair,
        mix_weights,
        *constants,
        (inverse, update, mixed),
        projected,
        beta_in,
    )
    mix_grads = column_mixer_grads(
        mixer_in,
        signal_grads,
        gated,
        branch_all,
        jax.ShapeDtypeStruct((size, 2, strip, 5 * HEAD), LOW),
    )
    chip = column_chip(near, far)
    mixer_grad = column_total(chip)
    ffn_total = scatter_end(ffn_grads, ffn_sent, ffn_back)
    mix_sent = scatter_send(mix_grads)
    mix_sent = after((swap_mp(mix_sent[0]), swap_across(mix_sent[1])), mixer_grad)
    mix_back = scatter_turn(mix_grads, mix_sent)
    mix_total = scatter_end(mix_grads, mix_sent, mix_back)
    out_low = (middle + after(down_sum, mix_back)).astype(LOW)

    def placed(total, earlier=None):
        return along_column(at_core, (total[:, 0], total[:, 1]), earlier).transpose(1, 0, 2, 3)

    ffn_pieces = placed(ffn_total)
    ffn_out = wide(
        ffn_pieces[:, :, : 2 * hidden]
        .reshape(2 * size, 2, hidden, strip)
        .transpose(1, 0, 2, 3)
        .reshape(2, -1, strip)
        .transpose(2, 0, 1)
    )
    down_out = wide(ffn_pieces[:, :, 2 * hidden :].reshape(-1, strip))
    mix_pieces = placed(mix_total, ffn_pieces).reshape(2 * size, strip, 5, HEAD)
    mix_out = wide(mix_pieces[:, :, :4].transpose(1, 2, 0, 3).reshape(strip, 4, -1))
    out_out = wide(mix_pieces[:, :, 4].reshape(-1, strip))
    beta_weight_grad = contract(beta_grad.astype(LOW), mixer_in, 0, 0)
    weighted_one = mixer_grad * gain_one
    first_scale = lax.rsqrt(jnp.mean(rows * rows, -1, keepdims=True) + 1e-06)
    norm_one_grad = jnp.sum(mixer_grad * rows * first_scale, 0, keepdims=True)
    inner_one = jnp.mean(weighted_one * rows, -1, keepdims=True)
    grad_low = (
        middle_grad + first_scale * weighted_one - rows * (first_scale**3 * inner_one)
    ).astype(LOW)
    out = tokens_out(out_low)
    grad_input = wide(tokens_out(grad_low))

    conv_sides = jnp.stack(turn(at_far_side, jnp.split(jnp.sum(conv_grad, 0), 2, axis=1)))
    beta_sides = from_column(
        jnp.concatenate(turn(at_far_side, (beta_weight_grad[:1], beta_weight_grad[1:])), 0)
    )
    vector = jnp.concatenate(
        [
            conv_sides.reshape(-1, HEAD),
            beta_sides.reshape(-1, HEAD),
            from_column(norm_one_grad).reshape(-1, HEAD),
            from_column(norm_two_grad).reshape(-1, HEAD),
            jnp.sum(head_grad, 0),
        ]
    )
    vector = after(vector, mix_back)
    vector = vector + swap_mp(vector)
    vector = vector + swap_across(vector)
    vectors = jnp.stack(turn(at_core, (vector, swap_core(vector))))
    vectors = everyone(vectors, place)
    ends = [2 * lines, 2 * lines + 4 * span // HEAD]
    own_width = dmod * width + place * strip
    taps_own = conv_kernel.shape[2]
    at = (dmod * size + place) * taps_own
    conv_head = at // HEAD
    conv_out = lax.dynamic_slice(
        vectors,
        (conv_head % size, conv_head // size, side * lines, at % HEAD),
        (1, 1, lines, taps_own),
    ).reshape(conv_kernel.shape)
    beta_out = (
        lax.dynamic_slice(
            vectors[:, :, ends[0] : ends[1]].reshape(size, 2, 2, 2 * span),
            (0, 0, side, own_width),
            (size, 2, 1, strip),
        )
        .reshape(size, 2, strip)
        .transpose(2, 1, 0)
        .reshape(strip, group_heads)
    )
    sums = jnp.sum(vectors[:, :, ends[1] :], (0, 1))
    norms = sums[:-1].reshape(2, -1)
    norm_one_out, norm_two_out = (
        lax.dynamic_slice_in_dim(norms[i], own_width, strip, 0) for i in (0, 1)
    )
    head_out = lax.dynamic_slice_in_dim(sums[-1], place * head_norm.size, head_norm.size, 0)
    return (
        out,
        grad_input,
        norm_one_out,
        mix_out,
        beta_out,
        conv_out,
        head_out,
        out_out,
        norm_two_out,
        ffn_out,
        down_out,
    )


def solution(mesh):
    sizes = dict(mesh.shape)
    columns = sizes["mp"] * sizes["dmod"] // 2
    body = column_body if columns == sizes["dp"] else plane_body
    wide = P(("dmod", "dp"))
    tokens = P(None, "dp", None, "dmod")
    weights = (
        wide,
        P(("dmod", "dp"), None, "mp"),
        P(("dmod", "dp"), "mp"),
        P(None, None, ("mp", "dmod", "dp")),
        P("dp"),
        P("mp", ("dmod", "dp")),
        wide,
        P(("dmod", "dp"), None, "mp"),
        P("mp", ("dmod", "dp")),
    )
    ids = P(None, "dp", None)
    return jax.shard_map(
        body,
        mesh=mesh,
        in_specs=(tokens, ids, ids, P()) + weights + (tokens,),
        out_specs=(tokens, tokens) + weights,
        check_vma=False,
    )
```

```python
import jax
import jax.numpy as jnp
from jax import lax
from jax.experimental import pallas as pl
from jax.experimental.pallas import tpu as pltpu
from jax.sharding import PartitionSpec as P

D = 2048
HEAD = 128
LOW = jnp.bfloat16
WIDE = jnp.float32
LONGEST_RING = 1
CORE = [(i, i ^ 1) for i in range(4)]
ACROSS = [(i, i ^ 2) for i in range(4)]
SWAP = [(0, 1), (1, 0)]


def halves(values):
    high = values.astype(LOW)
    return high, (values - high.astype(WIDE)).astype(LOW)


def product(left, right, left_dim, right_dim):
    def one(a, b):
        return lax.dot_general(
            a, b, (((left_dim,), (right_dim,)), ((), ())), preferred_element_type=WIDE
        )

    return one(left[0], right[0]) + (one(left[0], right[1]) + one(left[1], right[0]))


def sigmoid(values):
    return 1.0 / (1.0 + jnp.exp(-values))


def masks_of(seg_col, seg_row):
    length = seg_col.shape[0]
    rows = lax.broadcasted_iota(jnp.int32, (length, length), 0)
    cols = lax.broadcasted_iota(jnp.int32, (length, length), 1)
    same = seg_col == seg_row
    return rows, cols, same & (cols < rows), same & (cols <= rows)


def kept_of(seg_col, taps):
    length = seg_col.shape[0]
    wide = jnp.broadcast_to(seg_col, (length, HEAD))
    place = lax.broadcasted_iota(jnp.int32, (length, HEAD), 0)
    return [
        ((pltpu.roll(wide, shift, 0) == wide) & (place >= shift)).astype(WIDE)
        for shift in range(1, taps)
    ]


def convolve(signal, kernel, kept):
    taps = kernel.shape[0]
    total = signal * kernel[taps - 1 : taps]
    for shift in range(1, taps):
        moved = pltpu.roll(signal, shift, 0) * kept[shift - 1]
        total = total + moved * kernel[taps - 1 - shift : taps - shift]
    return total


def single(left, right):
    return lax.dot_general(
        left.astype(LOW),
        right.astype(LOW),
        (((1,), (0,)), ((), ())),
        preferred_element_type=WIDE,
    )


def invert(lowers, rows, cols):
    length = lowers[0].shape[0]
    eye = (rows == cols).astype(WIDE)
    pair = (rows // 2) == (cols // 2)
    inverses = [eye - jnp.where(pair, lower, 0.0) for lower in lowers]
    size = 2
    while size < length:
        cross = ((rows // (2 * size)) == (cols // (2 * size))) & ((rows // size) != (cols // size))
        steps = [
            single(inverse, jnp.where(cross, lower, 0.0))
            for inverse, lower in zip(inverses, lowers)
        ]
        inverses = [
            inverse - single(step, inverse) for step, inverse in zip(steps, inverses)
        ]
        size *= 2
    rests = [
        eye - inverse - product(halves(lower), halves(inverse), 1, 0)
        for inverse, lower in zip(inverses, lowers)
    ]
    return [inverse + single(inverse, rest) for inverse, rest in zip(inverses, rests)]


def forward_heads(signals, beta_in, conv, kept, masks, gain):
    rows, cols, strict, inclusive = masks
    taps = conv[0].shape[0] // 3
    lowers, held = [], []
    for head in range(len(signals)):
        convolved = []
        for part in range(3):
            kernel = conv[head][part * taps : (part + 1) * taps]
            pre = convolve(signals[head][part], kernel, kept)
            convolved.append(pre * sigmoid(pre))
        query = convolved[0] * (
            lax.rsqrt(jnp.sum(convolved[0] * convolved[0], 1, keepdims=True) + 1e-06) * HEAD**-0.5
        )
        key = convolved[1] * lax.rsqrt(
            jnp.sum(convolved[1] * convolved[1], 1, keepdims=True) + 1e-06
        )
        beta = sigmoid(beta_in[head])
        key_parts = halves(key)
        gram = product(key_parts, key_parts, 1, 1)
        lowers.append(jnp.where(strict, gram * beta, 0.0))
        scores = jnp.where(inclusive, product(halves(query), key_parts, 1, 1), 0.0)
        held.append((halves(scores), halves(convolved[2] * beta)))
    out = []
    for head, inverse in enumerate(invert(lowers, rows, cols)):
        scores, target = held[head]
        update = product(halves(inverse), target, 1, 0)
        mixed = product(scores, halves(update), 1, 0)
        scale = lax.rsqrt(jnp.sum(mixed * mixed, 1, keepdims=True) * (1.0 / HEAD) + 1e-05)
        gate = signals[head][3]
        gated = (mixed * scale * gain * (gate * sigmoid(gate))).astype(LOW)
        out.append((gated, inverse, update, mixed))
    return out


def backward_head(signals, beta_in, conv, kept, masks, gain, inverse, update, mixed, grad):
    rows, cols, strict, inclusive = masks
    length = grad.shape[0]
    taps = conv.shape[0] // 3
    before, gates, convolved = [], [], []
    for part in range(3):
        pre = convolve(signals[part], conv[part * taps : (part + 1) * taps], kept)
        before.append(pre)
        gates.append(sigmoid(pre))
        convolved.append(pre * gates[part])
    query_unit = lax.rsqrt(jnp.sum(convolved[0] * convolved[0], 1, keepdims=True) + 1e-06)
    key_unit = lax.rsqrt(jnp.sum(convolved[1] * convolved[1], 1, keepdims=True) + 1e-06)
    query = convolved[0] * (query_unit * HEAD**-0.5)
    key = convolved[1] * key_unit
    beta = sigmoid(beta_in)
    gate = signals[3]
    gate_sigma = sigmoid(gate)
    opened = gate * gate_sigma
    scale = lax.rsqrt(jnp.sum(mixed * mixed, 1, keepdims=True) * (1.0 / HEAD) + 1e-05)
    normed = mixed * scale
    head_grad = jnp.sum(grad * opened * normed, 0, keepdims=True)
    inner = grad * opened * gain
    mixed_grad = scale * inner - mixed * (
        scale * scale * scale * (jnp.sum(inner * mixed, 1, keepdims=True) * (1.0 / HEAD))
    )
    gate_grad = grad * normed * gain * gate_sigma * (1.0 + gate * (1.0 - gate_sigma))
    key_parts = halves(key)
    query_parts = halves(query)
    update_parts = halves(update)
    mixed_parts = halves(mixed_grad)
    gram = product(key_parts, key_parts, 1, 1)
    scores = jnp.where(inclusive, product(query_parts, key_parts, 1, 1), 0.0)
    scores_grad = halves(jnp.where(inclusive, product(mixed_parts, update_parts, 1, 1), 0.0))
    update_grad = product(halves(scores), mixed_parts, 0, 0)
    solved = product(halves(inverse), halves(update_grad), 0, 0)
    system_grad = jnp.where(strict, -product(halves(solved), update_parts, 1, 1), 0.0)
    gram_grad = halves(system_grad * beta)
    query_grad = product(scores_grad, key_parts, 1, 0)
    key_grad = (
        product(scores_grad, query_parts, 0, 0)
        + product(gram_grad, key_parts, 1, 0)
        + product(gram_grad, key_parts, 0, 0)
    )
    beta_grad = jnp.sum(system_grad * gram, 1, keepdims=True) + jnp.sum(
        solved * convolved[2], 1, keepdims=True
    )
    beta_grad = beta_grad * beta * (1.0 - beta)
    conv_grads = [
        HEAD**-0.5
        * (
            query_grad * query_unit
            - convolved[0]
            * (
                query_unit
                * query_unit
                * query_unit
                * jnp.sum(convolved[0] * query_grad, 1, keepdims=True)
            )
        ),
        key_grad * key_unit
        - convolved[1]
        * (key_unit * key_unit * key_unit * jnp.sum(convolved[1] * key_grad, 1, keepdims=True)),
        solved * beta,
    ]
    lines = [None] * (3 * taps)
    signal_grads = []
    for part in range(3):
        sigma = gates[part]
        error = conv_grads[part] * sigma * (1.0 + before[part] * (1.0 - sigma))
        kernel = conv[part * taps : (part + 1) * taps]
        total = error * kernel[taps - 1 : taps]
        last = part * taps + taps - 1
        lines[last] = jnp.sum(error * signals[part], 0, keepdims=True)
        for shift in range(1, taps):
            held = error * kept[shift - 1]
            lines[last - shift] = jnp.sum(
                held * pltpu.roll(signals[part], shift, 0), 0, keepdims=True
            )
            total = total + pltpu.roll(held, length - shift, 0) * (
                kernel[taps - 1 - shift : taps - shift]
            )
        signal_grads.append(total.astype(LOW))
    signal_grads.append(gate_grad.astype(LOW))
    return signal_grads, beta_grad, lines, head_grad


def head_lanes(head):
    return slice(head * HEAD, (head + 1) * HEAD)


def mixer_forward_kernel(*refs):
    parts = refs[:2]
    beta_ref, col_ref, row_ref, conv_ref, head_ref = refs[2:7]
    gated_ref, inverse_ref, update_ref, mixed_ref = refs[7:]
    masks = masks_of(col_ref[...], row_ref[0])
    kept = kept_of(col_ref[...], conv_ref.shape[0] // 3)
    results = forward_heads(
        [[parts[head][:, head_lanes(part)] for part in range(4)] for head in range(2)],
        [beta_ref[:, head : head + 1] for head in range(2)],
        [conv_ref[:, head_lanes(head)] for head in range(2)],
        kept,
        masks,
        head_ref[...],
    )
    for head, result in enumerate(results):
        own = head_lanes(head)
        gated_ref[:, own], inverse_ref[0, head], update_ref[:, own], mixed_ref[:, own] = result


def mixer_backward_kernel(*refs):
    parts = refs[:2]
    beta_ref, col_ref, row_ref, conv_ref, head_ref = refs[2:7]
    inverse_ref, update_ref, mixed_ref, grad_ref = refs[7:11]
    out_ref, beta_grad_ref, conv_grad_ref, head_grad_ref = refs[11:]
    masks = masks_of(col_ref[...], row_ref[0])
    kept = kept_of(col_ref[...], conv_ref.shape[0] // 3)
    head_grad = jnp.zeros((1, HEAD), WIDE)
    for head in range(2):
        own = head_lanes(head)
        grads, beta_grad, lines, gain_grad = backward_head(
            [parts[head][:, head_lanes(part)] for part in range(4)],
            beta_ref[:, head : head + 1],
            conv_ref[:, own],
            kept,
            masks,
            head_ref[...],
            inverse_ref[0, head],
            update_ref[:, own],
            mixed_ref[:, own],
            grad_ref[:, own],
        )
        head_grad = head_grad + gain_grad
        beta_grad_ref[:, head : head + 1] = beta_grad
        for line, values in enumerate(lines):
            conv_grad_ref[0, line : line + 1, own] = values
        for part in range(4):
            out_ref[:, head_lanes(4 * head + part)] = grads[part]
    head_grad_ref[0] = head_grad


def mixer_specs(length, lines):
    part = pl.BlockSpec((length, 4 * HEAD), lambda i: (i, 0))
    return [
        part,
        part,
        pl.BlockSpec((length, 2), lambda i: (i, 0)),
        pl.BlockSpec((length, 1), lambda i: (i, 0)),
        pl.BlockSpec((1, 1, length), lambda i: (i, 0, 0)),
        pl.BlockSpec((lines, 2 * HEAD), lambda i: (0, 0)),
        pl.BlockSpec((1, HEAD), lambda i: (0, 0)),
    ]


def saved_specs(length):
    return [
        pl.BlockSpec((1, 2, length, length), lambda i: (i, 0, 0, 0)),
        pl.BlockSpec((length, 2 * HEAD), lambda i: (i, 0)),
        pl.BlockSpec((length, 2 * HEAD), lambda i: (i, 0)),
    ]


def saved_shapes(count, length):
    return [
        jax.ShapeDtypeStruct((count, 2, length, length), WIDE),
        jax.ShapeDtypeStruct((count * length, 2 * HEAD), WIDE),
        jax.ShapeDtypeStruct((count * length, 2 * HEAD), WIDE),
    ]


def grad_specs(length, lines):
    return [
        pl.BlockSpec((length, 8 * HEAD), lambda i: (i, 0)),
        pl.BlockSpec((length, 2), lambda i: (i, 0)),
        pl.BlockSpec((1, lines, 2 * HEAD), lambda i: (i, 0, 0)),
        pl.BlockSpec((1, 1, HEAD), lambda i: (i, 0, 0)),
    ]


def grad_shapes(count, length, lines):
    return [
        jax.ShapeDtypeStruct((count * length, 8 * HEAD), LOW),
        jax.ShapeDtypeStruct((count * length, 2), WIDE),
        jax.ShapeDtypeStruct((count, lines, 2 * HEAD), WIDE),
        jax.ShapeDtypeStruct((count, 1, HEAD), WIDE),
    ]


def mixer_forward(inputs):
    count, _, length = inputs[4].shape
    return pl.pallas_call(
        mixer_forward_kernel,
        grid=(count,),
        in_specs=mixer_specs(length, inputs[5].shape[0]),
        out_specs=[pl.BlockSpec((length, 2 * HEAD), lambda i: (i, 0))] + saved_specs(length),
        out_shape=[jax.ShapeDtypeStruct((count * length, 2 * HEAD), LOW)]
        + saved_shapes(count, length),
        compiler_params=pltpu.CompilerParams(vmem_limit_bytes=32 << 20),
        name="mixer_forward",
    )(*inputs)


def mixer_backward(inputs, saved, grad):
    count, _, length = inputs[4].shape
    lines = inputs[5].shape[0]
    return pl.pallas_call(
        mixer_backward_kernel,
        grid=(count,),
        in_specs=mixer_specs(length, lines)
        + saved_specs(length)
        + [pl.BlockSpec((length, 2 * HEAD), lambda i: (i, 0))],
        out_specs=grad_specs(length, lines),
        out_shape=grad_shapes(count, length, lines),
        compiler_params=pltpu.CompilerParams(vmem_limit_bytes=32 << 20),
        name="mixer_backward",
    )(*inputs, *saved, grad)


def beside(refs, rows, lanes=slice(None)):
    return jnp.concatenate(
        [ref[z, c, rows, lanes] for ref in refs for z in range(ref.shape[0]) for c in range(2)], 1
    )


def atop(refs, lanes):
    return jnp.concatenate(
        [ref[z, c, :, lanes] for ref in refs for z in range(ref.shape[0]) for c in range(2)], 0
    )


def both(weight_refs, far, rows, lanes=slice(None)):
    return jnp.concatenate([beside(weight_refs[i][far], rows, lanes) for i in range(2)], 0)


def turned(left, right):
    return lax.dot_general(
        left, right, (((0,), (0,)), ((), ())), preferred_element_type=WIDE
    )


def straight(left, right):
    return lax.dot_general(
        left, right, (((1,), (0,)), ((), ())), preferred_element_type=WIDE
    )


def crossed(left, right):
    return lax.dot_general(
        left, right, (((1,), (1,)), ((), ())), preferred_element_type=WIDE
    )


def collect(token_refs, hold_ref):
    for step in range(2):

        @pl.when(pl.program_id(0) == step)
        def _():
            hold_ref[...] = token_refs[step][...]


def deal(pair_refs, values, lanes):
    for step in range(2):

        @pl.when(pl.program_id(0) == step)
        def _():
            pair_refs[step][:, lanes] = values.astype(LOW)


def whole(values):
    rank = len(values.shape)
    return pl.BlockSpec(values.shape, lambda i: (0,) * rank)


def split_refs(refs, sizes):
    out, start = [], 0
    for size in sizes:
        out.append(refs[start : start + size])
        start += size
    return out


def flat(grid):
    return [item for pair in grid for items in pair for item in items]


def nested(refs, grid):
    lists = split_refs(refs, [len(items) for pair in grid for items in pair])
    return [lists[:2], lists[2:]]


def call(kernel, inputs, in_specs, out_specs, out_shape, scratch, name, grid=2):
    return pl.pallas_call(
        kernel,
        grid=(grid,),
        in_specs=in_specs,
        out_specs=out_specs,
        out_shape=out_shape,
        scratch_shapes=scratch,
        compiler_params=pltpu.CompilerParams(vmem_limit_bytes=44 << 20),
        cost_estimate=pl.CostEstimate(
            flops=6 * 10**9, bytes_accessed=8 << 20, transcendentals=0
        ),
        name=name,
    )(*inputs)


QKVG = slice(0, 4 * HEAD)
OUT = slice(4 * HEAD, 5 * HEAD)


def column_forward(tokens, weights, gain, beta_weights, seg_col, seg_row, conv, head_gain):
    count, _, length = seg_row.shape
    width = tokens[0].shape[1]
    half = width // 2
    span = [slice(0, half), slice(half, width)]
    pieces = flat(weights)

    def kernel(*refs):
        token_refs, weight_refs, rest = split_refs(refs, [2, len(pieces), 17])
        gain_ref, beta_ref, col_ref, row_ref, conv_ref, head_ref = rest[:6]
        gated_ref, inverse_ref, update_ref, mixed_ref = rest[6:10]
        mixer_ref, first_ref, second_ref, beta_in_ref = rest[10:14]
        pair_refs, hold_ref = rest[14:16], rest[16]
        weight_refs = nested(weight_refs, weights)
        collect(token_refs, hold_ref)
        values = hold_ref[...].astype(WIDE)
        scale = lax.rsqrt(jnp.sum(values * values, 1, keepdims=True) * (1.0 / D) + 1e-06)
        mixer_ref[...] = (values * scale * gain_ref[...]).astype(LOW)
        masks = masks_of(col_ref[...], row_ref[0])
        kept = kept_of(col_ref[...], conv_ref.shape[0] // 3)
        mixer_in = mixer_ref[...].astype(WIDE)
        beta_in = []
        for head, projected_ref in enumerate((first_ref, second_ref)):
            projected_ref[...] = sum(
                straight(mixer_ref[:, span[far]], atop(weight_refs[head][far], QKVG))
                for far in range(2)
            )
            beta_in.append(
                jnp.sum(mixer_in * beta_ref[head : head + 1, :].astype(WIDE), 1, keepdims=True)
            )
            beta_in_ref[:, head : head + 1] = beta_in[head]
        results = forward_heads(
            [
                [ref[:, head_lanes(part)] for part in range(4)]
                for ref in (first_ref, second_ref)
            ],
            beta_in,
            [conv_ref[:, head_lanes(head)] for head in range(2)],
            kept,
            masks,
            head_ref[...],
        )
        for head, result in enumerate(results):
            own = head_lanes(head)
            gated_ref[:, own], inverse_ref[0, head], update_ref[:, own], mixed_ref[:, own] = result
        for far in range(2):
            branch = straight(gated_ref[...], both(weight_refs, far, slice(None), OUT))
            deal(pair_refs, branch, span[far])

    inputs = list(tokens) + pieces + [gain, beta_weights, seg_col, seg_row, conv, head_gain]
    in_specs = [whole(item) for item in inputs]
    in_specs[-4] = pl.BlockSpec((length, 1), lambda i: (i, 0))
    in_specs[-3] = pl.BlockSpec((1, 1, length), lambda i: (i, 0, 0))
    step = lambda lanes: pl.BlockSpec((length, lanes), lambda i: (i, 0))
    shape = lambda lanes, kind: jax.ShapeDtypeStruct((count * length, lanes), kind)
    out = jax.ShapeDtypeStruct((length, width), LOW)
    return call(
        kernel,
        inputs,
        in_specs,
        [step(2 * HEAD)]
        + saved_specs(length)
        + [step(width), step(4 * HEAD), step(4 * HEAD), step(2)]
        + [whole(out)] * 2,
        [shape(2 * HEAD, LOW)]
        + saved_shapes(count, length)
        + [shape(width, LOW), shape(4 * HEAD, WIDE), shape(4 * HEAD, WIDE), shape(2, WIDE)]
        + [out] * 2,
        [pltpu.VMEM((length, width), LOW)],
        "column_forward",
    )


def ffn_rows_of(hidden):
    return [slice(n * hidden, (n + 1) * hidden) for n in range(3)]


def column_ffn(tokens, ways, scales, weights, hidden):
    length, width = tokens[0].shape
    half = width // 2
    span = [slice(0, half), slice(half, width)]
    pieces = flat(weights)
    gate_rows, up_rows, down_rows = ffn_rows_of(hidden)

    def kernel(*refs):
        token_refs, way_refs, (scale_ref,), weight_refs, rest = split_refs(
            refs, [2, 2, 1, len(pieces), 7]
        )
        weight_refs = nested(weight_refs, weights)
        pair_refs, token_ref, way_ref = rest[:2], rest[2], rest[3]
        active_ref, gate_ref, up_ref = rest[4:]
        collect(token_refs, token_ref)
        collect(way_refs, way_ref)
        way_ref[...] = (way_ref[...].astype(WIDE) * scale_ref[...]).astype(LOW)
        gate, upward = (
            sum(crossed(token_ref[:, span[far]], both(weight_refs, far, rows)) for far in range(2))
            for rows in (gate_rows, up_rows)
        )
        sigma = sigmoid(gate)
        opened = gate * sigma
        active_ref[...] = (opened * upward).astype(LOW)
        grad = sum(
            crossed(way_ref[:, span[far]], both(weight_refs, far, down_rows)) for far in range(2)
        )
        gate_ref[...] = (grad * upward * sigma * (1.0 + gate * (1.0 - sigma))).astype(LOW)
        up_ref[...] = (grad * opened).astype(LOW)
        for far in range(2):
            values = straight(gate_ref[...], both(weight_refs, far, gate_rows)) + straight(
                up_ref[...], both(weight_refs, far, up_rows)
            )
            deal(pair_refs, values, span[far])

    inputs = list(tokens) + list(ways) + [scales] + pieces
    in_specs = [whole(item) for item in inputs]
    in_specs[4] = pl.BlockSpec((length, 1), lambda i: (i, 0))
    out = jax.ShapeDtypeStruct((length, width), LOW)
    step = lambda lanes: pl.BlockSpec((length, lanes), lambda i: (i, 0))
    shape = lambda lanes: jax.ShapeDtypeStruct((2 * length, lanes), LOW)
    return call(
        kernel,
        inputs,
        in_specs,
        [whole(out)] * 2 + [step(width)] * 2 + [step(2 * hidden)] * 3,
        [out] * 2 + [shape(width)] * 2 + [shape(2 * hidden)] * 3,
        [],
        "column_ffn",
    )


def write_beside(ref, rows, lanes, values):
    size = ref.shape[0]
    strip = values.shape[1] // (2 * size)
    for z in range(size):
        for c in range(2):
            start = (2 * z + c) * strip
            ref[z, c, rows, lanes] = values[:, start : start + strip].astype(LOW)


def column_ffn_grads(active, gate_grad, up_grad, tokens, ways, weights, grad):
    hidden = active.shape[1] // 2
    count, width = ways.shape
    length, half = count // 2, width // 2
    pieces = flat(weights)
    rows = ffn_rows_of(hidden)

    def kernel(active_ref, gate_ref, up_ref, token_ref, way_ref, *refs):
        weight_refs = nested(refs[: len(pieces)], weights)
        near_ref, far_ref, *out = refs[len(pieces) :]
        for far in range(2):
            lanes = slice(far * half, (far + 1) * half)
            values = straight(active_ref[...], both(weight_refs, far, rows[2])).astype(LOW)
            near_ref[:, lanes] = values[:length]
            far_ref[:, lanes] = values[length:]
            for n, left_ref, right_ref in (
                (0, gate_ref, token_ref), (1, up_ref, token_ref), (2, active_ref, way_ref)
            ):
                values = turned(left_ref[...], right_ref[:, lanes])
                for i in range(2):
                    write_beside(
                        out[2 * i + far],
                        rows[n],
                        slice(None),
                        values[i * hidden : (i + 1) * hidden],
                    )

    inputs = [active, gate_grad, up_grad, tokens, ways] + pieces
    out = jax.ShapeDtypeStruct((length, width), LOW)
    near, far, *grads = call(
        kernel,
        inputs,
        [whole(item) for item in inputs],
        [whole(out)] * 2 + [whole(grad)] * 4,
        [out] * 2 + [grad] * 4,
        [],
        "column_ffn_grads",
        grid=1,
    )
    return near, far, [grads[:2], grads[2:]]


def column_backward(
    grads, weights, beta_weights, seg_col, seg_row, conv, head_gain, saved, projected, beta_in
):
    count, _, length = seg_row.shape
    lines = conv.shape[0]
    width = grads[0].shape[1]
    half = width // 2
    span = [slice(0, half), slice(half, width)]
    pieces = flat(weights)

    def kernel(*refs):
        token_refs, weight_refs, rest = split_refs(refs, [2, len(pieces), 18])
        weight_refs = nested(weight_refs, weights)
        beta_ref, col_ref, row_ref, conv_ref, head_ref = rest[:5]
        inverse_ref, update_ref, mixed_ref, first_ref, second_ref, beta_in_ref = rest[5:11]
        signal_ref, beta_grad_ref, conv_grad_ref, head_grad_ref = rest[11:15]
        pair_refs, hold_ref = rest[15:17], rest[17]
        collect(token_refs, hold_ref)
        masks = masks_of(col_ref[...], row_ref[0])
        kept = kept_of(col_ref[...], conv_ref.shape[0] // 3)
        head_grad = jnp.zeros((1, HEAD), WIDE)
        beta_grads = []
        grad = sum(
            crossed(hold_ref[:, span[far]], both(weight_refs, far, slice(None), OUT))
            for far in range(2)
        )
        for head, projected_ref in enumerate((first_ref, second_ref)):
            own = head_lanes(head)
            signal_grads, beta_grad, conv_lines, gain_grad = backward_head(
                [projected_ref[:, head_lanes(part)] for part in range(4)],
                beta_in_ref[:, head : head + 1],
                conv_ref[:, own],
                kept,
                masks,
                head_ref[...],
                inverse_ref[0, head],
                update_ref[:, own],
                mixed_ref[:, own],
                grad[:, own],
            )
            head_grad = head_grad + gain_grad
            beta_grads.append(beta_grad.astype(LOW).astype(WIDE))
            beta_grad_ref[:, head : head + 1] = beta_grad
            for line, values in enumerate(conv_lines):
                conv_grad_ref[0, line : line + 1, own] = values
            for part in range(4):
                signal_ref[:, head_lanes(4 * head + part)] = signal_grads[part]
        head_grad_ref[0] = head_grad
        for far in range(2):
            values = sum(
                crossed(
                    signal_ref[:, 4 * HEAD * head : 4 * HEAD * (head + 1)],
                    atop(weight_refs[head][far], QKVG),
                )
                + beta_grads[head] * beta_ref[head : head + 1, span[far]].astype(WIDE)
                for head in range(2)
            )
            deal(pair_refs, values, span[far])

    inputs = (
        list(grads)
        + pieces
        + [beta_weights, seg_col, seg_row, conv, head_gain]
        + list(saved)
        + list(projected)
        + [beta_in]
    )
    in_specs = [whole(item) for item in inputs]
    step = lambda lanes: pl.BlockSpec((length, lanes), lambda i: (i, 0))
    in_specs[-10] = step(1)
    in_specs[-9] = pl.BlockSpec((1, 1, length), lambda i: (i, 0, 0))
    in_specs[-6:] = saved_specs(length) + [step(4 * HEAD), step(4 * HEAD), step(2)]
    out = jax.ShapeDtypeStruct((length, width), LOW)
    return call(
        kernel,
        inputs,
        in_specs,
        grad_specs(length, lines) + [whole(out)] * 2 + [step(width)],
        grad_shapes(count, length, lines)
        + [out] * 2
        + [jax.ShapeDtypeStruct((count * length, width), LOW)],
        [],
        "column_backward",
    )


def column_mixer_grads(mixer_in, signal_grads, gated, ways, grad):
    half = mixer_in.shape[1] // 2
    strip = grad.shape[2]

    def kernel(mixer_ref, signal_ref, gated_ref, way_ref, *grad_refs):
        for far in range(2):
            lanes = slice(far * half, (far + 1) * half)
            outs = turned(gated_ref[...], way_ref[:, lanes])
            for head in range(2):
                ref = grad_refs[2 * head + far]
                values = turned(
                    mixer_ref[:, lanes], signal_ref[:, 4 * HEAD * head : 4 * HEAD * (head + 1)]
                ).astype(LOW)
                for z in range(ref.shape[0]):
                    for c in range(2):
                        start = (2 * z + c) * strip
                        ref[z, c, :, QKVG] = values[start : start + strip]
                write_beside(ref, slice(None), OUT, outs[head_lanes(head)])

    inputs = [mixer_in, signal_grads, gated, ways]
    grads = call(
        kernel,
        inputs,
        [whole(item) for item in inputs],
        [whole(grad)] * 4,
        [grad] * 4,
        [],
        "column_mixer_grads",
        grid=1,
    )
    return [grads[:2], grads[2:]]


def contract(left, right, left_dim, right_dim):
    return lax.dot_general(
        left, right, (((left_dim,), (right_dim,)), ((), ())), preferred_element_type=WIDE
    )


def after(values, earlier):
    return lax.optimization_barrier((values, earlier))[0]


def exclusive_order(blocks):
    place = lax.axis_index("dmod")
    for bit in (1, 2):
        flip = (place & bit) != 0
        blocks = [jnp.where(flip, blocks[i ^ bit], blocks[i]) for i in range(4)]
    return blocks


def trade(blocks):
    return [blocks[0]] + [
        lax.ppermute(blocks[m], "dmod", [(i, i ^ m) for i in range(4)]) for m in (1, 2, 3)
    ]


def gather_width(values):
    far = lax.ppermute(values, "dmod", ACROSS)
    near = lax.ppermute(values, "dmod", CORE)
    return [values, near, far, lax.ppermute(far, "dmod", CORE)]


def scatter_width(blocks):
    near = lax.ppermute(blocks[1].astype(LOW), "dmod", CORE)
    cross = lax.ppermute(blocks[3].astype(LOW), "dmod", CORE)
    far = lax.ppermute((blocks[2] + cross.astype(WIDE)).astype(LOW), "dmod", ACROSS)
    return blocks[0] + near.astype(WIDE) + far.astype(WIDE)


def sum_pair(values):
    low = values.astype(LOW)
    return low.astype(WIDE) + lax.ppermute(low, "mp", SWAP).astype(WIDE)


def row_total(values):
    return lax.psum(values, "dmod")


class Ring:
    def __init__(self):
        self.size = lax.axis_size("dp")
        self.parts = 1

    def order(self, values):
        return values

    def gather(self, values):
        return [lax.all_gather(values, "dp", axis=1, tiled=True)]

    def scatter(self, make):
        return lax.psum_scatter(
            make(0).astype(LOW), "dp", scatter_dimension=1, tiled=True
        ).astype(WIDE)


def plane_body(
    block_input,
    segment_ids,
    group_ids,
    group_weight,
    mixer_norm,
    w_mix,
    w_beta,
    conv_kernel,
    head_norm,
    w_out,
    ffn_norm,
    w_ffn_in,
    w_ffn_down,
    cotangent,
):
    ring = Ring()
    parts = ring.parts
    micro, seqs, length, width = block_input.shape
    tokens = micro * seqs * length
    block = width // parts
    strip = w_mix.shape[0]
    span = w_mix.shape[2] // 4
    hidden = w_ffn_in.shape[2] // 4
    dmod = lax.axis_index("dmod")
    data_size = ring.size
    place = lax.axis_index("dp")

    lines = conv_kernel.shape[0] * conv_kernel.shape[1]
    pack = jnp.concatenate(
        [
            conv_kernel.reshape(-1),
            head_norm,
            mixer_norm,
            ffn_norm,
            w_beta.T.reshape(-1),
        ]
    )
    packs = lax.all_gather(pack, "dp", axis=0)
    sizes = [conv_kernel.size, head_norm.size, strip, strip, w_beta.size]
    cuts = [sum(sizes[:i]) for i in range(6)]
    conv = (
        packs[:, cuts[0] : cuts[1]]
        .reshape(data_size, lines, -1)
        .transpose(1, 0, 2)
        .reshape(lines, span)
        .astype(WIDE)
    )
    head_gain = packs[:, cuts[1] : cuts[2]].reshape(1, -1).astype(WIDE)
    gain_one = ring.order(packs[:, cuts[2] : cuts[3]].reshape(1, -1).astype(WIDE))
    gain_two = ring.order(packs[:, cuts[3] : cuts[4]].reshape(1, -1).astype(WIDE))
    beta_weights = ring.order(
        packs[:, cuts[4] : cuts[5]]
        .reshape(data_size, -1, strip)
        .transpose(1, 0, 2)
        .reshape(-1, width)
    )

    out_rows = jnp.concatenate(exclusive_order(jnp.split(w_out, 4, axis=0)), 0)
    out_halves = jnp.split(out_rows.T, 2, axis=1)
    mix_own = jnp.stack(trade(exclusive_order(jnp.split(w_mix, 4, axis=2))))
    mix_halves = [
        mix_own[:, :, :, head * HEAD : (head + 1) * HEAD].reshape(4, strip, 4 * HEAD)
        for head in (0, 1)
    ]
    ffn_own = jnp.stack(trade(exclusive_order(jnp.split(w_ffn_in, 4, axis=2))))
    ffn_halves = [ffn_own[:, :, 0], ffn_own[:, :, 1]]
    down_own = trade(exclusive_order(jnp.split(w_ffn_down, 4, axis=0)))
    down_halves = [
        jnp.stack([down_own[0].T, down_own[1].T]),
        jnp.stack([down_own[2].T, down_own[3].T]),
    ]

    def chain(half):
        first = ring.gather(out_halves[half][None])
        second = ring.gather(after(mix_halves[half], first[-1]))
        third = ring.gather(after(ffn_halves[half], second[-1]))
        fourth = ring.gather(after(down_halves[half], third[-1]))
        return first, second, third, fourth

    chains = [chain(0), chain(1)]
    out_weights = jnp.concatenate(
        [
            jnp.concatenate([part[0] for part in chains[0][0]], 0),
            jnp.concatenate([part[0] for part in chains[1][0]], 0),
        ],
        1,
    )
    mix_parts = [[part.reshape(4 * block, -1) for part in each[1]] for each in chains]
    ffn_parts = [[part.reshape(4 * block, -1) for part in each[2]] for each in chains]
    down_parts = [[part.reshape(2 * block, -1) for part in each[3]] for each in chains]

    marks = (group_ids.reshape(tokens, 1) == jnp.arange(group_weight.shape[0])[None]).astype(WIDE)
    counts = lax.psum(jnp.sum(marks, 0), "dp")
    table = group_weight * (tokens * data_size / group_weight.shape[0]) / counts
    scales = jnp.sum(marks * table, -1, keepdims=True)
    direction = ring.order(cotangent.reshape(tokens, width).astype(WIDE)) * scales
    direction_low = direction.astype(LOW)

    def by_part(slots):
        return [
            jnp.concatenate([slot[:, k * block : (k + 1) * block] for slot in slots], 1)
            for k in range(parts)
        ]

    def by_slot(pieces):
        return [
            jnp.concatenate([piece[:, m * block : (m + 1) * block] for piece in pieces], 1)
            for m in range(pieces[0].shape[1] // block)
        ]

    direction_parts = by_part(gather_width(direction_low))

    rows = ring.order(block_input.reshape(tokens, width).astype(WIDE))
    first_scale = lax.rsqrt(row_total(jnp.sum(rows * rows, -1, keepdims=True)) / D + 1e-06)
    mixer_in = (rows * first_scale * gain_one).astype(LOW)
    mixer_parts = by_part(gather_width(mixer_in))
    projected = [
        sum(jnp.dot(mixer_parts[k], mix_parts[half][k], preferred_element_type=WIDE) for k in range(parts))
        for half in (0, 1)
    ]
    beta_all = row_total(contract(beta_weights, mixer_in, 1, 1))
    heads = span // HEAD
    beta_in = lax.dynamic_slice_in_dim(beta_all, dmod * heads, heads, 0).T
    seg_col = segment_ids.reshape(tokens, 1)
    seg_row = segment_ids.reshape(micro * seqs, 1, length)
    mixer_args = list(projected) + [
        beta_in, seg_col, seg_row, conv, head_gain
    ]
    gated, *saved = mixer_forward(mixer_args)
    gated_all = jnp.concatenate(gather_width(gated), 1)
    middle = rows + sum_pair(contract(gated_all, out_weights, 1, 1))

    second_scale = lax.rsqrt(row_total(jnp.sum(middle * middle, -1, keepdims=True)) / D + 1e-06)
    ffn_in = (middle * second_scale * gain_two).astype(LOW)
    ffn_in_parts = by_part(gather_width(ffn_in))
    gate, upward = (
        sum(jnp.dot(ffn_in_parts[k], ffn_parts[half][k], preferred_element_type=WIDE) for k in range(parts))
        for half in (0, 1)
    )
    sigma = sigmoid(gate)
    active = (gate * sigma * upward).astype(LOW)
    down_slots = sum(
        (
            by_slot([contract(active, down_parts[half][k], 1, 1) for k in range(parts)])
            for half in (0, 1)
        ),
        [],
    )
    result = middle + sum_pair(scatter_width(down_slots))
    out = ring.order(result).astype(LOW).reshape(block_input.shape)

    down_grads = [
        ring.scatter(
            lambda k: contract(
                direction_parts[k][:, 2 * half * block : 2 * (half + 1) * block], active, 0, 0
            ).reshape(2, block, hidden)
        )
        for half in (0, 1)
    ]
    active_grad = sum(
        jnp.dot(
            direction_parts[k][:, 2 * half * block : 2 * (half + 1) * block],
            down_parts[half][k],
            preferred_element_type=WIDE,
        )
        for k in range(parts)
        for half in (0, 1)
    )
    gate_grad = (active_grad * upward * sigma * (1.0 + gate * (1.0 - sigma))).astype(LOW)
    upward_grad = (active_grad * gate * sigma).astype(LOW)
    ffn_slots = by_slot(
        [
            contract(gate_grad, ffn_parts[0][k], 1, 1) + contract(upward_grad, ffn_parts[1][k], 1, 1)
            for k in range(parts)
        ]
    )
    ffn_grads = [
        ring.scatter(lambda k: contract(ffn_in_parts[k], grad, 0, 0).reshape(4, block, hidden))
        for grad in (gate_grad, upward_grad)
    ]
    ffn_in_grad = sum_pair(scatter_width(ffn_slots))
    weighted_two = ffn_in_grad * gain_two
    norm_two_grad = jnp.sum(ffn_in_grad * middle * second_scale, 0)
    inner_two = row_total(jnp.sum(weighted_two * middle, -1, keepdims=True))
    middle_grad = (
        direction + second_scale * weighted_two - middle * (second_scale**3 * inner_two / D)
    )

    branch_low = middle_grad.astype(LOW)
    out_grads = [
        ring.scatter(
            lambda k: contract(
                branch_low[:, k * block : (k + 1) * block],
                gated_all[:, 2 * half * span : 2 * (half + 1) * span],
                0,
                0,
            )[None]
        )
        for half in (0, 1)
    ]
    gated_slots = jnp.split(jnp.dot(branch_low, out_weights, preferred_element_type=WIDE), 4, axis=1)
    gated_grad = scatter_width(gated_slots)
    projected_grad, beta_grad, conv_grad, head_grad = mixer_backward(
        mixer_args, saved, gated_grad
    )
    projected_slots = gather_width(projected_grad)
    mix_grads = [
        ring.scatter(
            lambda k: contract(
                mixer_in[:, k * block : (k + 1) * block],
                jnp.concatenate(projected_slots[2 * half : 2 * half + 2], 1),
                0,
                0,
            )[None]
        )
        for half in (0, 1)
    ]
    beta_slots = jnp.concatenate(
        exclusive_order(gather_width(beta_grad.T.astype(LOW))), 0
    )
    beta_weight_grad = contract(beta_slots, mixer_in, 1, 0)
    mixer_slots = by_slot(
        [
            contract(projected_grad[:, : 2 * span], mix_parts[0][k], 1, 1)
            + contract(projected_grad[:, 2 * span :], mix_parts[1][k], 1, 1)
            for k in range(parts)
        ]
    )
    mixer_grad = sum_pair(scatter_width(mixer_slots) + contract(beta_slots, beta_weights, 0, 0))
    weighted_one = mixer_grad * gain_one
    norm_one_grad = jnp.sum(mixer_grad * rows * first_scale, 0)
    inner_one = row_total(jnp.sum(weighted_one * rows, -1, keepdims=True))
    grad_input = ring.order(
        middle_grad + first_scale * weighted_one - rows * (first_scale**3 * inner_one / D)
    ).reshape(block_input.shape)

    head_total = lax.psum(jnp.sum(head_grad, (0, 1)), ("dp", "mp", "dmod"))
    head_out = lax.dynamic_slice_in_dim(head_total, place * head_norm.size, head_norm.size, 0)
    small = jnp.concatenate(
        [
            jnp.sum(conv_grad, 0),
            ring.order(jnp.stack([norm_one_grad, norm_two_grad]))
            .reshape(2, data_size, -1)
            .transpose(1, 0, 2)
            .reshape(data_size, -1)
            .reshape(-1)
            .reshape(-1, span),
            ring.order(beta_weight_grad)
            .reshape(-1, data_size, strip)
            .transpose(1, 0, 2)
            .reshape(-1, span),
        ],
        0,
    )
    conv_part = (
        small[:lines].reshape(lines, data_size, -1).transpose(1, 0, 2).reshape(data_size, -1)
    )
    norm_part = small[lines : lines + 2 * width // span].reshape(data_size, -1)
    beta_part = small[lines + 2 * width // span :].reshape(data_size, -1)
    small_own = lax.psum_scatter(
        jnp.concatenate([conv_part, norm_part, beta_part], 1), "dp", scatter_dimension=0
    )
    conv_out = small_own[: conv_kernel.size].reshape(conv_kernel.shape)
    norm_one_out = small_own[conv_kernel.size : conv_kernel.size + strip]
    norm_two_out = small_own[conv_kernel.size + strip : conv_kernel.size + 2 * strip]
    beta_out = small_own[conv_kernel.size + 2 * strip :].reshape(-1, strip).T

    def placed(blocks):
        return exclusive_order(trade([values.astype(LOW) for values in blocks]))

    ffn_out = jnp.stack(
        [
            jnp.concatenate([values.astype(WIDE) for values in placed(list(grad))], 1)
            for grad in ffn_grads
        ],
        1,
    )
    down_out = jnp.concatenate(
        [
            values.astype(WIDE).T
            for values in placed(list(down_grads[0]) + list(down_grads[1]))
        ],
        0,
    )
    out_out = jnp.concatenate(
        exclusive_order(jnp.split(jnp.concatenate([grad[0] for grad in out_grads], 1).T, 4, axis=0)),
        0,
    )
    mix_blocks = sum((jnp.split(grad[0], 2, axis=1) for grad in mix_grads), [])
    mix_out = jnp.concatenate(
        [
            values.reshape(strip, 2, 4, HEAD).transpose(0, 2, 1, 3).reshape(strip, 4, span)
            for values in exclusive_order(mix_blocks)
        ],
        2,
    )
    return (
        out,
        grad_input,
        norm_one_out,
        mix_out,
        beta_out,
        conv_out,
        head_out,
        out_out,
        norm_two_out,
        ffn_out,
        down_out,
    )


def exchange(values, axis):
    return lax.all_to_all(values, axis, 0, 0, tiled=True)


def swap_mp(values):
    return lax.ppermute(values, "mp", SWAP)


def swap_core(values):
    return lax.ppermute(values, "dmod", CORE)


def swap_across(values):
    return lax.ppermute(values, "dmod", ACROSS)


def swap_dp(values, k):
    return lax.ppermute(values, "dp", [(i, i ^ k) for i in range(lax.axis_size("dp"))])


def trade_blocks(blocks, axis, place):
    size = len(blocks)
    blocks = by_difference(blocks, place)
    moved = [blocks[0]] + [
        lax.ppermute(blocks[k], axis, [(i, i ^ k) for i in range(size)]) for k in range(1, size)
    ]
    return by_difference(moved, place)


def by_difference(blocks, place):
    bit = 1
    while bit < len(blocks):
        flip = (place & bit) != 0
        blocks = [jnp.where(flip, blocks[i ^ bit], blocks[i]) for i in range(len(blocks))]
        bit *= 2
    return blocks


def everyone(values, place):
    size = lax.axis_size("dp")
    values = values[None]
    bit = 1
    while bit < size:
        values = jnp.concatenate(turn((place & bit) != 0, (values, swap_dp(values, bit))), 0)
        bit *= 2
    return values


def turn(flag, pair):
    return jnp.where(flag, pair[1], pair[0]), jnp.where(flag, pair[0], pair[1])


def chip_blocks(core, pair):
    keep, send = turn(core, pair)
    return jnp.stack(turn(core, (keep, swap_core(send))), 1)


def along_column(core, pair, earlier=None):
    both = chip_blocks(core, pair)
    if earlier is not None:
        both = after(both, earlier)
    return exchange(both, "dp")


def gather_columns(values, earlier=None, later=None):
    if earlier is not None:
        values = after(values, earlier)
    half = values.shape[0] // 2
    over = swap_mp(values)
    far = swap_across(values)
    corner = (over[:half], far[half:])
    if later is not None:
        corner = after(corner, later)
    both = [swap_across(corner[0]), swap_mp(corner[1])]
    return [[[values], [far]], [[over], both]]


def wide(values):
    return values.astype(WIDE)


def scatter_send(grid):
    half = grid[0][0].shape[0] // 2
    return (
        jnp.concatenate([grid[1][0][:half], grid[1][1][:half]], 0),
        jnp.concatenate([grid[0][1][half:], grid[1][1][half:]], 0),
    )


def scatter_turn(grid, sent):
    half = grid[0][0].shape[0] // 2
    top = wide(grid[0][1][:half]) + wide(sent[0][half:])
    low = wide(grid[1][0][half:]) + wide(sent[1][half:])
    return top.astype(LOW), low.astype(LOW)


def scatter_end(grid, sent, back):
    half = grid[0][0].shape[0] // 2
    top = wide(grid[0][0][:half]) + wide(sent[0][:half]) + wide(swap_across(back[0]))
    low = wide(grid[0][0][half:]) + wide(sent[1][:half]) + wide(swap_mp(back[1]))
    return jnp.concatenate([top, low], 0).astype(LOW)


def column_tokens(values):
    size = lax.axis_size("dp")
    moved = [values] + [swap_dp(values, k) for k in range(1, size)]
    mine = jnp.concatenate(by_difference(moved, lax.axis_index("dp")), 0)
    return [mine, swap_core(mine)]


def column_chip(near, far):
    return (wide(near) + wide(swap_core(far))).astype(LOW)


def column_total(chip):
    size = lax.axis_size("dp")
    moved = exchange(chip, "dp").reshape(size, chip.shape[0] // size, -1)
    return jnp.sum(wide(moved), 0)


def column_hops(chip):
    size = lax.axis_size("dp")
    blocks = by_difference(jnp.split(chip, size), lax.axis_index("dp"))
    return sum([wide(blocks[0])] + [wide(swap_dp(blocks[k], k)) for k in range(1, size)])


def column_body(
    block_input,
    segment_ids,
    group_ids,
    group_weight,
    mixer_norm,
    w_mix,
    w_beta,
    conv_kernel,
    head_norm,
    w_out,
    ffn_norm,
    w_ffn_in,
    w_ffn_down,
    cotangent,
):
    place = lax.axis_index("dp")
    size = lax.axis_size("dp")
    side = lax.axis_index("mp")
    dmod = lax.axis_index("dmod")
    row, core = dmod // 2, dmod % 2
    at_far_side, at_far_row, at_core = side == 1, row == 1, core == 1
    micro, _, length, width = block_input.shape
    share = length // size
    strip = w_mix.shape[0]
    groups = group_weight.shape[0]
    group_heads = w_beta.shape[1]
    hidden = w_ffn_down.shape[0] // (2 * size)
    span = 2 * width

    def to_column(values):
        lead = values.shape[:-1]
        values = values.reshape(lead + (2, 2, size, strip))
        values = jnp.swapaxes(values, -2, -3).reshape(lead + (2, span))
        return jnp.concatenate(turn(at_far_row, (values[..., 0, :], values[..., 1, :])), -1)

    def from_column(values):
        lead = values.shape[:-1]
        halves_of = turn(at_far_row, (values[..., :span], values[..., span:]))
        values = jnp.stack(halves_of, -2).reshape(lead + (2, size, 2, strip))
        return jnp.swapaxes(values, -2, -3).reshape(lead + (2 * span,))

    def over_dp(values):
        values = values.reshape(micro, size, share, width)
        moved = trade_blocks([values[:, z] for z in range(size)], "dp", place)
        moved = jnp.where(at_far_side, jnp.stack(moved[2:]), jnp.stack(moved[:2]))
        return moved.reshape(4, share, width)

    def over_dmod(moved):
        moved = trade_blocks([moved[j] for j in range(4)], "dmod", dmod)
        return to_column(jnp.concatenate(moved, 1))

    def tokens_out(values):
        blocks = jnp.split(from_column(values), 4, axis=1)
        moved = jnp.stack(trade_blocks(blocks, "dmod", dmod)).reshape(2, micro, share, width)
        moved = jnp.concatenate(turn(at_far_side, (moved, swap_mp(moved))), 0)
        moved = trade_blocks([moved[z] for z in range(size)], "dp", place)
        return jnp.stack(moved, 1).reshape(block_input.shape)

    blocks = w_mix.reshape(strip, 4, 2, size, HEAD).transpose(2, 3, 0, 1, 4)
    blocks = blocks.reshape(2, size, strip, 4 * HEAD)
    blocks = jnp.concatenate([blocks, w_out.reshape(2, size, HEAD, strip)], 3)
    mix_blocks = chip_blocks(at_core, (blocks[0], blocks[1]))
    mix_pieces = exchange(mix_blocks, "dp")
    block_input, cotangent, conv_kernel, w_ffn_in, w_ffn_down = after(
        (block_input, cotangent, conv_kernel, w_ffn_in, w_ffn_down), mix_blocks
    )
    blocks = jnp.concatenate(
        [
            w_ffn_in.transpose(1, 2, 0).reshape(2, 2 * size, hidden, strip),
            w_ffn_down.reshape(1, 2 * size, hidden, strip),
        ],
        0,
    )
    blocks = blocks.transpose(1, 0, 2, 3).reshape(2, size, 3 * hidden, strip)
    ffn_blocks = chip_blocks(at_core, (blocks[0], blocks[1]))

    small = [
        conv_kernel.reshape(-1),
        head_norm,
        mixer_norm,
        ffn_norm,
        w_beta.T.reshape(-1),
        segment_ids.reshape(-1).astype(LOW),
        group_ids.reshape(-1).astype(LOW),
    ]
    count = sum(item.size for item in small)
    pack = jnp.concatenate(small + [jnp.zeros((-count % HEAD,), LOW)]).reshape(-1, HEAD)
    packs = everyone(pack, place)
    packs = jnp.stack(turn(at_far_side, (packs, swap_mp(packs))))
    packs = jnp.stack(turn(at_core, (packs, swap_core(packs))))
    packs = jnp.stack(turn(at_far_row, (packs, swap_across(packs))))
    packs = packs.reshape(2, 2, 2, size, -1)

    tokens_low, way_moved = over_dp(block_input), over_dp(cotangent)
    tokens_low = over_dmod(after(tokens_low, (mix_pieces, packs, ffn_blocks)))
    rows = wide(tokens_low)
    tokens_pair = column_tokens(tokens_low)
    mix_weights = gather_columns(mix_pieces)
    ffn_pieces = exchange(ffn_blocks, "dp")
    way_low = over_dmod(after(way_moved, tokens_pair[0]))

    fields = []
    start = 0
    for item in small:
        fields.append(packs[..., start : start + item.size])
        start += item.size
    lines = conv_kernel.shape[0] * conv_kernel.shape[1]
    heads = 2 * group_heads
    local_head = size * core + place
    own_heads = [group_heads * side + local_head, group_heads * (1 - side) + local_head]
    conv_all = (
        fields[0]
        .reshape(2, 2, 2, size, lines, -1)
        .transpose(4, 2, 0, 1, 3, 5)
        .reshape(lines, heads * HEAD)
    )
    conv = wide(
        jnp.concatenate(
            [lax.dynamic_slice_in_dim(conv_all, head * HEAD, HEAD, 1) for head in own_heads], 1
        )
    )
    head_gain = wide(fields[1][0, 0, 0].reshape(1, HEAD))
    gain_one = to_column(wide(fields[2][:, :, 0].reshape(1, -1)))
    gain_two = to_column(wide(fields[3][:, :, 0].reshape(1, -1)))
    beta_rows = (
        fields[4]
        .reshape(2, 2, 2, size, group_heads, strip)
        .transpose(2, 4, 0, 1, 3, 5)
        .reshape(heads, -1)
    )
    beta_weights = to_column(
        jnp.concatenate([lax.dynamic_slice_in_dim(beta_rows, head, 1, 0) for head in own_heads], 0)
    )
    sequence = 2 * side + row
    segments = lax.dynamic_index_in_dim(fields[5][0, 0, 0], sequence, 0, keepdims=False)
    segments = segments.reshape(micro, length).astype(jnp.int32)
    segments = jnp.concatenate(turn(at_core, (segments[:1], segments[1:])), 0)
    seg_col = segments.reshape(-1, 1)
    seg_row = segments.reshape(micro, 1, length)
    all_groups = fields[6][0, 0, 0].reshape(-1).astype(jnp.int32)
    names = jnp.arange(groups, dtype=jnp.int32)
    counts = jnp.sum((all_groups[:, None] == names[None]).astype(WIDE), 0)
    table = group_weight * (all_groups.shape[0] / groups) / counts
    own_groups = lax.dynamic_slice_in_dim(all_groups, sequence * micro * length, micro * length, 0)
    scales = jnp.sum((own_groups[:, None] == names[None]).astype(WIDE) * table, -1, keepdims=True)
    scales = jnp.concatenate(turn(at_core, (scales[:length], scales[length:])), 0)

    constants = [beta_weights, seg_col, seg_row, conv, head_gain]
    gated, inverse, update, mixed, mixer_in, *projected, beta_in, near, far = column_forward(
        tokens_pair, mix_weights, gain_one, *constants
    )
    middle = rows + column_total(after(column_chip(near, far), ffn_pieces))

    second_scale = lax.rsqrt(jnp.mean(middle * middle, -1, keepdims=True) + 1e-06)
    ffn_low = (middle * second_scale * gain_two).astype(LOW)
    way_pair = column_tokens(after(way_low, middle))
    direction = wide(way_low) * lax.dynamic_slice_in_dim(scales, place * share, share, 0)
    ffn_pair = column_tokens(ffn_low)
    ffn_weights = gather_columns(ffn_pieces, mix_weights[1][1])
    near, far, ffn_in, directions, active, gate_grad, up_grad = column_ffn(
        ffn_pair, way_pair, scales, ffn_weights, hidden
    )
    chip = column_chip(near, far)
    ffn_in_grad = column_hops(chip)
    near, far, ffn_grads = column_ffn_grads(
        after(active, chip),
        gate_grad,
        up_grad,
        ffn_in,
        directions,
        ffn_weights,
        jax.ShapeDtypeStruct((size, 2, 3 * hidden, strip), LOW),
    )
    out_chip = column_chip(near, far)
    ffn_sent = scatter_send(ffn_grads)
    ffn_in_grad = after(ffn_in_grad, out_chip)
    ffn_sent = swap_mp(ffn_sent[0]), swap_across(ffn_sent[1])

    weighted_two = ffn_in_grad * gain_two
    norm_two_grad = jnp.sum(ffn_in_grad * middle * second_scale, 0, keepdims=True)
    inner_two = jnp.mean(weighted_two * middle, -1, keepdims=True)
    middle_grad = (
        direction + second_scale * weighted_two - middle * (second_scale**3 * inner_two)
    )
    branch_pair = column_tokens(middle_grad.astype(LOW))
    down_sum = column_total(after(out_chip, branch_pair[0]))
    ffn_back = scatter_turn(ffn_grads, ffn_sent)

    signal_grads, beta_grad, conv_grad, head_grad, near, far, branch_all = column_backward(
        branch_pair,
        mix_weights,
        *constants,
        (inverse, update, mixed),
        projected,
        beta_in,
    )
    mix_grads = column_mixer_grads(
        mixer_in,
        signal_grads,
        gated,
        branch_all,
        jax.ShapeDtypeStruct((size, 2, strip, 5 * HEAD), LOW),
    )
    chip = column_chip(near, far)
    mixer_grad = column_total(chip)
    ffn_total = scatter_end(ffn_grads, ffn_sent, ffn_back)
    mix_sent = scatter_send(mix_grads)
    mix_sent = after((swap_mp(mix_sent[0]), swap_across(mix_sent[1])), mixer_grad)
    mix_back = scatter_turn(mix_grads, mix_sent)
    mix_total = scatter_end(mix_grads, mix_sent, mix_back)
    out_low = (middle + after(down_sum, mix_back)).astype(LOW)

    def placed(total, earlier=None):
        return along_column(at_core, (total[:, 0], total[:, 1]), earlier).transpose(1, 0, 2, 3)

    ffn_pieces = placed(ffn_total)
    ffn_out = wide(
        ffn_pieces[:, :, : 2 * hidden]
        .reshape(2 * size, 2, hidden, strip)
        .transpose(1, 0, 2, 3)
        .reshape(2, -1, strip)
        .transpose(2, 0, 1)
    )
    down_out = wide(ffn_pieces[:, :, 2 * hidden :].reshape(-1, strip))
    mix_pieces = placed(mix_total, ffn_pieces).reshape(2 * size, strip, 5, HEAD)
    mix_out = wide(mix_pieces[:, :, :4].transpose(1, 2, 0, 3).reshape(strip, 4, -1))
    out_out = wide(mix_pieces[:, :, 4].reshape(-1, strip))
    beta_weight_grad = contract(beta_grad.astype(LOW), mixer_in, 0, 0)
    weighted_one = mixer_grad * gain_one
    first_scale = lax.rsqrt(jnp.mean(rows * rows, -1, keepdims=True) + 1e-06)
    norm_one_grad = jnp.sum(mixer_grad * rows * first_scale, 0, keepdims=True)
    inner_one = jnp.mean(weighted_one * rows, -1, keepdims=True)
    grad_low = (
        middle_grad + first_scale * weighted_one - rows * (first_scale**3 * inner_one)
    ).astype(LOW)
    out = tokens_out(out_low)
    grad_input = wide(tokens_out(grad_low))

    conv_sides = jnp.stack(turn(at_far_side, jnp.split(jnp.sum(conv_grad, 0), 2, axis=1)))
    beta_sides = from_column(
        jnp.concatenate(turn(at_far_side, (beta_weight_grad[:1], beta_weight_grad[1:])), 0)
    )
    vector = jnp.concatenate(
        [
            conv_sides.reshape(-1, HEAD),
            beta_sides.reshape(-1, HEAD),
            from_column(norm_one_grad).reshape(-1, HEAD),
            from_column(norm_two_grad).reshape(-1, HEAD),
            jnp.sum(head_grad, 0),
        ]
    )
    vector = after(vector, mix_back)
    vector = vector + swap_mp(vector)
    vector = vector + swap_across(vector)
    vectors = jnp.stack(turn(at_core, (vector, swap_core(vector))))
    vectors = everyone(vectors, place)
    ends = [2 * lines, 2 * lines + 4 * span // HEAD]
    own_width = dmod * width + place * strip
    taps_own = conv_kernel.shape[2]
    at = (dmod * size + place) * taps_own
    conv_head = at // HEAD
    conv_out = lax.dynamic_slice(
        vectors,
        (conv_head % size, conv_head // size, side * lines, at % HEAD),
        (1, 1, lines, taps_own),
    ).reshape(conv_kernel.shape)
    beta_out = (
        lax.dynamic_slice(
            vectors[:, :, ends[0] : ends[1]].reshape(size, 2, 2, 2 * span),
            (0, 0, side, own_width),
            (size, 2, 1, strip),
        )
        .reshape(size, 2, strip)
        .transpose(2, 1, 0)
        .reshape(strip, group_heads)
    )
    sums = jnp.sum(vectors[:, :, ends[1] :], (0, 1))
    norms = sums[:-1].reshape(2, -1)
    norm_one_out, norm_two_out = (
        lax.dynamic_slice_in_dim(norms[i], own_width, strip, 0) for i in (0, 1)
    )
    head_out = lax.dynamic_slice_in_dim(sums[-1], place * head_norm.size, head_norm.size, 0)
    return (
        out,
        grad_input,
        norm_one_out,
        mix_out,
        beta_out,
        conv_out,
        head_out,
        out_out,
        norm_two_out,
        ffn_out,
        down_out,
    )


def solution(mesh):
    sizes = dict(mesh.shape)
    columns = sizes["mp"] * sizes["dmod"] // 2
    body = column_body if columns == sizes["dp"] else plane_body
    wide = P(("dmod", "dp"))
    tokens = P(None, "dp", None, "dmod")
    weights = (
        wide,
        P(("dmod", "dp"), None, "mp"),
        P(("dmod", "dp"), "mp"),
        P(None, None, ("mp", "dmod", "dp")),
        P("dp"),
        P("mp", ("dmod", "dp")),
        wide,
        P(("dmod", "dp"), None, "mp"),
        P("mp", ("dmod", "dp")),
    )
    ids = P(None, "dp", None)
    return jax.shard_map(
        body,
        mesh=mesh,
        in_specs=(tokens, ids, ids, P()) + weights + (tokens,),
        out_specs=(tokens, tokens) + weights,
        check_vma=False,
    )
```

```python
import jax
import jax.numpy as jnp
from jax import lax
from jax.experimental import pallas as pl
from jax.experimental.pallas import tpu as pltpu
from jax.sharding import PartitionSpec as P

D = 2048
HEAD = 128
LOW = jnp.bfloat16
WIDE = jnp.float32
LONGEST_RING = 1
CORE = [(i, i ^ 1) for i in range(4)]
ACROSS = [(i, i ^ 2) for i in range(4)]
SWAP = [(0, 1), (1, 0)]


def halves(values):
    high = values.astype(LOW)
    return high, (values - high.astype(WIDE)).astype(LOW)


def product(left, right, left_dim, right_dim):
    def one(a, b):
        return lax.dot_general(
            a, b, (((left_dim,), (right_dim,)), ((), ())), preferred_element_type=WIDE
        )

    return one(left[0], right[0]) + (one(left[0], right[1]) + one(left[1], right[0]))


def sigmoid(values):
    return 1.0 / (1.0 + jnp.exp(-values))


def masks_of(seg_col, seg_row):
    length = seg_col.shape[0]
    rows = lax.broadcasted_iota(jnp.int32, (length, length), 0)
    cols = lax.broadcasted_iota(jnp.int32, (length, length), 1)
    same = seg_col == seg_row
    return rows, cols, same & (cols < rows), same & (cols <= rows)


def kept_of(seg_col, taps):
    length = seg_col.shape[0]
    wide = jnp.broadcast_to(seg_col, (length, HEAD))
    place = lax.broadcasted_iota(jnp.int32, (length, HEAD), 0)
    return [
        ((pltpu.roll(wide, shift, 0) == wide) & (place >= shift)).astype(WIDE)
        for shift in range(1, taps)
    ]


def convolve(signal, kernel, kept):
    taps = kernel.shape[0]
    total = signal * kernel[taps - 1 : taps]
    for shift in range(1, taps):
        moved = pltpu.roll(signal, shift, 0) * kept[shift - 1]
        total = total + moved * kernel[taps - 1 - shift : taps - shift]
    return total


def single(left, right):
    return lax.dot_general(
        left.astype(LOW),
        right.astype(LOW),
        (((1,), (0,)), ((), ())),
        preferred_element_type=WIDE,
    )


def invert(lowers, rows, cols):
    length = lowers[0].shape[0]
    eye = (rows == cols).astype(WIDE)
    pair = (rows // 2) == (cols // 2)
    inverses = [eye - jnp.where(pair, lower, 0.0) for lower in lowers]
    size = 2
    while size < length:
        cross = ((rows // (2 * size)) == (cols // (2 * size))) & ((rows // size) != (cols // size))
        steps = [
            single(inverse, jnp.where(cross, lower, 0.0))
            for inverse, lower in zip(inverses, lowers)
        ]
        inverses = [
            inverse - single(step, inverse) for step, inverse in zip(steps, inverses)
        ]
        size *= 2
    rests = [
        eye - inverse - product(halves(lower), halves(inverse), 1, 0)
        for inverse, lower in zip(inverses, lowers)
    ]
    return [inverse + single(inverse, rest) for inverse, rest in zip(inverses, rests)]


def forward_heads(signals, beta_in, conv, kept, masks, gain):
    rows, cols, strict, inclusive = masks
    taps = conv[0].shape[0] // 3
    lowers, held = [], []
    for head in range(len(signals)):
        convolved = []
        for part in range(3):
            kernel = conv[head][part * taps : (part + 1) * taps]
            pre = convolve(signals[head][part], kernel, kept)
            convolved.append(pre * sigmoid(pre))
        query = convolved[0] * (
            lax.rsqrt(jnp.sum(convolved[0] * convolved[0], 1, keepdims=True) + 1e-06) * HEAD**-0.5
        )
        key = convolved[1] * lax.rsqrt(
            jnp.sum(convolved[1] * convolved[1], 1, keepdims=True) + 1e-06
        )
        beta = sigmoid(beta_in[head])
        key_parts = halves(key)
        gram = product(key_parts, key_parts, 1, 1)
        lowers.append(jnp.where(strict, gram * beta, 0.0))
        scores = jnp.where(inclusive, product(halves(query), key_parts, 1, 1), 0.0)
        held.append((halves(scores), halves(convolved[2] * beta)))
    out = []
    for head, inverse in enumerate(invert(lowers, rows, cols)):
        scores, target = held[head]
        update = product(halves(inverse), target, 1, 0)
        mixed = product(scores, halves(update), 1, 0)
        scale = lax.rsqrt(jnp.sum(mixed * mixed, 1, keepdims=True) * (1.0 / HEAD) + 1e-05)
        gate = signals[head][3]
        gated = (mixed * scale * gain * (gate * sigmoid(gate))).astype(LOW)
        out.append((gated, inverse, update, mixed))
    return out


def backward_head(signals, beta_in, conv, kept, masks, gain, inverse, update, mixed, grad):
    rows, cols, strict, inclusive = masks
    length = grad.shape[0]
    taps = conv.shape[0] // 3
    before, gates, convolved = [], [], []
    for part in range(3):
        pre = convolve(signals[part], conv[part * taps : (part + 1) * taps], kept)
        before.append(pre)
        gates.append(sigmoid(pre))
        convolved.append(pre * gates[part])
    query_unit = lax.rsqrt(jnp.sum(convolved[0] * convolved[0], 1, keepdims=True) + 1e-06)
    key_unit = lax.rsqrt(jnp.sum(convolved[1] * convolved[1], 1, keepdims=True) + 1e-06)
    query = convolved[0] * (query_unit * HEAD**-0.5)
    key = convolved[1] * key_unit
    beta = sigmoid(beta_in)
    gate = signals[3]
    gate_sigma = sigmoid(gate)
    opened = gate * gate_sigma
    scale = lax.rsqrt(jnp.sum(mixed * mixed, 1, keepdims=True) * (1.0 / HEAD) + 1e-05)
    normed = mixed * scale
    head_grad = jnp.sum(grad * opened * normed, 0, keepdims=True)
    inner = grad * opened * gain
    mixed_grad = scale * inner - mixed * (
        scale * scale * scale * (jnp.sum(inner * mixed, 1, keepdims=True) * (1.0 / HEAD))
    )
    gate_grad = grad * normed * gain * gate_sigma * (1.0 + gate * (1.0 - gate_sigma))
    key_parts = halves(key)
    query_parts = halves(query)
    update_parts = halves(update)
    mixed_parts = halves(mixed_grad)
    gram = product(key_parts, key_parts, 1, 1)
    scores = jnp.where(inclusive, product(query_parts, key_parts, 1, 1), 0.0)
    scores_grad = halves(jnp.where(inclusive, product(mixed_parts, update_parts, 1, 1), 0.0))
    update_grad = product(halves(scores), mixed_parts, 0, 0)
    solved = product(halves(inverse), halves(update_grad), 0, 0)
    system_grad = jnp.where(strict, -product(halves(solved), update_parts, 1, 1), 0.0)
    gram_grad = halves(system_grad * beta)
    query_grad = product(scores_grad, key_parts, 1, 0)
    key_grad = (
        product(scores_grad, query_parts, 0, 0)
        + product(gram_grad, key_parts, 1, 0)
        + product(gram_grad, key_parts, 0, 0)
    )
    beta_grad = jnp.sum(system_grad * gram, 1, keepdims=True) + jnp.sum(
        solved * convolved[2], 1, keepdims=True
    )
    beta_grad = beta_grad * beta * (1.0 - beta)
    conv_grads = [
        HEAD**-0.5
        * (
            query_grad * query_unit
            - convolved[0]
            * (
                query_unit
                * query_unit
                * query_unit
                * jnp.sum(convolved[0] * query_grad, 1, keepdims=True)
            )
        ),
        key_grad * key_unit
        - convolved[1]
        * (key_unit * key_unit * key_unit * jnp.sum(convolved[1] * key_grad, 1, keepdims=True)),
        solved * beta,
    ]
    lines = [None] * (3 * taps)
    signal_grads = []
    for part in range(3):
        sigma = gates[part]
        error = conv_grads[part] * sigma * (1.0 + before[part] * (1.0 - sigma))
        kernel = conv[part * taps : (part + 1) * taps]
        total = error * kernel[taps - 1 : taps]
        last = part * taps + taps - 1
        lines[last] = jnp.sum(error * signals[part], 0, keepdims=True)
        for shift in range(1, taps):
            held = error * kept[shift - 1]
            lines[last - shift] = jnp.sum(
                held * pltpu.roll(signals[part], shift, 0), 0, keepdims=True
            )
            total = total + pltpu.roll(held, length - shift, 0) * (
                kernel[taps - 1 - shift : taps - shift]
            )
        signal_grads.append(total.astype(LOW))
    signal_grads.append(gate_grad.astype(LOW))
    return signal_grads, beta_grad, lines, head_grad


def head_lanes(head):
    return slice(head * HEAD, (head + 1) * HEAD)


def mixer_forward_kernel(*refs):
    parts = refs[:2]
    beta_ref, col_ref, row_ref, conv_ref, head_ref = refs[2:7]
    gated_ref, inverse_ref, update_ref, mixed_ref = refs[7:]
    masks = masks_of(col_ref[...], row_ref[0])
    kept = kept_of(col_ref[...], conv_ref.shape[0] // 3)
    results = forward_heads(
        [[parts[head][:, head_lanes(part)] for part in range(4)] for head in range(2)],
        [beta_ref[:, head : head + 1] for head in range(2)],
        [conv_ref[:, head_lanes(head)] for head in range(2)],
        kept,
        masks,
        head_ref[...],
    )
    for head, result in enumerate(results):
        own = head_lanes(head)
        gated_ref[:, own], inverse_ref[0, head], update_ref[:, own], mixed_ref[:, own] = result


def mixer_backward_kernel(*refs):
    parts = refs[:2]
    beta_ref, col_ref, row_ref, conv_ref, head_ref = refs[2:7]
    inverse_ref, update_ref, mixed_ref, grad_ref = refs[7:11]
    out_ref, beta_grad_ref, conv_grad_ref, head_grad_ref = refs[11:]
    masks = masks_of(col_ref[...], row_ref[0])
    kept = kept_of(col_ref[...], conv_ref.shape[0] // 3)
    head_grad = jnp.zeros((1, HEAD), WIDE)
    for head in range(2):
        own = head_lanes(head)
        grads, beta_grad, lines, gain_grad = backward_head(
            [parts[head][:, head_lanes(part)] for part in range(4)],
            beta_ref[:, head : head + 1],
            conv_ref[:, own],
            kept,
            masks,
            head_ref[...],
            inverse_ref[0, head],
            update_ref[:, own],
            mixed_ref[:, own],
            grad_ref[:, own],
        )
        head_grad = head_grad + gain_grad
        beta_grad_ref[:, head : head + 1] = beta_grad
        for line, values in enumerate(lines):
            conv_grad_ref[0, line : line + 1, own] = values
        for part in range(4):
            out_ref[:, head_lanes(4 * head + part)] = grads[part]
    head_grad_ref[0] = head_grad


def mixer_specs(length, lines):
    part = pl.BlockSpec((length, 4 * HEAD), lambda i: (i, 0))
    return [
        part,
        part,
        pl.BlockSpec((length, 2), lambda i: (i, 0)),
        pl.BlockSpec((length, 1), lambda i: (i, 0)),
        pl.BlockSpec((1, 1, length), lambda i: (i, 0, 0)),
        pl.BlockSpec((lines, 2 * HEAD), lambda i: (0, 0)),
        pl.BlockSpec((1, HEAD), lambda i: (0, 0)),
    ]


def saved_specs(length):
    return [
        pl.BlockSpec((1, 2, length, length), lambda i: (i, 0, 0, 0)),
        pl.BlockSpec((length, 2 * HEAD), lambda i: (i, 0)),
        pl.BlockSpec((length, 2 * HEAD), lambda i: (i, 0)),
    ]


def saved_shapes(count, length):
    return [
        jax.ShapeDtypeStruct((count, 2, length, length), WIDE),
        jax.ShapeDtypeStruct((count * length, 2 * HEAD), WIDE),
        jax.ShapeDtypeStruct((count * length, 2 * HEAD), WIDE),
    ]


def grad_specs(length, lines):
    return [
        pl.BlockSpec((length, 8 * HEAD), lambda i: (i, 0)),
        pl.BlockSpec((length, 2), lambda i: (i, 0)),
        pl.BlockSpec((1, lines, 2 * HEAD), lambda i: (i, 0, 0)),
        pl.BlockSpec((1, 1, HEAD), lambda i: (i, 0, 0)),
    ]


def grad_shapes(count, length, lines):
    return [
        jax.ShapeDtypeStruct((count * length, 8 * HEAD), LOW),
        jax.ShapeDtypeStruct((count * length, 2), WIDE),
        jax.ShapeDtypeStruct((count, lines, 2 * HEAD), WIDE),
        jax.ShapeDtypeStruct((count, 1, HEAD), WIDE),
    ]


def mixer_forward(inputs):
    count, _, length = inputs[4].shape
    return pl.pallas_call(
        mixer_forward_kernel,
        grid=(count,),
        in_specs=mixer_specs(length, inputs[5].shape[0]),
        out_specs=[pl.BlockSpec((length, 2 * HEAD), lambda i: (i, 0))] + saved_specs(length),
        out_shape=[jax.ShapeDtypeStruct((count * length, 2 * HEAD), LOW)]
        + saved_shapes(count, length),
        compiler_params=pltpu.CompilerParams(vmem_limit_bytes=32 << 20),
        name="mixer_forward",
    )(*inputs)


def mixer_backward(inputs, saved, grad):
    count, _, length = inputs[4].shape
    lines = inputs[5].shape[0]
    return pl.pallas_call(
        mixer_backward_kernel,
        grid=(count,),
        in_specs=mixer_specs(length, lines)
        + saved_specs(length)
        + [pl.BlockSpec((length, 2 * HEAD), lambda i: (i, 0))],
        out_specs=grad_specs(length, lines),
        out_shape=grad_shapes(count, length, lines),
        compiler_params=pltpu.CompilerParams(vmem_limit_bytes=32 << 20),
        name="mixer_backward",
    )(*inputs, *saved, grad)


def beside(refs, rows, lanes=slice(None)):
    return jnp.concatenate(
        [ref[z, c, rows, lanes] for ref in refs for z in range(ref.shape[0]) for c in range(2)], 1
    )


def atop(refs, lanes):
    return jnp.concatenate(
        [ref[z, c, :, lanes] for ref in refs for z in range(ref.shape[0]) for c in range(2)], 0
    )


def both(weight_refs, far, rows, lanes=slice(None)):
    return jnp.concatenate([beside(weight_refs[i][far], rows, lanes) for i in range(2)], 0)


def turned(left, right):
    return lax.dot_general(
        left, right, (((0,), (0,)), ((), ())), preferred_element_type=WIDE
    )


def straight(left, right):
    return lax.dot_general(
        left, right, (((1,), (0,)), ((), ())), preferred_element_type=WIDE
    )


def crossed(left, right):
    return lax.dot_general(
        left, right, (((1,), (1,)), ((), ())), preferred_element_type=WIDE
    )


def collect(token_refs, hold_ref):
    for step in range(2):

        @pl.when(pl.program_id(0) == step)
        def _():
            hold_ref[...] = token_refs[step][...]


def deal(pair_refs, values, lanes):
    for step in range(2):

        @pl.when(pl.program_id(0) == step)
        def _():
            pair_refs[step][:, lanes] = values.astype(LOW)


def whole(values):
    rank = len(values.shape)
    return pl.BlockSpec(values.shape, lambda i: (0,) * rank)


def split_refs(refs, sizes):
    out, start = [], 0
    for size in sizes:
        out.append(refs[start : start + size])
        start += size
    return out


def flat(grid):
    return [item for pair in grid for items in pair for item in items]


def nested(refs, grid):
    lists = split_refs(refs, [len(items) for pair in grid for items in pair])
    return [lists[:2], lists[2:]]


def call(kernel, inputs, in_specs, out_specs, out_shape, scratch, name, grid=2, work=6):
    return pl.pallas_call(
        kernel,
        grid=(grid,),
        in_specs=in_specs,
        out_specs=out_specs,
        out_shape=out_shape,
        scratch_shapes=scratch,
        compiler_params=pltpu.CompilerParams(vmem_limit_bytes=44 << 20),
        cost_estimate=pl.CostEstimate(
            flops=work * 10**9, bytes_accessed=8 << 20, transcendentals=0
        ),
        name=name,
    )(*inputs)


QKVG = slice(0, 4 * HEAD)
OUT = slice(4 * HEAD, 5 * HEAD)


def column_forward(tokens, weights, gain, beta_weights, seg_col, seg_row, conv, head_gain):
    count, _, length = seg_row.shape
    width = tokens[0].shape[1]
    half = width // 2
    span = [slice(0, half), slice(half, width)]
    pieces = flat(weights)

    def kernel(*refs):
        token_refs, weight_refs, rest = split_refs(refs, [2, len(pieces), 17])
        gain_ref, beta_ref, col_ref, row_ref, conv_ref, head_ref = rest[:6]
        gated_ref, inverse_ref, update_ref, mixed_ref = rest[6:10]
        mixer_ref, first_ref, second_ref, beta_in_ref = rest[10:14]
        pair_refs, hold_ref = rest[14:16], rest[16]
        weight_refs = nested(weight_refs, weights)
        collect(token_refs, hold_ref)
        values = hold_ref[...].astype(WIDE)
        scale = lax.rsqrt(jnp.sum(values * values, 1, keepdims=True) * (1.0 / D) + 1e-06)
        mixer_ref[...] = (values * scale * gain_ref[...]).astype(LOW)
        masks = masks_of(col_ref[...], row_ref[0])
        kept = kept_of(col_ref[...], conv_ref.shape[0] // 3)
        mixer_in = mixer_ref[...].astype(WIDE)
        beta_in = []
        for head, projected_ref in enumerate((first_ref, second_ref)):
            projected_ref[...] = sum(
                straight(mixer_ref[:, span[far]], atop(weight_refs[head][far], QKVG))
                for far in range(2)
            )
            beta_in.append(
                jnp.sum(mixer_in * beta_ref[head : head + 1, :].astype(WIDE), 1, keepdims=True)
            )
            beta_in_ref[:, head : head + 1] = beta_in[head]
        results = forward_heads(
            [
                [ref[:, head_lanes(part)] for part in range(4)]
                for ref in (first_ref, second_ref)
            ],
            beta_in,
            [conv_ref[:, head_lanes(head)] for head in range(2)],
            kept,
            masks,
            head_ref[...],
        )
        for head, result in enumerate(results):
            own = head_lanes(head)
            gated_ref[:, own], inverse_ref[0, head], update_ref[:, own], mixed_ref[:, own] = result
        for far in range(2):
            branch = straight(gated_ref[...], both(weight_refs, far, slice(None), OUT))
            deal(pair_refs, branch, span[far])

    inputs = list(tokens) + pieces + [gain, beta_weights, seg_col, seg_row, conv, head_gain]
    in_specs = [whole(item) for item in inputs]
    in_specs[-4] = pl.BlockSpec((length, 1), lambda i: (i, 0))
    in_specs[-3] = pl.BlockSpec((1, 1, length), lambda i: (i, 0, 0))
    step = lambda lanes: pl.BlockSpec((length, lanes), lambda i: (i, 0))
    shape = lambda lanes, kind: jax.ShapeDtypeStruct((count * length, lanes), kind)
    out = jax.ShapeDtypeStruct((length, width), LOW)
    return call(
        kernel,
        inputs,
        in_specs,
        [step(2 * HEAD)]
        + saved_specs(length)
        + [step(width), step(4 * HEAD), step(4 * HEAD), step(2)]
        + [whole(out)] * 2,
        [shape(2 * HEAD, LOW)]
        + saved_shapes(count, length)
        + [shape(width, LOW), shape(4 * HEAD, WIDE), shape(4 * HEAD, WIDE), shape(2, WIDE)]
        + [out] * 2,
        [pltpu.VMEM((length, width), LOW)],
        "column_forward",
    )


def ffn_rows_of(hidden):
    return [slice(n * hidden, (n + 1) * hidden) for n in range(3)]


def column_ffn(tokens, ways, scales, weights, hidden):
    length, width = tokens[0].shape
    half = width // 2
    span = [slice(0, half), slice(half, width)]
    pieces = flat(weights)
    gate_rows, up_rows, down_rows = ffn_rows_of(hidden)

    def kernel(*refs):
        token_refs, way_refs, (scale_ref,), weight_refs, rest = split_refs(
            refs, [2, 2, 1, len(pieces), 7]
        )
        weight_refs = nested(weight_refs, weights)
        pair_refs, token_ref, way_ref = rest[:2], rest[2], rest[3]
        active_ref, gate_ref, up_ref = rest[4:]
        collect(token_refs, token_ref)
        collect(way_refs, way_ref)
        way_ref[...] = (way_ref[...].astype(WIDE) * scale_ref[...]).astype(LOW)
        gate, upward = (
            sum(crossed(token_ref[:, span[far]], both(weight_refs, far, rows)) for far in range(2))
            for rows in (gate_rows, up_rows)
        )
        sigma = sigmoid(gate)
        opened = gate * sigma
        active_ref[...] = (opened * upward).astype(LOW)
        grad = sum(
            crossed(way_ref[:, span[far]], both(weight_refs, far, down_rows)) for far in range(2)
        )
        gate_ref[...] = (grad * upward * sigma * (1.0 + gate * (1.0 - sigma))).astype(LOW)
        up_ref[...] = (grad * opened).astype(LOW)
        for far in range(2):
            values = straight(gate_ref[...], both(weight_refs, far, gate_rows)) + straight(
                up_ref[...], both(weight_refs, far, up_rows)
            )
            deal(pair_refs, values, span[far])

    inputs = list(tokens) + list(ways) + [scales] + pieces
    in_specs = [whole(item) for item in inputs]
    in_specs[4] = pl.BlockSpec((length, 1), lambda i: (i, 0))
    out = jax.ShapeDtypeStruct((length, width), LOW)
    step = lambda lanes: pl.BlockSpec((length, lanes), lambda i: (i, 0))
    shape = lambda lanes: jax.ShapeDtypeStruct((2 * length, lanes), LOW)
    return call(
        kernel,
        inputs,
        in_specs,
        [whole(out)] * 2 + [step(width)] * 2 + [step(2 * hidden)] * 3,
        [out] * 2 + [shape(width)] * 2 + [shape(2 * hidden)] * 3,
        [],
        "column_ffn",
    )


def write_beside(ref, rows, lanes, values):
    size = ref.shape[0]
    strip = values.shape[1] // (2 * size)
    for z in range(size):
        for c in range(2):
            start = (2 * z + c) * strip
            ref[z, c, rows, lanes] = values[:, start : start + strip].astype(LOW)


def column_ffn_grads(active, gate_grad, up_grad, tokens, ways, weights, grad):
    hidden = active.shape[1] // 2
    count, width = ways.shape
    length, half = count // 2, width // 2
    pieces = flat(weights)
    rows = ffn_rows_of(hidden)

    def kernel(active_ref, gate_ref, up_ref, token_ref, way_ref, *refs):
        weight_refs = nested(refs[: len(pieces)], weights)
        near_ref, far_ref, *out = refs[len(pieces) :]
        for far in range(2):
            lanes = slice(far * half, (far + 1) * half)
            values = straight(active_ref[...], both(weight_refs, far, rows[2])).astype(LOW)
            near_ref[:, lanes] = values[:length]
            far_ref[:, lanes] = values[length:]
            for n, left_ref, right_ref in (
                (0, gate_ref, token_ref), (1, up_ref, token_ref), (2, active_ref, way_ref)
            ):
                values = turned(left_ref[...], right_ref[:, lanes])
                for i in range(2):
                    write_beside(
                        out[2 * i + far],
                        rows[n],
                        slice(None),
                        values[i * hidden : (i + 1) * hidden],
                    )

    inputs = [active, gate_grad, up_grad, tokens, ways] + pieces
    out = jax.ShapeDtypeStruct((length, width), LOW)
    near, far, *grads = call(
        kernel,
        inputs,
        [whole(item) for item in inputs],
        [whole(out)] * 2 + [whole(grad)] * 4,
        [out] * 2 + [grad] * 4,
        [],
        "column_ffn_grads",
        grid=1,
        work=10,
    )
    return near, far, [grads[:2], grads[2:]]


def column_backward(
    grads, weights, beta_weights, seg_col, seg_row, conv, head_gain, saved, projected, beta_in
):
    count, _, length = seg_row.shape
    lines = conv.shape[0]
    width = grads[0].shape[1]
    half = width // 2
    span = [slice(0, half), slice(half, width)]
    pieces = flat(weights)

    def kernel(*refs):
        token_refs, weight_refs, rest = split_refs(refs, [2, len(pieces), 18])
        weight_refs = nested(weight_refs, weights)
        beta_ref, col_ref, row_ref, conv_ref, head_ref = rest[:5]
        inverse_ref, update_ref, mixed_ref, first_ref, second_ref, beta_in_ref = rest[5:11]
        signal_ref, beta_grad_ref, conv_grad_ref, head_grad_ref = rest[11:15]
        pair_refs, hold_ref = rest[15:17], rest[17]
        collect(token_refs, hold_ref)
        masks = masks_of(col_ref[...], row_ref[0])
        kept = kept_of(col_ref[...], conv_ref.shape[0] // 3)
        head_grad = jnp.zeros((1, HEAD), WIDE)
        beta_grads = []
        grad = sum(
            crossed(hold_ref[:, span[far]], both(weight_refs, far, slice(None), OUT))
            for far in range(2)
        )
        for head, projected_ref in enumerate((first_ref, second_ref)):
            own = head_lanes(head)
            signal_grads, beta_grad, conv_lines, gain_grad = backward_head(
                [projected_ref[:, head_lanes(part)] for part in range(4)],
                beta_in_ref[:, head : head + 1],
                conv_ref[:, own],
                kept,
                masks,
                head_ref[...],
                inverse_ref[0, head],
                update_ref[:, own],
                mixed_ref[:, own],
                grad[:, own],
            )
            head_grad = head_grad + gain_grad
            beta_grads.append(beta_grad.astype(LOW).astype(WIDE))
            beta_grad_ref[:, head : head + 1] = beta_grad
            for line, values in enumerate(conv_lines):
                conv_grad_ref[0, line : line + 1, own] = values
            for part in range(4):
                signal_ref[:, head_lanes(4 * head + part)] = signal_grads[part]
        head_grad_ref[0] = head_grad
        for far in range(2):
            values = sum(
                crossed(
                    signal_ref[:, 4 * HEAD * head : 4 * HEAD * (head + 1)],
                    atop(weight_refs[head][far], QKVG),
                )
                + beta_grads[head] * beta_ref[head : head + 1, span[far]].astype(WIDE)
                for head in range(2)
            )
            deal(pair_refs, values, span[far])

    inputs = (
        list(grads)
        + pieces
        + [beta_weights, seg_col, seg_row, conv, head_gain]
        + list(saved)
        + list(projected)
        + [beta_in]
    )
    in_specs = [whole(item) for item in inputs]
    step = lambda lanes: pl.BlockSpec((length, lanes), lambda i: (i, 0))
    in_specs[-10] = step(1)
    in_specs[-9] = pl.BlockSpec((1, 1, length), lambda i: (i, 0, 0))
    in_specs[-6:] = saved_specs(length) + [step(4 * HEAD), step(4 * HEAD), step(2)]
    out = jax.ShapeDtypeStruct((length, width), LOW)
    return call(
        kernel,
        inputs,
        in_specs,
        grad_specs(length, lines) + [whole(out)] * 2 + [step(width)],
        grad_shapes(count, length, lines)
        + [out] * 2
        + [jax.ShapeDtypeStruct((count * length, width), LOW)],
        [],
        "column_backward",
    )


def column_mixer_grads(mixer_in, signal_grads, gated, ways, grad):
    half = mixer_in.shape[1] // 2
    strip = grad.shape[2]

    def kernel(mixer_ref, signal_ref, gated_ref, way_ref, *grad_refs):
        for far in range(2):
            lanes = slice(far * half, (far + 1) * half)
            outs = turned(gated_ref[...], way_ref[:, lanes])
            for head in range(2):
                ref = grad_refs[2 * head + far]
                values = turned(
                    mixer_ref[:, lanes], signal_ref[:, 4 * HEAD * head : 4 * HEAD * (head + 1)]
                ).astype(LOW)
                for z in range(ref.shape[0]):
                    for c in range(2):
                        start = (2 * z + c) * strip
                        ref[z, c, :, QKVG] = values[start : start + strip]
                write_beside(ref, slice(None), OUT, outs[head_lanes(head)])

    inputs = [mixer_in, signal_grads, gated, ways]
    grads = call(
        kernel,
        inputs,
        [whole(item) for item in inputs],
        [whole(grad)] * 4,
        [grad] * 4,
        [],
        "column_mixer_grads",
        grid=1,
    )
    return [grads[:2], grads[2:]]


def contract(left, right, left_dim, right_dim):
    return lax.dot_general(
        left, right, (((left_dim,), (right_dim,)), ((), ())), preferred_element_type=WIDE
    )


def after(values, earlier):
    return lax.optimization_barrier((values, earlier))[0]


def exclusive_order(blocks):
    place = lax.axis_index("dmod")
    for bit in (1, 2):
        flip = (place & bit) != 0
        blocks = [jnp.where(flip, blocks[i ^ bit], blocks[i]) for i in range(4)]
    return blocks


def trade(blocks):
    return [blocks[0]] + [
        lax.ppermute(blocks[m], "dmod", [(i, i ^ m) for i in range(4)]) for m in (1, 2, 3)
    ]


def gather_width(values):
    far = lax.ppermute(values, "dmod", ACROSS)
    near = lax.ppermute(values, "dmod", CORE)
    return [values, near, far, lax.ppermute(far, "dmod", CORE)]


def scatter_width(blocks):
    near = lax.ppermute(blocks[1].astype(LOW), "dmod", CORE)
    cross = lax.ppermute(blocks[3].astype(LOW), "dmod", CORE)
    far = lax.ppermute((blocks[2] + cross.astype(WIDE)).astype(LOW), "dmod", ACROSS)
    return blocks[0] + near.astype(WIDE) + far.astype(WIDE)


def sum_pair(values):
    low = values.astype(LOW)
    return low.astype(WIDE) + lax.ppermute(low, "mp", SWAP).astype(WIDE)


def row_total(values):
    return lax.psum(values, "dmod")


class Ring:
    def __init__(self):
        self.size = lax.axis_size("dp")
        self.parts = 1

    def order(self, values):
        return values

    def gather(self, values):
        return [lax.all_gather(values, "dp", axis=1, tiled=True)]

    def scatter(self, make):
        return lax.psum_scatter(
            make(0).astype(LOW), "dp", scatter_dimension=1, tiled=True
        ).astype(WIDE)


def plane_body(
    block_input,
    segment_ids,
    group_ids,
    group_weight,
    mixer_norm,
    w_mix,
    w_beta,
    conv_kernel,
    head_norm,
    w_out,
    ffn_norm,
    w_ffn_in,
    w_ffn_down,
    cotangent,
):
    ring = Ring()
    parts = ring.parts
    micro, seqs, length, width = block_input.shape
    tokens = micro * seqs * length
    block = width // parts
    strip = w_mix.shape[0]
    span = w_mix.shape[2] // 4
    hidden = w_ffn_in.shape[2] // 4
    dmod = lax.axis_index("dmod")
    data_size = ring.size
    place = lax.axis_index("dp")

    lines = conv_kernel.shape[0] * conv_kernel.shape[1]
    pack = jnp.concatenate(
        [
            conv_kernel.reshape(-1),
            head_norm,
            mixer_norm,
            ffn_norm,
            w_beta.T.reshape(-1),
        ]
    )
    packs = lax.all_gather(pack, "dp", axis=0)
    sizes = [conv_kernel.size, head_norm.size, strip, strip, w_beta.size]
    cuts = [sum(sizes[:i]) for i in range(6)]
    conv = (
        packs[:, cuts[0] : cuts[1]]
        .reshape(data_size, lines, -1)
        .transpose(1, 0, 2)
        .reshape(lines, span)
        .astype(WIDE)
    )
    head_gain = packs[:, cuts[1] : cuts[2]].reshape(1, -1).astype(WIDE)
    gain_one = ring.order(packs[:, cuts[2] : cuts[3]].reshape(1, -1).astype(WIDE))
    gain_two = ring.order(packs[:, cuts[3] : cuts[4]].reshape(1, -1).astype(WIDE))
    beta_weights = ring.order(
        packs[:, cuts[4] : cuts[5]]
        .reshape(data_size, -1, strip)
        .transpose(1, 0, 2)
        .reshape(-1, width)
    )

    out_rows = jnp.concatenate(exclusive_order(jnp.split(w_out, 4, axis=0)), 0)
    out_halves = jnp.split(out_rows.T, 2, axis=1)
    mix_own = jnp.stack(trade(exclusive_order(jnp.split(w_mix, 4, axis=2))))
    mix_halves = [
        mix_own[:, :, :, head * HEAD : (head + 1) * HEAD].reshape(4, strip, 4 * HEAD)
        for head in (0, 1)
    ]
    ffn_own = jnp.stack(trade(exclusive_order(jnp.split(w_ffn_in, 4, axis=2))))
    ffn_halves = [ffn_own[:, :, 0], ffn_own[:, :, 1]]
    down_own = trade(exclusive_order(jnp.split(w_ffn_down, 4, axis=0)))
    down_halves = [
        jnp.stack([down_own[0].T, down_own[1].T]),
        jnp.stack([down_own[2].T, down_own[3].T]),
    ]

    def chain(half):
        first = ring.gather(out_halves[half][None])
        second = ring.gather(after(mix_halves[half], first[-1]))
        third = ring.gather(after(ffn_halves[half], second[-1]))
        fourth = ring.gather(after(down_halves[half], third[-1]))
        return first, second, third, fourth

    chains = [chain(0), chain(1)]
    out_weights = jnp.concatenate(
        [
            jnp.concatenate([part[0] for part in chains[0][0]], 0),
            jnp.concatenate([part[0] for part in chains[1][0]], 0),
        ],
        1,
    )
    mix_parts = [[part.reshape(4 * block, -1) for part in each[1]] for each in chains]
    ffn_parts = [[part.reshape(4 * block, -1) for part in each[2]] for each in chains]
    down_parts = [[part.reshape(2 * block, -1) for part in each[3]] for each in chains]

    marks = (group_ids.reshape(tokens, 1) == jnp.arange(group_weight.shape[0])[None]).astype(WIDE)
    counts = lax.psum(jnp.sum(marks, 0), "dp")
    table = group_weight * (tokens * data_size / group_weight.shape[0]) / counts
    scales = jnp.sum(marks * table, -1, keepdims=True)
    direction = ring.order(cotangent.reshape(tokens, width).astype(WIDE)) * scales
    direction_low = direction.astype(LOW)

    def by_part(slots):
        return [
            jnp.concatenate([slot[:, k * block : (k + 1) * block] for slot in slots], 1)
            for k in range(parts)
        ]

    def by_slot(pieces):
        return [
            jnp.concatenate([piece[:, m * block : (m + 1) * block] for piece in pieces], 1)
            for m in range(pieces[0].shape[1] // block)
        ]

    direction_parts = by_part(gather_width(direction_low))

    rows = ring.order(block_input.reshape(tokens, width).astype(WIDE))
    first_scale = lax.rsqrt(row_total(jnp.sum(rows * rows, -1, keepdims=True)) / D + 1e-06)
    mixer_in = (rows * first_scale * gain_one).astype(LOW)
    mixer_parts = by_part(gather_width(mixer_in))
    projected = [
        sum(jnp.dot(mixer_parts[k], mix_parts[half][k], preferred_element_type=WIDE) for k in range(parts))
        for half in (0, 1)
    ]
    beta_all = row_total(contract(beta_weights, mixer_in, 1, 1))
    heads = span // HEAD
    beta_in = lax.dynamic_slice_in_dim(beta_all, dmod * heads, heads, 0).T
    seg_col = segment_ids.reshape(tokens, 1)
    seg_row = segment_ids.reshape(micro * seqs, 1, length)
    mixer_args = list(projected) + [
        beta_in, seg_col, seg_row, conv, head_gain
    ]
    gated, *saved = mixer_forward(mixer_args)
    gated_all = jnp.concatenate(gather_width(gated), 1)
    middle = rows + sum_pair(contract(gated_all, out_weights, 1, 1))

    second_scale = lax.rsqrt(row_total(jnp.sum(middle * middle, -1, keepdims=True)) / D + 1e-06)
    ffn_in = (middle * second_scale * gain_two).astype(LOW)
    ffn_in_parts = by_part(gather_width(ffn_in))
    gate, upward = (
        sum(jnp.dot(ffn_in_parts[k], ffn_parts[half][k], preferred_element_type=WIDE) for k in range(parts))
        for half in (0, 1)
    )
    sigma = sigmoid(gate)
    active = (gate * sigma * upward).astype(LOW)
    down_slots = sum(
        (
            by_slot([contract(active, down_parts[half][k], 1, 1) for k in range(parts)])
            for half in (0, 1)
        ),
        [],
    )
    result = middle + sum_pair(scatter_width(down_slots))
    out = ring.order(result).astype(LOW).reshape(block_input.shape)

    down_grads = [
        ring.scatter(
            lambda k: contract(
                direction_parts[k][:, 2 * half * block : 2 * (half + 1) * block], active, 0, 0
            ).reshape(2, block, hidden)
        )
        for half in (0, 1)
    ]
    active_grad = sum(
        jnp.dot(
            direction_parts[k][:, 2 * half * block : 2 * (half + 1) * block],
            down_parts[half][k],
            preferred_element_type=WIDE,
        )
        for k in range(parts)
        for half in (0, 1)
    )
    gate_grad = (active_grad * upward * sigma * (1.0 + gate * (1.0 - sigma))).astype(LOW)
    upward_grad = (active_grad * gate * sigma).astype(LOW)
    ffn_slots = by_slot(
        [
            contract(gate_grad, ffn_parts[0][k], 1, 1) + contract(upward_grad, ffn_parts[1][k], 1, 1)
            for k in range(parts)
        ]
    )
    ffn_grads = [
        ring.scatter(lambda k: contract(ffn_in_parts[k], grad, 0, 0).reshape(4, block, hidden))
        for grad in (gate_grad, upward_grad)
    ]
    ffn_in_grad = sum_pair(scatter_width(ffn_slots))
    weighted_two = ffn_in_grad * gain_two
    norm_two_grad = jnp.sum(ffn_in_grad * middle * second_scale, 0)
    inner_two = row_total(jnp.sum(weighted_two * middle, -1, keepdims=True))
    middle_grad = (
        direction + second_scale * weighted_two - middle * (second_scale**3 * inner_two / D)
    )

    branch_low = middle_grad.astype(LOW)
    out_grads = [
        ring.scatter(
            lambda k: contract(
                branch_low[:, k * block : (k + 1) * block],
                gated_all[:, 2 * half * span : 2 * (half + 1) * span],
                0,
                0,
            )[None]
        )
        for half in (0, 1)
    ]
    gated_slots = jnp.split(jnp.dot(branch_low, out_weights, preferred_element_type=WIDE), 4, axis=1)
    gated_grad = scatter_width(gated_slots)
    projected_grad, beta_grad, conv_grad, head_grad = mixer_backward(
        mixer_args, saved, gated_grad
    )
    projected_slots = gather_width(projected_grad)
    mix_grads = [
        ring.scatter(
            lambda k: contract(
                mixer_in[:, k * block : (k + 1) * block],
                jnp.concatenate(projected_slots[2 * half : 2 * half + 2], 1),
                0,
                0,
            )[None]
        )
        for half in (0, 1)
    ]
    beta_slots = jnp.concatenate(
        exclusive_order(gather_width(beta_grad.T.astype(LOW))), 0
    )
    beta_weight_grad = contract(beta_slots, mixer_in, 1, 0)
    mixer_slots = by_slot(
        [
            contract(projected_grad[:, : 2 * span], mix_parts[0][k], 1, 1)
            + contract(projected_grad[:, 2 * span :], mix_parts[1][k], 1, 1)
            for k in range(parts)
        ]
    )
    mixer_grad = sum_pair(scatter_width(mixer_slots) + contract(beta_slots, beta_weights, 0, 0))
    weighted_one = mixer_grad * gain_one
    norm_one_grad = jnp.sum(mixer_grad * rows * first_scale, 0)
    inner_one = row_total(jnp.sum(weighted_one * rows, -1, keepdims=True))
    grad_input = ring.order(
        middle_grad + first_scale * weighted_one - rows * (first_scale**3 * inner_one / D)
    ).reshape(block_input.shape)

    head_total = lax.psum(jnp.sum(head_grad, (0, 1)), ("dp", "mp", "dmod"))
    head_out = lax.dynamic_slice_in_dim(head_total, place * head_norm.size, head_norm.size, 0)
    small = jnp.concatenate(
        [
            jnp.sum(conv_grad, 0),
            ring.order(jnp.stack([norm_one_grad, norm_two_grad]))
            .reshape(2, data_size, -1)
            .transpose(1, 0, 2)
            .reshape(data_size, -1)
            .reshape(-1)
            .reshape(-1, span),
            ring.order(beta_weight_grad)
            .reshape(-1, data_size, strip)
            .transpose(1, 0, 2)
            .reshape(-1, span),
        ],
        0,
    )
    conv_part = (
        small[:lines].reshape(lines, data_size, -1).transpose(1, 0, 2).reshape(data_size, -1)
    )
    norm_part = small[lines : lines + 2 * width // span].reshape(data_size, -1)
    beta_part = small[lines + 2 * width // span :].reshape(data_size, -1)
    small_own = lax.psum_scatter(
        jnp.concatenate([conv_part, norm_part, beta_part], 1), "dp", scatter_dimension=0
    )
    conv_out = small_own[: conv_kernel.size].reshape(conv_kernel.shape)
    norm_one_out = small_own[conv_kernel.size : conv_kernel.size + strip]
    norm_two_out = small_own[conv_kernel.size + strip : conv_kernel.size + 2 * strip]
    beta_out = small_own[conv_kernel.size + 2 * strip :].reshape(-1, strip).T

    def placed(blocks):
        return exclusive_order(trade([values.astype(LOW) for values in blocks]))

    ffn_out = jnp.stack(
        [
            jnp.concatenate([values.astype(WIDE) for values in placed(list(grad))], 1)
            for grad in ffn_grads
        ],
        1,
    )
    down_out = jnp.concatenate(
        [
            values.astype(WIDE).T
            for values in placed(list(down_grads[0]) + list(down_grads[1]))
        ],
        0,
    )
    out_out = jnp.concatenate(
        exclusive_order(jnp.split(jnp.concatenate([grad[0] for grad in out_grads], 1).T, 4, axis=0)),
        0,
    )
    mix_blocks = sum((jnp.split(grad[0], 2, axis=1) for grad in mix_grads), [])
    mix_out = jnp.concatenate(
        [
            values.reshape(strip, 2, 4, HEAD).transpose(0, 2, 1, 3).reshape(strip, 4, span)
            for values in exclusive_order(mix_blocks)
        ],
        2,
    )
    return (
        out,
        grad_input,
        norm_one_out,
        mix_out,
        beta_out,
        conv_out,
        head_out,
        out_out,
        norm_two_out,
        ffn_out,
        down_out,
    )


def exchange(values, axis):
    return lax.all_to_all(values, axis, 0, 0, tiled=True)


def swap_mp(values):
    return lax.ppermute(values, "mp", SWAP)


def swap_core(values):
    return lax.ppermute(values, "dmod", CORE)


def swap_across(values):
    return lax.ppermute(values, "dmod", ACROSS)


def swap_dp(values, k):
    return lax.ppermute(values, "dp", [(i, i ^ k) for i in range(lax.axis_size("dp"))])


def trade_blocks(blocks, axis, place):
    size = len(blocks)
    blocks = by_difference(blocks, place)
    moved = [blocks[0]] + [
        lax.ppermute(blocks[k], axis, [(i, i ^ k) for i in range(size)]) for k in range(1, size)
    ]
    return by_difference(moved, place)


def by_difference(blocks, place):
    bit = 1
    while bit < len(blocks):
        flip = (place & bit) != 0
        blocks = [jnp.where(flip, blocks[i ^ bit], blocks[i]) for i in range(len(blocks))]
        bit *= 2
    return blocks


def everyone(values, place):
    size = lax.axis_size("dp")
    values = values[None]
    bit = 1
    while bit < size:
        values = jnp.concatenate(turn((place & bit) != 0, (values, swap_dp(values, bit))), 0)
        bit *= 2
    return values


def turn(flag, pair):
    return jnp.where(flag, pair[1], pair[0]), jnp.where(flag, pair[0], pair[1])


def chip_blocks(core, pair):
    keep, send = turn(core, pair)
    return jnp.stack(turn(core, (keep, swap_core(send))), 1)


def along_column(core, pair, earlier=None):
    both = chip_blocks(core, pair)
    if earlier is not None:
        both = after(both, earlier)
    return exchange(both, "dp")


def gather_columns(values, earlier=None, later=None):
    if earlier is not None:
        values = after(values, earlier)
    half = values.shape[0] // 2
    over = swap_mp(values)
    far = swap_across(values)
    corner = (over[:half], far[half:])
    if later is not None:
        corner = after(corner, later)
    both = [swap_across(corner[0]), swap_mp(corner[1])]
    return [[[values], [far]], [[over], both]]


def wide(values):
    return values.astype(WIDE)


def scatter_send(grid):
    half = grid[0][0].shape[0] // 2
    return (
        jnp.concatenate([grid[1][0][:half], grid[1][1][:half]], 0),
        jnp.concatenate([grid[0][1][half:], grid[1][1][half:]], 0),
    )


def scatter_turn(grid, sent):
    half = grid[0][0].shape[0] // 2
    top = wide(grid[0][1][:half]) + wide(sent[0][half:])
    low = wide(grid[1][0][half:]) + wide(sent[1][half:])
    return top.astype(LOW), low.astype(LOW)


def scatter_end(grid, sent, back):
    half = grid[0][0].shape[0] // 2
    top = wide(grid[0][0][:half]) + wide(sent[0][:half]) + wide(swap_across(back[0]))
    low = wide(grid[0][0][half:]) + wide(sent[1][:half]) + wide(swap_mp(back[1]))
    return jnp.concatenate([top, low], 0).astype(LOW)


def column_tokens(values):
    size = lax.axis_size("dp")
    moved = [values] + [swap_dp(values, k) for k in range(1, size)]
    mine = jnp.concatenate(by_difference(moved, lax.axis_index("dp")), 0)
    return [mine, swap_core(mine)]


def column_chip(near, far):
    return (wide(near) + wide(swap_core(far))).astype(LOW)


def column_total(chip):
    size = lax.axis_size("dp")
    moved = exchange(chip, "dp").reshape(size, chip.shape[0] // size, -1)
    return jnp.sum(wide(moved), 0)


def column_hops(chip):
    size = lax.axis_size("dp")
    blocks = by_difference(jnp.split(chip, size), lax.axis_index("dp"))
    return sum([wide(blocks[0])] + [wide(swap_dp(blocks[k], k)) for k in range(1, size)])


def column_body(
    block_input,
    segment_ids,
    group_ids,
    group_weight,
    mixer_norm,
    w_mix,
    w_beta,
    conv_kernel,
    head_norm,
    w_out,
    ffn_norm,
    w_ffn_in,
    w_ffn_down,
    cotangent,
):
    place = lax.axis_index("dp")
    size = lax.axis_size("dp")
    side = lax.axis_index("mp")
    dmod = lax.axis_index("dmod")
    row, core = dmod // 2, dmod % 2
    at_far_side, at_far_row, at_core = side == 1, row == 1, core == 1
    micro, _, length, width = block_input.shape
    share = length // size
    strip = w_mix.shape[0]
    groups = group_weight.shape[0]
    group_heads = w_beta.shape[1]
    hidden = w_ffn_down.shape[0] // (2 * size)
    span = 2 * width

    def to_column(values):
        lead = values.shape[:-1]
        values = values.reshape(lead + (2, 2, size, strip))
        values = jnp.swapaxes(values, -2, -3).reshape(lead + (2, span))
        return jnp.concatenate(turn(at_far_row, (values[..., 0, :], values[..., 1, :])), -1)

    def from_column(values):
        lead = values.shape[:-1]
        halves_of = turn(at_far_row, (values[..., :span], values[..., span:]))
        values = jnp.stack(halves_of, -2).reshape(lead + (2, size, 2, strip))
        return jnp.swapaxes(values, -2, -3).reshape(lead + (2 * span,))

    def over_dp(values):
        values = values.reshape(micro, size, share, width)
        moved = trade_blocks([values[:, z] for z in range(size)], "dp", place)
        moved = jnp.where(at_far_side, jnp.stack(moved[2:]), jnp.stack(moved[:2]))
        return moved.reshape(4, share, width)

    def over_dmod(moved):
        moved = trade_blocks([moved[j] for j in range(4)], "dmod", dmod)
        return to_column(jnp.concatenate(moved, 1))

    def tokens_out(values):
        blocks = jnp.split(from_column(values), 4, axis=1)
        moved = jnp.stack(trade_blocks(blocks, "dmod", dmod)).reshape(2, micro, share, width)
        moved = jnp.concatenate(turn(at_far_side, (moved, swap_mp(moved))), 0)
        moved = trade_blocks([moved[z] for z in range(size)], "dp", place)
        return jnp.stack(moved, 1).reshape(block_input.shape)

    blocks = w_mix.reshape(strip, 4, 2, size, HEAD).transpose(2, 3, 0, 1, 4)
    blocks = blocks.reshape(2, size, strip, 4 * HEAD)
    blocks = jnp.concatenate([blocks, w_out.reshape(2, size, HEAD, strip)], 3)
    mix_blocks = chip_blocks(at_core, (blocks[0], blocks[1]))
    mix_pieces = exchange(mix_blocks, "dp")
    block_input, cotangent, conv_kernel, w_ffn_in, w_ffn_down = after(
        (block_input, cotangent, conv_kernel, w_ffn_in, w_ffn_down), mix_blocks
    )
    blocks = jnp.concatenate(
        [
            w_ffn_in.transpose(1, 2, 0).reshape(2, 2 * size, hidden, strip),
            w_ffn_down.reshape(1, 2 * size, hidden, strip),
        ],
        0,
    )
    blocks = blocks.transpose(1, 0, 2, 3).reshape(2, size, 3 * hidden, strip)
    ffn_blocks = chip_blocks(at_core, (blocks[0], blocks[1]))

    small = [
        conv_kernel.reshape(-1),
        head_norm,
        mixer_norm,
        ffn_norm,
        w_beta.T.reshape(-1),
        segment_ids.reshape(-1).astype(LOW),
        group_ids.reshape(-1).astype(LOW),
    ]
    count = sum(item.size for item in small)
    pack = jnp.concatenate(small + [jnp.zeros((-count % HEAD,), LOW)]).reshape(-1, HEAD)
    packs = everyone(pack, place)
    packs = jnp.stack(turn(at_far_side, (packs, swap_mp(packs))))
    packs = jnp.stack(turn(at_core, (packs, swap_core(packs))))
    packs = jnp.stack(turn(at_far_row, (packs, swap_across(packs))))
    packs = packs.reshape(2, 2, 2, size, -1)

    tokens_low, way_moved = over_dp(block_input), over_dp(cotangent)
    tokens_low = over_dmod(after(tokens_low, (mix_pieces, packs, ffn_blocks)))
    rows = wide(tokens_low)
    tokens_pair = column_tokens(tokens_low)
    mix_weights = gather_columns(mix_pieces)
    ffn_pieces = exchange(ffn_blocks, "dp")
    way_low = over_dmod(after(way_moved, tokens_pair[0]))

    fields = []
    start = 0
    for item in small:
        fields.append(packs[..., start : start + item.size])
        start += item.size
    lines = conv_kernel.shape[0] * conv_kernel.shape[1]
    heads = 2 * group_heads
    local_head = size * core + place
    own_heads = [group_heads * side + local_head, group_heads * (1 - side) + local_head]
    conv_all = (
        fields[0]
        .reshape(2, 2, 2, size, lines, -1)
        .transpose(4, 2, 0, 1, 3, 5)
        .reshape(lines, heads * HEAD)
    )
    conv = wide(
        jnp.concatenate(
            [lax.dynamic_slice_in_dim(conv_all, head * HEAD, HEAD, 1) for head in own_heads], 1
        )
    )
    head_gain = wide(fields[1][0, 0, 0].reshape(1, HEAD))
    gain_one = to_column(wide(fields[2][:, :, 0].reshape(1, -1)))
    gain_two = to_column(wide(fields[3][:, :, 0].reshape(1, -1)))
    beta_rows = (
        fields[4]
        .reshape(2, 2, 2, size, group_heads, strip)
        .transpose(2, 4, 0, 1, 3, 5)
        .reshape(heads, -1)
    )
    beta_weights = to_column(
        jnp.concatenate([lax.dynamic_slice_in_dim(beta_rows, head, 1, 0) for head in own_heads], 0)
    )
    sequence = 2 * side + row
    segments = lax.dynamic_index_in_dim(fields[5][0, 0, 0], sequence, 0, keepdims=False)
    segments = segments.reshape(micro, length).astype(jnp.int32)
    segments = jnp.concatenate(turn(at_core, (segments[:1], segments[1:])), 0)
    seg_col = segments.reshape(-1, 1)
    seg_row = segments.reshape(micro, 1, length)
    all_groups = fields[6][0, 0, 0].reshape(-1).astype(jnp.int32)
    names = jnp.arange(groups, dtype=jnp.int32)
    counts = jnp.sum((all_groups[:, None] == names[None]).astype(WIDE), 0)
    table = group_weight * (all_groups.shape[0] / groups) / counts
    own_groups = lax.dynamic_slice_in_dim(all_groups, sequence * micro * length, micro * length, 0)
    scales = jnp.sum((own_groups[:, None] == names[None]).astype(WIDE) * table, -1, keepdims=True)
    scales = jnp.concatenate(turn(at_core, (scales[:length], scales[length:])), 0)

    constants = [beta_weights, seg_col, seg_row, conv, head_gain]
    gated, inverse, update, mixed, mixer_in, *projected, beta_in, near, far = column_forward(
        tokens_pair, mix_weights, gain_one, *constants
    )
    middle = rows + column_total(after(column_chip(near, far), ffn_pieces))

    second_scale = lax.rsqrt(jnp.mean(middle * middle, -1, keepdims=True) + 1e-06)
    ffn_low = (middle * second_scale * gain_two).astype(LOW)
    way_pair = column_tokens(after(way_low, middle))
    direction = wide(way_low) * lax.dynamic_slice_in_dim(scales, place * share, share, 0)
    ffn_pair = column_tokens(ffn_low)
    ffn_weights = gather_columns(ffn_pieces, mix_weights[1][1])
    near, far, ffn_in, directions, active, gate_grad, up_grad = column_ffn(
        ffn_pair, way_pair, scales, ffn_weights, hidden
    )
    chip = column_chip(near, far)
    ffn_in_grad = column_hops(chip)
    near, far, ffn_grads = column_ffn_grads(
        after(active, chip),
        gate_grad,
        up_grad,
        ffn_in,
        directions,
        ffn_weights,
        jax.ShapeDtypeStruct((size, 2, 3 * hidden, strip), LOW),
    )
    out_chip = column_chip(near, far)
    ffn_sent = scatter_send(ffn_grads)
    ffn_in_grad = after(ffn_in_grad, out_chip)
    ffn_sent = swap_mp(ffn_sent[0]), swap_across(ffn_sent[1])

    weighted_two = ffn_in_grad * gain_two
    norm_two_grad = jnp.sum(ffn_in_grad * middle * second_scale, 0, keepdims=True)
    inner_two = jnp.mean(weighted_two * middle, -1, keepdims=True)
    middle_grad = (
        direction + second_scale * weighted_two - middle * (second_scale**3 * inner_two)
    )
    branch_pair = column_tokens(middle_grad.astype(LOW))
    down_sum = column_total(after(out_chip, branch_pair[0]))
    ffn_back = scatter_turn(ffn_grads, ffn_sent)

    signal_grads, beta_grad, conv_grad, head_grad, near, far, branch_all = column_backward(
        branch_pair,
        mix_weights,
        *constants,
        (inverse, update, mixed),
        projected,
        beta_in,
    )
    mix_grads = column_mixer_grads(
        mixer_in,
        signal_grads,
        gated,
        branch_all,
        jax.ShapeDtypeStruct((size, 2, strip, 5 * HEAD), LOW),
    )
    chip = column_chip(near, far)
    mixer_grad = column_total(chip)
    ffn_total = scatter_end(ffn_grads, ffn_sent, ffn_back)
    mix_sent = scatter_send(mix_grads)
    mix_sent = after((swap_mp(mix_sent[0]), swap_across(mix_sent[1])), mixer_grad)
    mix_back = scatter_turn(mix_grads, mix_sent)
    mix_total = scatter_end(mix_grads, mix_sent, mix_back)
    out_low = (middle + after(down_sum, mix_back)).astype(LOW)

    def placed(total, earlier=None):
        return along_column(at_core, (total[:, 0], total[:, 1]), earlier).transpose(1, 0, 2, 3)

    ffn_pieces = placed(ffn_total)
    ffn_out = wide(
        ffn_pieces[:, :, : 2 * hidden]
        .reshape(2 * size, 2, hidden, strip)
        .transpose(1, 0, 2, 3)
        .reshape(2, -1, strip)
        .transpose(2, 0, 1)
    )
    down_out = wide(ffn_pieces[:, :, 2 * hidden :].reshape(-1, strip))
    mix_pieces = placed(mix_total, ffn_pieces).reshape(2 * size, strip, 5, HEAD)
    mix_out = wide(mix_pieces[:, :, :4].transpose(1, 2, 0, 3).reshape(strip, 4, -1))
    out_out = wide(mix_pieces[:, :, 4].reshape(-1, strip))
    beta_weight_grad = contract(beta_grad.astype(LOW), mixer_in, 0, 0)
    weighted_one = mixer_grad * gain_one
    first_scale = lax.rsqrt(jnp.mean(rows * rows, -1, keepdims=True) + 1e-06)
    norm_one_grad = jnp.sum(mixer_grad * rows * first_scale, 0, keepdims=True)
    inner_one = jnp.mean(weighted_one * rows, -1, keepdims=True)
    grad_low = (
        middle_grad + first_scale * weighted_one - rows * (first_scale**3 * inner_one)
    ).astype(LOW)
    out = tokens_out(out_low)
    grad_input = wide(tokens_out(grad_low))

    conv_sides = jnp.stack(turn(at_far_side, jnp.split(jnp.sum(conv_grad, 0), 2, axis=1)))
    beta_sides = from_column(
        jnp.concatenate(turn(at_far_side, (beta_weight_grad[:1], beta_weight_grad[1:])), 0)
    )
    vector = jnp.concatenate(
        [
            conv_sides.reshape(-1, HEAD),
            beta_sides.reshape(-1, HEAD),
            from_column(norm_one_grad).reshape(-1, HEAD),
            from_column(norm_two_grad).reshape(-1, HEAD),
            jnp.sum(head_grad, 0),
        ]
    )
    vector = after(vector, mix_back)
    vector = vector + swap_mp(vector)
    vector = vector + swap_across(vector)
    vectors = jnp.stack(turn(at_core, (vector, swap_core(vector))))
    vectors = everyone(vectors, place)
    ends = [2 * lines, 2 * lines + 4 * span // HEAD]
    own_width = dmod * width + place * strip
    taps_own = conv_kernel.shape[2]
    at = (dmod * size + place) * taps_own
    conv_head = at // HEAD
    conv_out = lax.dynamic_slice(
        vectors,
        (conv_head % size, conv_head // size, side * lines, at % HEAD),
        (1, 1, lines, taps_own),
    ).reshape(conv_kernel.shape)
    beta_out = (
        lax.dynamic_slice(
            vectors[:, :, ends[0] : ends[1]].reshape(size, 2, 2, 2 * span),
            (0, 0, side, own_width),
            (size, 2, 1, strip),
        )
        .reshape(size, 2, strip)
        .transpose(2, 1, 0)
        .reshape(strip, group_heads)
    )
    sums = jnp.sum(vectors[:, :, ends[1] :], (0, 1))
    norms = sums[:-1].reshape(2, -1)
    norm_one_out, norm_two_out = (
        lax.dynamic_slice_in_dim(norms[i], own_width, strip, 0) for i in (0, 1)
    )
    head_out = lax.dynamic_slice_in_dim(sums[-1], place * head_norm.size, head_norm.size, 0)
    return (
        out,
        grad_input,
        norm_one_out,
        mix_out,
        beta_out,
        conv_out,
        head_out,
        out_out,
        norm_two_out,
        ffn_out,
        down_out,
    )


def solution(mesh):
    sizes = dict(mesh.shape)
    columns = sizes["mp"] * sizes["dmod"] // 2
    body = column_body if columns == sizes["dp"] else plane_body
    wide = P(("dmod", "dp"))
    tokens = P(None, "dp", None, "dmod")
    weights = (
        wide,
        P(("dmod", "dp"), None, "mp"),
        P(("dmod", "dp"), "mp"),
        P(None, None, ("mp", "dmod", "dp")),
        P("dp"),
        P("mp", ("dmod", "dp")),
        wide,
        P(("dmod", "dp"), None, "mp"),
        P("mp", ("dmod", "dp")),
    )
    ids = P(None, "dp", None)
    return jax.shard_map(
        body,
        mesh=mesh,
        in_specs=(tokens, ids, ids, P()) + weights + (tokens,),
        out_specs=(tokens, tokens) + weights,
        check_vma=False,
    )
```
